32 devices in a mesh: coarse: 8 (over z, x), fine: 4 (over y, core).
Axes of the slice: x: 2, y: 2, z: 4, core: 2. Of those that a mesh axis runs over, the one named last changes fastest.
Arguments:
- node_feats: bfloat16 [65536, 256], P(('coarse', 'fine')), may hold values from -6 to 6
- grad_out: bfloat16 [65536, 256], P(('coarse', 'fine')), may hold values from -6 to 6
- cluster_ids: int32 [65536], P(('coarse', 'fine')), may hold values from 0 to 8191, as said below
- halo_lists: int32 [1024], P('coarse'), may hold values from 0 to 1023, as said below
- edge_sources: int32 [32768], P('coarse'), may hold values from 0 to 1151, as said below
- w_edge_in: bfloat16 [512, 256], replicated, may hold values from -0.25 to 0.25
- b_edge_in: bfloat16 [256], replicated, may hold values from -4 to 4
- w_edge_out: bfloat16 [256, 256], replicated, may hold values from -0.375 to 0.375
- w_unpool: bfloat16 [256, 256], replicated, may hold values from -0.375 to 0.375
Outputs:
- grad_feats: bfloat16 [65536, 256], P(('coarse', 'fine'))
- grad_w_in: float32 [512, 256], replicated
- grad_b_in: float32 [256], replicated
- grad_w_out: float32 [256, 256], replicated
- grad_unpool: float32 [256, 256], replicated
The draws below stay inside these ranges and needn't reach their ends.
Inputs may be any that keep to these rules, and one draw needn't show every extreme that they name: `cluster_ids`: the fine nodes on the devices of coarse index g lie in cells g*1024 to (g+1)*1024 - 1. `halo_lists`: each owner's block of 128 entries holds distinct indices. `edge_sources`: each owner's block of 4096 entries takes every value of its range at least once.
All inputs are finite; a program needn't handle non-finite values.
Results may differ from the reference program's by a relative error of at most 0.0065.
Values may be sent and summed in bfloat16 or wider, within the bound.
No kernel may reach another device: no remote copies, remote signals or barrier semaphores. Data moves between devices by JAX's collectives and lax.ppermute only.
A program may use at most 128 MiB of HBM per device.

```python
import jax
import jax.numpy as jnp
from jax import lax

H = 256
NF_DEV = 2048
K = 4
CD = 1024
HS = 64
CELLS = 8192
NODES = 65536
EDGES = 32768
N_FINE = 4


def draw_cluster_ids(key, part):
    key = jax.random.fold_in(key, 11)
    row_ids = jnp.arange(NODES, dtype=jnp.int32)
    group_rows = NF_DEV * N_FINE
    groups = row_ids // group_rows
    position = row_ids % group_rows
    local_ids = jax.random.randint(key, (NODES,), 0, CD, dtype=jnp.int32)
    local_ids = jnp.where(position == 0, CD - 1, jnp.where(position == 1, 0, local_ids))
    return (groups * CD + local_ids).astype(jnp.int32)


def one_list(sub_key):
    return jax.random.permutation(sub_key, CD)[:2 * HS].astype(jnp.int32)


def draw_halo_lists(key, part):
    key = jax.random.fold_in(key, 23)
    sub_keys = jax.random.split(key, CELLS // CD)
    return jax.vmap(one_list)(sub_keys).reshape(-1).astype(jnp.int32)


def owner_sources(sub_key):
    first_key, second_key, third_key = jax.random.split(sub_key, 3)
    rows = CD + 2 * HS
    covered = jax.random.permutation(first_key, rows).astype(jnp.int32)
    others = jax.random.randint(second_key, (CD * K - rows,), 0, rows, dtype=jnp.int32)
    joined = jnp.concatenate([covered, others])
    order = jax.random.permutation(third_key, CD * K)
    return jnp.take(joined, order).astype(jnp.int32)


def draw_edge_sources(key, part):
    key = jax.random.fold_in(key, 37)
    sub_keys = jax.random.split(key, CELLS // CD)
    return jax.vmap(owner_sources)(sub_keys).reshape(-1).astype(jnp.int32)


def shard_levels(key, shape, pieces, least, largest):
    factor_of = 1.0
    for axis_at, blocks in pieces:
        steps = jax.random.uniform(jax.random.fold_in(jax.random.fold_in(key, 6), axis_at), (blocks,), jnp.float32, least / len(pieces), largest / len(pieces))
        factor_of = factor_of * jnp.repeat(jnp.exp(steps), shape[axis_at] // blocks).reshape((-1,) + (1,) * (len(shape) - 1 - axis_at))
    return factor_of


def gaussian(stream_key, dims, deviation, bound, shards=(), kind=jnp.bfloat16):
    loudness = shard_levels(stream_key, dims, shards, -0.22, 0.18) if shards else 1.0
    array = jax.random.normal(stream_key, dims, jnp.float32) * deviation * loudness
    return jnp.minimum(jnp.maximum(array, -bound), bound).astype(kind)


def setup_inputs(seed: int = 0) -> dict:
    splits = jax.random.split(jax.random.key(seed), 10)
    return {
        "node_feats": gaussian(splits[0], (NODES, H), 1.0, 6.0, ((0, 32),)),
        "grad_out": gaussian(splits[1], (NODES, H), 1.0, 6.0, ((0, 32),)),
        "cluster_ids": draw_cluster_ids(jax.random.fold_in(splits[9], 71), 0),
        "halo_lists": draw_halo_lists(jax.random.fold_in(splits[9], 71), 0),
        "edge_sources": draw_edge_sources(jax.random.fold_in(splits[9], 71), 0),
        "w_edge_in": gaussian(splits[5], (2 * H, H), (2 * H) ** -0.5, 0.25),
        "b_edge_in": gaussian(splits[6], (H,), 1.0, 4.0),
        "w_edge_out": gaussian(splits[7], (H, H), H ** -0.5, 0.375),
        "w_unpool": gaussian(splits[8], (H, H), H ** -0.5, 0.375),
    }


def edge_work(dst_bf, dst_full, extended, sources, grad_sum_bf, w_edge_in, b_edge_in, w_edge_out, w_unpool):
    row_count = dst_bf.shape[0]
    feature_width = dst_bf.shape[1]
    fan_count = sources.shape[0] // row_count
    dst_rep = jnp.repeat(dst_bf, fan_count, axis=0)
    src_feats = jnp.take(extended, sources, axis=0)
    joined = jnp.concatenate([dst_rep, src_feats], axis=1)
    pre_act = jnp.dot(joined, w_edge_in, preferred_element_type=jnp.float32) + b_edge_in.astype(jnp.float32)
    sigmoid_act = jax.nn.sigmoid(pre_act)
    hidden = (pre_act * sigmoid_act).astype(jnp.bfloat16)
    messages = jnp.dot(hidden, w_edge_out, preferred_element_type=jnp.float32)
    aggregate = messages.reshape(row_count, fan_count, feature_width).sum(axis=1)
    new_coarse = (dst_full + aggregate).astype(jnp.bfloat16)
    grad_new = jnp.dot(grad_sum_bf, w_unpool.T, preferred_element_type=jnp.float32).astype(jnp.bfloat16)
    grad_up = jnp.dot(new_coarse.T, grad_sum_bf, preferred_element_type=jnp.float32)
    grad_msg = jnp.repeat(grad_new, fan_count, axis=0)
    grad_w2 = jnp.dot(hidden.T, grad_msg, preferred_element_type=jnp.float32)
    grad_hidden = jnp.dot(grad_msg, w_edge_out.T, preferred_element_type=jnp.float32)
    grad_act = (grad_hidden * sigmoid_act * (1.0 + pre_act * (1.0 - sigmoid_act))).astype(jnp.bfloat16)
    grad_w1 = jnp.dot(joined.T, grad_act, preferred_element_type=jnp.float32)
    grad_b1 = jnp.sum(grad_act.astype(jnp.float32), axis=0)
    grad_joined = jnp.dot(grad_act, w_edge_in.T, preferred_element_type=jnp.float32)
    grad_dst = grad_new.astype(jnp.float32) + grad_joined[:, :feature_width].reshape(row_count, fan_count, feature_width).sum(axis=1)
    grad_src = jax.ops.segment_sum(grad_joined[:, feature_width:], sources, num_segments=extended.shape[0])
    return grad_dst, grad_src, grad_up, grad_w2, grad_w1, grad_b1


def take_rows(block, indices):
    return jnp.take(block, indices, axis=0)


def scatter_back(for_right, for_left, right_ids, left_ids):
    return jax.ops.segment_sum(for_right, right_ids, num_segments=CD) + jax.ops.segment_sum(for_left, left_ids, num_segments=CD)


def reference(node_feats, grad_out, cluster_ids, halo_lists, edge_sources, w_edge_in, b_edge_in, w_edge_out, w_unpool):
    pooled = jax.ops.segment_sum(node_feats.astype(jnp.float32), cluster_ids, num_segments=CELLS)
    grad_sum = jax.ops.segment_sum(grad_out.astype(jnp.float32), cluster_ids, num_segments=CELLS)
    pooled_bf = pooled.astype(jnp.bfloat16)
    grad_sum_bf = grad_sum.astype(jnp.bfloat16)
    owners = CELLS // CD
    blocks = pooled_bf.reshape(owners, CD, H)
    lists = halo_lists.reshape(owners, 2, HS)
    to_right = jax.vmap(take_rows)(blocks, lists[:, 0])
    to_left = jax.vmap(take_rows)(blocks, lists[:, 1])
    from_left = jnp.roll(to_right, 1, axis=0)
    from_right = jnp.roll(to_left, -1, axis=0)
    extended = jnp.concatenate([blocks, from_left, from_right], axis=1)

    def per_owner(items):
        return edge_work(items[0], items[1], items[2], items[3], items[4], w_edge_in, b_edge_in, w_edge_out, w_unpool)

    grad_dst, grad_src, grad_up, grad_w2, grad_w1, grad_b1 = lax.map(
        per_owner,
        (blocks, pooled.reshape(owners, CD, H), extended, edge_sources.reshape(owners, CD * K), grad_sum_bf.reshape(owners, CD, H)))
    back_left = grad_src[:, CD:CD + HS]
    back_right = grad_src[:, CD + HS:]
    for_right = jnp.roll(back_left, -1, axis=0)
    for_left = jnp.roll(back_right, 1, axis=0)
    returned = jax.vmap(scatter_back)(for_right, for_left, lists[:, 0], lists[:, 1])
    grad_pool = (grad_dst + grad_src[:, :CD] + returned).reshape(CELLS, H)
    grad_feats = (grad_out.astype(jnp.float32) + jnp.take(grad_pool, cluster_ids, axis=0)).astype(jnp.bfloat16)
    edge_scale = float(EDGES) ** -0.5
    cell_scale = float(CELLS) ** -0.5
    return (grad_feats, grad_w1.sum(axis=0) * edge_scale, grad_b1.sum(axis=0) * edge_scale,
            grad_w2.sum(axis=0) * edge_scale, grad_up.sum(axis=0) * cell_scale)
```

```python
import functools

import jax
import jax.numpy as jnp
from jax import lax
from jax.experimental import pallas as pl
from jax.experimental.pallas import tpu as pltpu
from jax.sharding import PartitionSpec as P

K = 4
BF = jnp.bfloat16
F32 = jnp.float32
LANES = 128
PACK = 16
MIB = 1 << 20


def dot(a, b):
    return jnp.dot(a, b, preferred_element_type=F32)


def dot_nt(a, b):
    return lax.dot_general(a, b, (((1,), (1,)), ((), ())), preferred_element_type=F32)


def dot_tn(a, b):
    return lax.dot_general(a, b, (((0,), (0,)), ((), ())), preferred_element_type=F32)


def bits_of(count):
    assert count > 1 and count & (count - 1) == 0
    return count.bit_length() - 1


def swap(x, axis, bit):
    count = lax.axis_size(axis)
    return lax.ppermute(x, axis, [(i, i ^ (1 << bit)) for i in range(count)])


def shift(x, axis, step):
    count = lax.axis_size(axis)
    return lax.ppermute(x, axis, [(i, (i + step) % count) for i in range(count)])


def send_owner(x, step, flip):
    owners, fines = lax.axis_size("coarse"), lax.axis_size("fine")
    pairs = [
        (g * fines + f, (g + step) % owners * fines + (f ^ (2 * flip)))
        for g in range(owners)
        for f in range(fines)
    ]
    return lax.ppermute(x, ("coarse", "fine"), pairs)


def call(body, outs, args, flops, vmem=16, scratch=(), anywhere=0):
    moved = sum(a.size * a.dtype.itemsize for a in (*args, *outs))
    spaces = [pltpu.HBM] * anywhere + [pltpu.VMEM] * (len(args) - anywhere)
    return pl.pallas_call(
        body,
        out_shape=outs,
        in_specs=[pl.BlockSpec(memory_space=space) for space in spaces],
        scratch_shapes=scratch,
        compiler_params=pltpu.CompilerParams(vmem_limit_bytes=vmem * MIB),
        cost_estimate=pl.CostEstimate(flops=int(flops), bytes_accessed=int(moved), transcendentals=0),
    )(*args)


def sds(shape, dtype):
    return jax.ShapeDtypeStruct(shape, dtype)


def column(row):
    blocks = [
        jnp.broadcast_to(row[:, i : i + LANES], (LANES, LANES)).T
        for i in range(0, row.shape[1], LANES)
    ]
    return blocks[0] if len(blocks) == 1 else jnp.concatenate(blocks, axis=0)


def hot_rows(row, width):
    ids = column(row)
    ids = jnp.concatenate([ids] * (width // LANES), axis=1)
    lane = lax.broadcasted_iota(jnp.int32, ids.shape, 1)
    return jnp.where(lane == ids, 1.0, 0.0).astype(BF)


def hot_columns(row, height, start=0):
    shape = (height, row.shape[1])
    at = lax.broadcasted_iota(jnp.int32, shape, 0)
    return jnp.where(at == row - start, 1.0, 0.0).astype(BF)


def pool_body(ids_hbm, x_hbm, keep_ref, send_ref, ids_ref, x_ref, sems):
    copies = [
        pltpu.make_async_copy(ids_hbm, ids_ref, sems.at[0]),
        pltpu.make_async_copy(x_hbm, x_ref, sems.at[1]),
    ]
    for copy in copies:
        copy.start()
    for copy in copies:
        copy.wait()
    half = keep_ref.shape[0]
    core = lax.axis_index("fine") % 2
    ids = lax.rem(ids_ref[...], 2 * half)
    x = x_ref[...]
    step = min(256, half)
    for out_ref, base in ((send_ref, (1 - core) * half), (keep_ref, core * half)):
        for t in range(0, half, step):
            out_ref[t : t + step, :] = dot(hot_columns(ids, step, base + t), x)


def halo_body(part_ref, lists_ref, right_ref, left_ref):
    half = part_ref.shape[0]
    width = right_ref.shape[0]
    core = lax.axis_index("fine") % 2
    picked = dot(hot_rows(lists_ref[...] - core * half, half), part_ref[...]).astype(BF)
    right_ref[...] = picked[:width]
    left_ref[...] = picked[width:]


def halo_sum_body(*refs):
    *parts, out_ref, slots = refs
    count = len(parts) // 2
    side = parts[0].shape[0]
    chip = lax.axis_index("fine") // 2
    for first, pieces in ((0, parts[:count]), (side, parts[count:])):
        for offset, piece in enumerate(pieces):
            slots[chip ^ offset] = piece[...].astype(F32)
        total = slots[0]
        for i in range(1, count):
            total = total + slots[i]
        out_ref[first : first + side, :] = total.astype(BF)


def core_order(half):
    core = lax.axis_index("fine") % 2
    at_own = pl.ds(pl.multiple_of(core * half, half), half)
    at_other = pl.ds(pl.multiple_of((1 - core) * half, half), half)
    return at_own, at_other


def forward_body(
    own_p, other_p, own_halo, other_halo, src_ref, w1_ref, b_ref,
    ext, hid, slope, feats,
):
    half, width = own_p.shape
    cells = 2 * half
    rows = ext.shape[0]
    at_own, at_other = core_order(half)
    ext[at_own, :] = own_p[...]
    ext[at_other, :] = other_p[...]
    ext[cells:, :] = own_halo[...] + other_halo[...]
    base = dot(ext[0:cells, :], w1_ref[0:width, :]) + b_ref[...].astype(F32)
    block = 256
    for k in range(K):
        for t in range(0, cells, block):
            part = src_ref[k : k + 1, t : t + block]
            feats[t : t + block, :] = dot(hot_rows(part, rows), ext[...]).astype(BF)
        pre = base + dot(feats[...], w1_ref[width : 2 * width, :])
        sig = 0.5 * jnp.tanh(0.5 * pre) + 0.5
        hidden = pre * sig
        hid[...] = hidden if k == 0 else hid[...] + hidden
        slope[k * cells : (k + 1) * cells, :] = sig + hidden * (1.0 - sig)


def split(x):
    high = x.astype(BF)
    return high, (x - high.astype(F32)).astype(BF)


def bias_rows(bias):
    high, low = split(bias)
    at = lax.broadcasted_iota(jnp.int32, (PACK, bias.shape[1]), 0)
    return jnp.where(at == 0, high.astype(F32), jnp.where(at == 1, low.astype(F32), 0.0))


def backward_body(
    own_g, other_g, ext, hid, slope, src_ref, w1_ref, wo_ref, wu_ref,
    gs_ref, ga_ref, gn_ref, back_l, back_r, send_ref,
    gsum, act, total,
):
    half, width = own_g.shape
    cells = 2 * half
    rows = ext.shape[0]
    side = back_l.shape[0]
    fine = lax.axis_index("fine")
    at_own, at_other = core_order(half)
    gsum[at_own, :] = own_g[...]
    gsum[at_other, :] = other_g[...]
    gn = dot_nt(gsum[...], wu_ref[...]).astype(BF)
    gn_ref[...] = gn
    grad = dot_nt(gn, wo_ref[...])
    for k in range(K):
        at = slice(k * cells, (k + 1) * cells)
        part = (grad * slope[at, :]).astype(BF)
        act[at, :] = part
        ga_ref[...] = part.astype(F32) if k == 0 else ga_ref[...] + part.astype(F32)
    step = LANES
    for r in range(0, rows, step):
        out = jnp.zeros((step, width), F32)
        for k in range(K):
            at = slice(k * cells, (k + 1) * cells)
            out += dot(hot_columns(src_ref[k : k + 1, :], step, r), act[at, :])
        gs_ref[r : r + step, :] = out
    back = dot_nt(gs_ref[cells:, :].astype(BF), w1_ref[width : 2 * width, :]).astype(BF)
    back_l[...] = back[:side]
    back_r[...] = back[side:]

    fines, coarses = lax.axis_size("fine"), lax.axis_size("coarse")
    per = 4 * width // fines
    n = min(per, width)
    for index in range(fines):

        @pl.when(fine == index)
        def _():
            for r in range(0, per, n):
                which, first = divmod(index * per + r, width)
                cols = slice(first, first + n)
                if which == 0:
                    high, low = split(ga_ref[...])
                    left = ext[0:cells, cols]
                    out = dot_tn(left, high) + dot_tn(left, low)
                elif which == 1:
                    high, low = split(gs_ref[...])
                    left = ext[:, cols]
                    out = dot_tn(left, high) + dot_tn(left, low)
                elif which == 2:
                    high, low = split(hid[:, cols])
                    out = dot_tn(high, gn_ref[...]) + dot_tn(low, gn_ref[...])
                else:
                    high, low = split(hid[...])
                    agg = dot(high, wo_ref[:, cols]) + dot(low, wo_ref[:, cols])
                    new = (ext[0:cells, cols].astype(F32) + agg).astype(BF)
                    out = dot_tn(new, gsum[...])
                total[r : r + n, :] = out

    bias = bias_rows(jnp.sum(ga_ref[...], axis=0, keepdims=True))
    share = per // coarses
    block = send_ref.shape[0] // coarses
    for g in range(coarses):
        parts = [total[g * share : (g + 1) * share, :], bias[: block - share]]
        send_ref[g * block : (g + 1) * block, :] = jnp.concatenate(parts, axis=0).astype(BF)


def share_body(recv, out_ref, bias_ref, *, share):
    count = lax.axis_size("coarse")
    block = recv.shape[0] // count
    total = recv[0:block, :].astype(F32)
    for g in range(1, count):
        total = total + recv[g * block : (g + 1) * block, :].astype(F32)
    each = out_ref.shape[0] // count
    rows = total[0:each].astype(BF)
    for g in range(count):
        out_ref[g * each : (g + 1) * each, :] = rows
    bias_ref[...] = bias_rows(total[share : share + 1] + total[share + 1 : share + 2]).astype(BF)


def join_body(parts, bias, out_ref):
    n = parts.shape[0]
    out_ref[0:n, :] = parts[...]
    out_ref[n : n + PACK, :] = bias[...]


def merge_body(own, other, out_ref, *, axis, bit):
    n = own.shape[0]
    side = lax.rem(lax.axis_index(axis) // (1 << bit), 2)
    out_ref[pl.ds(pl.multiple_of(side * n, n), n), :] = own[...]
    out_ref[pl.ds(pl.multiple_of((1 - side) * n, n), n), :] = other[...]


def merge(own, axis, bit):
    other = swap(own, axis, bit)
    n, width = own.shape
    body = functools.partial(merge_body, axis=axis, bit=bit)
    return call(body, (sds((2 * n, width), BF),), (own, other), 0)[0]


def weights_body(own, other, w1_ref, gb_ref, wo_ref, up_ref, *, per, share, edge_scale, cell_scale):
    width = own.shape[1]
    core = lax.axis_index("fine") % 2
    coarses = lax.axis_size("coarse")
    pieces = lax.axis_size("fine") // 2
    size = own.shape[0] // pieces
    each = (size - PACK) // coarses
    outs = ((w1_ref, 0, edge_scale), (w1_ref, width, edge_scale), (wo_ref, 0, edge_scale), (up_ref, 0, cell_scale))
    for index in range(2 * pieces):
        first = (index // 2) * size
        mine, theirs = own[first : first + size, :].astype(F32), other[first : first + size, :].astype(F32)
        value = jnp.where(core == index % 2, mine, theirs)
        if index == 0:
            at = size - PACK
            gb_ref[...] = (value[at : at + 1] + value[at + 1 : at + 2]) * edge_scale
        n = min(share, each)
        for g in range(coarses):
            which, row = divmod(index * per + g * n, width)
            out_ref, start, scale = outs[which]
            out_ref[start + row : start + row + n, :] = value[g * each : g * each + n] * scale


def pooled_grad_body(gs_ref, ga_ref, gn_ref, w1_ref, out_ref):
    cells, width = ga_ref.shape
    out_ref[...] = (
        gn_ref[...].astype(F32)
        + dot_nt(ga_ref[...].astype(BF), w1_ref[0:width, :])
        + dot_nt(gs_ref[0:cells, :].astype(BF), w1_ref[width : 2 * width, :])
    )


def feats_body(pool_ref, from_r, from_l, lists_ref, ids_ref, grad_ref, out_ref, table):
    cells = pool_ref.shape[0]
    nodes = grad_ref.shape[0]
    side = from_r.shape[0]
    lists = lists_ref[...]
    returned = jnp.concatenate([from_r[...], from_l[...]], axis=0)
    step = min(256, cells)
    for t in range(0, cells, step):
        add = dot(hot_columns(lists, step, t), returned)
        table[t : t + step, :] = (pool_ref[t : t + step, :] + add).astype(BF)
    block = 256
    for t in range(0, nodes, block):
        ids = lax.rem(ids_ref[:, t : t + block], cells)
        rows = dot(hot_rows(ids, cells), table[...])
        out_ref[t : t + block, :] = (grad_ref[t : t + block, :].astype(F32) + rows).astype(BF)


def local(
    node_feats, grad_out, cluster_ids, halo_lists, edge_sources, w_edge_in, b_edge_in, w_edge_out, w_unpool,
):
    nodes, width = node_feats.shape
    cells = edge_sources.shape[0] // K
    half = cells // 2
    side = halo_lists.shape[0] // 2
    rows = cells + 2 * side
    fines, coarses = lax.axis_size("fine"), lax.axis_size("coarse")
    fine_bits = bits_of(fines)
    ids = cluster_ids.reshape(1, nodes)
    lists = halo_lists.reshape(1, 2 * side)
    src = edge_sources.reshape(cells, K).T
    bias = b_edge_in.reshape(1, width)

    def pool(x):
        keep, send = call(
            pool_body, (sds((half, width), F32),) * 2, (ids, x), 2 * nodes * cells * width,
            scratch=(pltpu.VMEM(ids.shape, jnp.int32), pltpu.VMEM(x.shape, BF), pltpu.SemaphoreType.DMA((2,))),
            anywhere=2,
        )
        return keep + swap(send, "fine", 0)

    def across(part):
        for bit in range(1, fine_bits):
            part = part + swap(part.astype(BF), "fine", bit).astype(F32)
        return part.astype(BF)

    def halos(part):
        to_right, to_left = call(
            halo_body, (sds((side, width), BF),) * 2, (part.astype(BF), lists), 4 * side * half * width
        )
        arrived = [send_owner(to_right, 1, d) for d in range(fines // 2)]
        arrived += [send_owner(to_left, -1, d) for d in range(fines // 2)]
        own = call(
            halo_sum_body, (sds((2 * side, width), BF),), arrived, 0,
            scratch=(pltpu.VMEM((fines // 2, side, width), F32),),
        )[0]
        return own, swap(own, "fine", 0)

    part_p = pool(node_feats)
    own_p = across(part_p)
    own_halo, other_halo = halos(part_p)
    own_g = across(pool(grad_out))
    other_p = swap(own_p, "fine", 0)
    other_g = swap(own_g, "fine", 0)
    ext, hid, slope = call(
        forward_body,
        (sds((rows, width), BF), sds((cells, width), F32), sds((K * cells, width), F32)),
        (own_p, other_p, own_halo, other_halo, src, w_edge_in, bias),
        2 * K * cells * width * (rows + width),
        vmem=40,
        scratch=(pltpu.VMEM((cells, width), BF),),
    )
    per = 4 * width // fines
    share = per // coarses
    block = -(-(share + 2) // PACK) * PACK
    each = -(-share // PACK) * PACK
    gs, ga, gn, back_l, back_r, send = call(
        backward_body,
        (
            sds((rows, width), F32), sds((cells, width), F32), sds((cells, width), BF),
            sds((side, width), BF), sds((side, width), BF), sds((coarses * block, width), BF),
        ),
        (own_g, other_g, ext, hid, slope, src, w_edge_in, w_edge_out, w_unpool),
        2 * K * cells * width * rows,
        vmem=40,
        scratch=(
            pltpu.VMEM((cells, width), BF), pltpu.VMEM((cells * K, width), BF), pltpu.VMEM((per, width), F32),
        ),
    )
    recv = lax.all_to_all(send, "coarse", 0, 0, tiled=True)
    spread, bias_sum = call(
        functools.partial(share_body, share=share),
        (sds((coarses * each, width), BF), sds((PACK, width), BF)),
        (recv,),
        0,
    )
    part = lax.all_to_all(spread, "coarse", 0, 0, tiled=True)
    part = call(join_body, (sds((coarses * each + PACK, width), BF),), (part, bias_sum), 0)[0]

    from_r = shift(back_l, "coarse", -1)
    from_l = shift(back_r, "coarse", 1)
    pool_grad = call(
        pooled_grad_body, (sds((cells, width), F32),), (gs, ga, gn, w_edge_in), 4 * cells * width * width
    )[0]
    grad_feats = call(
        feats_body,
        (sds((nodes, width), BF),),
        (pool_grad, from_r, from_l, lists, ids, grad_out),
        2 * nodes * cells * width,
        vmem=24,
        scratch=(pltpu.VMEM((cells, width), BF),),
    )[0]

    for bit in range(1, fine_bits):
        part = merge(part, "fine", bit)
    other = swap(part, "fine", 0)
    total_cells = cells * coarses
    scales = dict(edge_scale=float(total_cells * K) ** -0.5, cell_scale=float(total_cells) ** -0.5)
    grad_w1, grad_b, grad_wo, grad_up = call(
        functools.partial(weights_body, per=per, share=share, **scales),
        (
            sds((2 * width, width), F32), sds((1, width), F32), sds((width, width), F32), sds((width, width), F32),
        ),
        (part, other),
        0,
    )
    return grad_feats, grad_w1, grad_b.reshape(width), grad_wo, grad_up


def solution(mesh):
    both = ("coarse", "fine")
    return jax.shard_map(
        local,
        mesh=mesh,
        in_specs=(P(both, None), P(both, None), P(both), P("coarse"), P("coarse"), P(), P(), P(), P()),
        out_specs=(P(both, None), P(), P(), P(), P()),
        check_vma=False,
    )
```

```python
import functools

import jax
import jax.numpy as jnp
from jax import lax
from jax.experimental import pallas as pl
from jax.experimental.pallas import tpu as pltpu
from jax.sharding import PartitionSpec as P

K = 4
BF = jnp.bfloat16
F32 = jnp.float32
LANES = 128
PACK = 16
MIB = 1 << 20


def dot(a, b):
    return jnp.dot(a, b, preferred_element_type=F32)


def dot_nt(a, b):
    return lax.dot_general(a, b, (((1,), (1,)), ((), ())), preferred_element_type=F32)


def dot_tn(a, b):
    return lax.dot_general(a, b, (((0,), (0,)), ((), ())), preferred_element_type=F32)


def bits_of(count):
    assert count > 1 and count & (count - 1) == 0
    return count.bit_length() - 1


def swap(x, axis, bit):
    count = lax.axis_size(axis)
    return lax.ppermute(x, axis, [(i, i ^ (1 << bit)) for i in range(count)])


def swap_both(x):
    owners, fines = lax.axis_size("coarse"), lax.axis_size("fine")
    pairs = [(g * fines + f, (g ^ 1) * fines + (f ^ 2)) for g in range(owners) for f in range(fines)]
    return lax.ppermute(x, ("coarse", "fine"), pairs)


def send_sides(x, flip=0):
    owners, fines = lax.axis_size("coarse"), lax.axis_size("fine")
    pairs = [
        (g * fines + f, (g + 1 - 2 * (f % 2)) % owners * fines + (f ^ (2 * flip)))
        for g in range(owners)
        for f in range(fines)
    ]
    return lax.ppermute(x, ("coarse", "fine"), pairs)


def call(body, outs, args, flops, vmem=16, scratch=(), after=()):
    moved = sum(a.size * a.dtype.itemsize for a in (*args, *outs))
    count, waited = len(args), len(after)

    def kernel(*refs):
        body(*refs[:count], *refs[count + waited :])

    specs = [pl.BlockSpec(memory_space=pltpu.VMEM)] * count + [pl.BlockSpec(memory_space=pl.ANY)] * waited
    return pl.pallas_call(
        kernel,
        out_shape=outs,
        in_specs=specs,
        scratch_shapes=scratch,
        compiler_params=pltpu.CompilerParams(vmem_limit_bytes=vmem * MIB),
        cost_estimate=pl.CostEstimate(flops=int(flops), bytes_accessed=int(moved), transcendentals=0),
    )(*args, *after)


def sds(shape, dtype):
    return jax.ShapeDtypeStruct(shape, dtype)


def column(row):
    blocks = [
        jnp.broadcast_to(row[:, i : i + LANES], (LANES, LANES)).T
        for i in range(0, row.shape[1], LANES)
    ]
    return blocks[0] if len(blocks) == 1 else jnp.concatenate(blocks, axis=0)


def hot_rows(row, width):
    ids = column(row)
    ids = jnp.concatenate([ids] * (width // LANES), axis=1)
    lane = lax.broadcasted_iota(jnp.int32, ids.shape, 1)
    return jnp.where(lane == ids, 1.0, 0.0).astype(BF)


def hot_columns(row, height, start=0):
    shape = (height, row.shape[1])
    at = lax.broadcasted_iota(jnp.int32, shape, 0)
    return jnp.where(at == row - start, 1.0, 0.0).astype(BF)


def pool_body(ids_ref, x_ref, keep_ref, send_ref):
    half = keep_ref.shape[0]
    core = lax.axis_index("fine") % 2
    ids = ids_ref[...]
    x = x_ref[...]
    step = min(256, half)
    for out_ref, base in ((send_ref, (1 - core) * half), (keep_ref, core * half)):
        for t in range(0, half, step):
            out_ref[t : t + step, :] = dot(hot_columns(ids, step, base + t), x)


def pick_body(part_ref, lists_ref, out_ref):
    half = part_ref.shape[0]
    core = lax.axis_index("fine") % 2
    out_ref[...] = dot(hot_rows(lists_ref[...] - core * half, half), part_ref[...]).astype(BF)


def side_body(own, other, out_ref):
    side = out_ref.shape[0]
    core = lax.axis_index("fine") % 2
    at = pl.ds(pl.multiple_of(core * side, side), side)
    out_ref[...] = own[at, :] + other[at, :]


def halo_sum_body(*refs):
    *parts, out_ref, slots = refs
    chip = lax.axis_index("fine") // 2
    for offset, part in enumerate(parts):
        slots[chip ^ offset] = part[...].astype(F32)
    total = slots[0]
    for i in range(1, len(parts)):
        total = total + slots[i]
    out_ref[...] = total.astype(BF)


def chip_body(keep, recv, part_ref, send_ref):
    total = keep[...] + recv[...]
    part_ref[...] = total
    send_ref[...] = total.astype(BF)


def across_body(part, recv, *out_refs):
    total = part[...] + recv[...].astype(F32)
    for ref in out_refs:
        ref[...] = total.astype(ref.dtype)


def core_order(half):
    core = lax.axis_index("fine") % 2
    at_own = pl.ds(pl.multiple_of(core * half, half), half)
    at_other = pl.ds(pl.multiple_of((1 - core) * half, half), half)
    return at_own, at_other


def forward_body(
    own_p, other_p, own_halo, other_halo, src_ref, w1_ref, b_ref,
    ext, hid, slope, feats, token_ref,
):
    half, width = own_p.shape
    cells = 2 * half
    rows = ext.shape[0]
    at_own, at_other = core_order(half)
    ext[at_own, :] = own_p[...]
    ext[at_other, :] = other_p[...]
    side = own_halo.shape[0]
    core = lax.axis_index("fine") % 2
    ext[pl.ds(pl.multiple_of(cells + core * side, PACK), side), :] = own_halo[...]
    ext[pl.ds(pl.multiple_of(cells + (1 - core) * side, PACK), side), :] = other_halo[...]
    token_ref[...] = jnp.zeros_like(token_ref)
    base = dot(ext[0:cells, :], w1_ref[0:width, :]) + b_ref[...].astype(F32)
    block = 512
    for k in range(K):
        for t in range(0, cells, block):
            part = src_ref[k : k + 1, t : t + block]
            at = k * cells + t
            feats[at : at + block, :] = dot(hot_rows(part, rows), ext[...]).astype(BF)
        at = slice(k * cells, (k + 1) * cells)
        pre = base + dot(feats[at, :], w1_ref[width : 2 * width, :])
        sig = 0.5 * jnp.tanh(0.5 * pre) + 0.5
        hidden = pre * sig
        hid[...] = hidden if k == 0 else hid[...] + hidden
        slope[at, :] = sig + hidden * (1.0 - sig)


def split(x):
    high = x.astype(BF)
    return high, (x - high.astype(F32)).astype(BF)


def bias_rows(bias):
    high, low = (part.astype(F32) for part in split(bias))
    at = lax.broadcasted_iota(jnp.int32, (PACK, bias.shape[1]), 0)
    return jnp.where(at == 0, high, jnp.where(at == 1, low, 0.0)).astype(BF), high + low


def axis_bit(axis, bit):
    return lax.rem(lax.axis_index(axis) // (1 << bit), 2)


def emit(total_ref, bias, bit, keep_ref, send_ref, bias_ref):
    n = keep_ref.shape[0]
    if n == total_ref.shape[0]:
        sent = total_ref[...].astype(BF)
        keep_ref[...] = sent.astype(F32)
    else:
        side = axis_bit("coarse", bit)
        keep_ref[...] = total_ref[pl.ds(pl.multiple_of(side * n, n), n), :]
        sent = total_ref[pl.ds(pl.multiple_of((1 - side) * n, n), n), :].astype(BF)
    rows, bias = bias_rows(bias)
    send_ref[0:n, :] = sent
    send_ref[n : n + PACK, :] = rows
    bias_ref[...] = jnp.broadcast_to(bias, bias_ref.shape)


def backward_body(
    own_g, other_g, ext, feats, hid, slope, wo_ref, wu_ref,
    act, ga_ref, gn_ref, keep_ref, send_ref, bias_ref,
    gsum, total,
):
    half, width = own_g.shape
    cells = 2 * half
    fine = lax.axis_index("fine")
    at_own, at_other = core_order(half)
    gsum[at_own, :] = own_g[...]
    gsum[at_other, :] = other_g[...]
    gn = dot_nt(gsum[...], wu_ref[...]).astype(BF)
    gn_ref[...] = gn
    grad = dot_nt(gn, wo_ref[...])
    ga = jnp.zeros((cells, width), F32)
    for k in range(K):
        at = slice(k * cells, (k + 1) * cells)
        part = (grad * slope[at, :]).astype(BF)
        act[at, :] = part
        ga = ga + part.astype(F32)
    ga_ref[...] = ga

    fines = lax.axis_size("fine")
    per = 4 * width // fines
    n = min(per, width)
    for index in range(fines):

        @pl.when(fine == index)
        def _():
            for r in range(0, per, n):
                which, first = divmod(index * per + r, width)
                cols = slice(first, first + n)
                if which == 0:
                    high, low = split(ga_ref[...])
                    left = ext[0:cells, cols]
                    out = dot_tn(left, high) + dot_tn(left, low)
                elif which == 1:
                    out = dot_tn(feats[:, cols], act[...])
                elif which == 2:
                    high, low = split(hid[:, cols])
                    out = dot_tn(high, gn_ref[...]) + dot_tn(low, gn_ref[...])
                else:
                    high, low = split(hid[...])
                    agg = dot(high, wo_ref[:, cols]) + dot(low, wo_ref[:, cols])
                    new = (ext[0:cells, cols].astype(F32) + agg).astype(BF)
                    out = dot_tn(new, gsum[...])
                total[r : r + n, :] = out

    emit(total, jnp.sum(ga_ref[...], axis=0, keepdims=True), 0, keep_ref, send_ref, bias_ref)


def received_bias(recv, n):
    return recv[n : n + 1, :].astype(F32) + recv[n + 1 : n + 2, :].astype(F32)


def stage_body(keep_in, recv, bias_in, keep_ref, send_ref, bias_ref, total, *, bit):
    n = keep_in.shape[0]
    total[...] = keep_in[...] + recv[0:n, :].astype(F32)
    emit(total, bias_in[0:1, :] + received_bias(recv, n), bit, keep_ref, send_ref, bias_ref)


def end_body(keep_in, recv, bias_in, out_ref):
    n = keep_in.shape[0]
    out_ref[0:n, :] = (keep_in[...] + recv[0:n, :].astype(F32)).astype(BF)
    out_ref[n : n + PACK, :] = bias_rows(bias_in[0:1, :] + received_bias(recv, n))[0]


def scatter(act, src_ref, first, count):
    cells = src_ref.shape[1]
    out = jnp.zeros((count, act.shape[1]), F32)
    for k in range(K):
        hot = hot_columns(src_ref[k : k + 1, :], count, first)
        out += dot(hot, act[k * cells : (k + 1) * cells, :])
    return out


def back_body(act, src_ref, w1_ref, out_ref, both):
    side, width = out_ref.shape
    rows = scatter(act, src_ref, src_ref.shape[1], 2 * side)
    both[...] = dot_nt(rows.astype(BF), w1_ref[width : 2 * width, :])
    core = lax.axis_index("fine") % 2
    out_ref[...] = both[pl.ds(pl.multiple_of((1 - core) * side, side), side), :].astype(BF)


def cell_grad_body(act, src_ref, ga_ref, gn_ref, w1_ref, out_ref, *, first):
    count, width = out_ref.shape
    step = min(512, count)
    for r in range(0, count, step):
        at = slice(first + r, first + r + step)
        rows = scatter(act, src_ref, first + r, step)
        out_ref[r : r + step, :] = (
            gn_ref[at, :].astype(F32)
            + dot_nt(ga_ref[at, :].astype(BF), w1_ref[0:width, :])
            + dot_nt(rows.astype(BF), w1_ref[width : 2 * width, :])
        )


def merge_body(own, other, *rest, bit):
    n = own.shape[0]
    out_ref = rest[-1]
    side = axis_bit("fine", bit)
    out_ref[pl.ds(pl.multiple_of(side * n, PACK), n), :] = own[...]
    out_ref[pl.ds(pl.multiple_of((1 - side) * n, PACK), n), :] = other[...]


def square_body(own, by_owner, by_chip, by_both, out_ref):
    size = out_ref.shape[0] // 2
    n = own.shape[0] - PACK
    half, chip = axis_bit("coarse", 0), axis_bit("fine", 1)
    for block, i, j in ((own, half, chip), (by_owner, 1 - half, chip), (by_chip, half, 1 - chip), (by_both, 1 - half, 1 - chip)):
        out_ref[pl.ds(pl.multiple_of(j * size + i * n, PACK), n), :] = block[0:n, :]
    for block, j in ((own, chip), (by_chip, 1 - chip)):
        out_ref[pl.ds(pl.multiple_of(j * size + 2 * n, PACK), PACK), :] = block[n:, :]


def weights_body(own, other, w1_ref, gb_ref, wo_ref, up_ref, *, per, edge_scale, cell_scale):
    width = own.shape[1]
    core = lax.axis_index("fine") % 2
    outs = ((w1_ref, 0, edge_scale), (w1_ref, width, edge_scale), (wo_ref, 0, edge_scale), (up_ref, 0, cell_scale))
    size = per + PACK
    n = min(per, width)
    for index in range(lax.axis_size("fine")):
        at = slice((index // 2) * size, (index // 2 + 1) * size)
        value = jnp.where(core == index % 2, own[at, :].astype(F32), other[at, :].astype(F32))
        if index == 0:
            gb_ref[...] = (value[per : per + 1] + value[per + 1 : per + 2]) * edge_scale
        for r in range(0, per, n):
            which, row = divmod(index * per + r, width)
            out_ref, start, scale = outs[which]
            out_ref[start + row : start + row + n, :] = value[r : r + n] * scale


def feats_body(*refs):
    *pool_refs, own_back, other_back, lists_ref, ids_ref, grad_ref, out_ref, token_ref, table = refs
    token_ref[...] = jnp.zeros_like(token_ref)
    cells = table.shape[0]
    nodes = grad_ref.shape[0]
    lists = lists_ref[...]
    core = lax.axis_index("fine") % 2
    side = own_back.shape[0]
    returned = jnp.concatenate([own_back[...], other_back[...]], axis=0)
    first, second = lists[:, :side], lists[:, side:]
    lists = jnp.where(core == 0, jnp.concatenate([second, first], axis=1), lists)
    step = pool_refs[0].shape[0]
    for i, pool_ref in enumerate(pool_refs):
        add = dot(hot_columns(lists, step, i * step), returned)
        table[i * step : (i + 1) * step, :] = (pool_ref[...] + add).astype(BF)
    block = 256
    for t in range(0, nodes, block):
        rows = dot(hot_rows(ids_ref[:, t : t + block], cells), table[...])
        out_ref[t : t + block, :] = (grad_ref[t : t + block, :].astype(F32) + rows).astype(BF)


def local(
    node_feats, grad_out, cluster_ids, halo_lists, edge_sources, w_edge_in, b_edge_in, w_edge_out, w_unpool,
):
    nodes, width = node_feats.shape
    cells = edge_sources.shape[0] // K
    half = cells // 2
    side = halo_lists.shape[0] // 2
    rows = cells + 2 * side
    fines, coarses = lax.axis_size("fine"), lax.axis_size("coarse")
    fine_bits, coarse_bits = bits_of(fines), bits_of(coarses)
    ids = lax.rem(cluster_ids, cells).reshape(1, nodes)
    lists = halo_lists.reshape(1, 2 * side)
    src = edge_sources.reshape(cells, K).T
    bias = b_edge_in.reshape(1, width)

    def pool(x):
        keep, send = call(pool_body, (sds((half, width), F32),) * 2, (ids, x), 2 * nodes * cells * width)
        outs = (sds((half, width), F32), sds((half, width), BF))
        return call(chip_body, outs, (keep, swap(send, "fine", 0)), 0)

    def across(part, send, after=()):
        for bit in range(1, fine_bits):
            recv = swap(send, "fine", bit)
            last = bit == fine_bits - 1
            outs = (sds((half, width), BF),) if last else (sds((half, width), F32), sds((half, width), BF))
            part, send = (*call(across_body, outs, (part, recv), 0, after=after), None)[:2]
        return part

    part_p, send_p = pool(node_feats)
    part_g, send_g = pool(grad_out)
    picked = call(pick_body, (sds((2 * side, width), BF),), (send_p, lists), 0, after=(send_g,))[0]
    sent = call(side_body, (sds((side, width), BF),), (picked, swap(picked, "fine", 0)), 0)[0]
    own_halo = call(
        halo_sum_body, (sds((side, width), BF),), [send_sides(sent, d) for d in range(fines // 2)], 0,
        scratch=(pltpu.VMEM((fines // 2, side, width), F32),),
    )[0]
    own_p = across(part_p, send_p, after=(own_halo,))
    other_halo = swap(own_halo, "fine", 0)
    other_p = swap(own_p, "fine", 0)
    ext, hid, slope, feats, forward_token = call(
        forward_body,
        (
            sds((rows, width), BF), sds((cells, width), F32),
            sds((K * cells, width), F32), sds((K * cells, width), BF), sds((8, LANES), F32),
        ),
        (own_p, other_p, own_halo, other_halo, src, w_edge_in, bias),
        2 * K * cells * width * (rows + width),
        vmem=32,
    )
    own_g = across(part_g, send_g, after=(forward_token,))
    other_g = swap(own_g, "fine", 0)
    per = 4 * width // fines
    first = per // 2
    act, ga, gn, keep, send, bias_sum = call(
        backward_body,
        (
            sds((K * cells, width), BF), sds((cells, width), F32), sds((cells, width), BF),
            sds((first, width), F32), sds((first + PACK, width), BF), sds((8, width), F32),
        ),
        (own_g, other_g, ext, feats, hid, slope, w_edge_out, w_unpool),
        2 * K * cells * width * width,
        vmem=32,
        scratch=(pltpu.VMEM((cells, width), BF), pltpu.VMEM((per, width), F32)),
    )

    back = call(
        back_body, (sds((side, width), BF),), (act, src, w_edge_in), 4 * K * side * cells * width,
        scratch=(pltpu.VMEM((2 * side, width), F32),),
    )[0]
    own_back = send_sides(back)
    other_back = swap(own_back, "fine", 0)
    cell_grads = [
        call(
            functools.partial(cell_grad_body, first=at),
            (sds((half, width), F32),),
            (act, src, ga, gn, w_edge_in),
            2 * K * half * cells * width,
        )[0]
        for at in (0, half)
    ]
    grad_feats, feats_token = call(
        feats_body,
        (sds((nodes, width), BF), sds((8, LANES), F32)),
        (*cell_grads, own_back, other_back, lists, ids, grad_out),
        2 * nodes * cells * width,
        vmem=24,
        scratch=(pltpu.VMEM((cells, width), BF),),
    )

    after = {1: (back,), 2: (cell_grads[0],)}
    for bit in range(1, coarse_bits):
        recv = swap(send, "coarse", bit - 1)
        keep, send, bias_sum = call(
            functools.partial(stage_body, bit=bit),
            (sds((first, width), F32), sds((first + PACK, width), BF), sds((8, width), F32)),
            (keep, recv, bias_sum),
            0,
            scratch=(pltpu.VMEM((first, width), F32),),
            after=after.get(bit, ()),
        )
    recv = swap(send, "coarse", coarse_bits - 1)
    part = call(
        end_body, (sds((first + PACK, width), BF),), (keep, recv, bias_sum), 0,
        after=(cell_grads[1], other_back),
    )[0]
    near = [swap(part, "coarse", 0), swap(part, "fine", 1), swap_both(part)]
    part = call(
        square_body, (sds((2 * (per + PACK), width), BF),), (part, *near), 0, after=(feats_token,)
    )[0]
    for bit in range(2, fine_bits):
        other = swap(part, "fine", bit)
        body = functools.partial(merge_body, bit=bit)
        part = call(body, (sds((2 * part.shape[0], width), BF),), (part, other), 0)[0]
    other = swap(part, "fine", 0)
    total_cells = cells * coarses
    scales = dict(edge_scale=float(total_cells * K) ** -0.5, cell_scale=float(total_cells) ** -0.5)
    grad_w1, grad_b, grad_wo, grad_up = call(
        functools.partial(weights_body, per=per, **scales),
        (
            sds((2 * width, width), F32), sds((1, width), F32), sds((width, width), F32), sds((width, width), F32),
        ),
        (part, other),
        0,
    )
    return grad_feats, grad_w1, grad_b.reshape(width), grad_wo, grad_up


def solution(mesh):
    both = ("coarse", "fine")
    return jax.shard_map(
        local,
        mesh=mesh,
        in_specs=(P(both, None), P(both, None), P(both), P("coarse"), P("coarse"), P(), P(), P(), P()),
        out_specs=(P(both, None), P(), P(), P(), P()),
        check_vma=False,
    )
```

```python
import functools

import jax
import jax.numpy as jnp
from jax import lax
from jax.experimental import pallas as pl
from jax.experimental.pallas import tpu as pltpu
from jax.sharding import PartitionSpec as P

K = 4
BF = jnp.bfloat16
F32 = jnp.float32
LANES = 128
PACK = 16
MIB = 1 << 20


def dot(a, b):
    return jnp.dot(a, b, preferred_element_type=F32)


def dot_nt(a, b):
    return lax.dot_general(a, b, (((1,), (1,)), ((), ())), preferred_element_type=F32)


def dot_tn(a, b):
    return lax.dot_general(a, b, (((0,), (0,)), ((), ())), preferred_element_type=F32)


def bits_of(count):
    assert count > 1 and count & (count - 1) == 0
    return count.bit_length() - 1


def swap(x, axis, bit):
    count = lax.axis_size(axis)
    return lax.ppermute(x, axis, [(i, i ^ (1 << bit)) for i in range(count)])


def swap_both(x):
    owners, fines = lax.axis_size("coarse"), lax.axis_size("fine")
    pairs = [(g * fines + f, (g ^ 1) * fines + (f ^ 2)) for g in range(owners) for f in range(fines)]
    return lax.ppermute(x, ("coarse", "fine"), pairs)


def send_sides(x):
    owners, fines = lax.axis_size("coarse"), lax.axis_size("fine")
    pairs = [
        (g * fines + f, (g + 1 - 2 * (f % 2)) % owners * fines + f)
        for g in range(owners)
        for f in range(fines)
    ]
    return lax.ppermute(x, ("coarse", "fine"), pairs)


def call(body, outs, args, flops, vmem=16, scratch=(), after=()):
    moved = sum(a.size * a.dtype.itemsize for a in (*args, *outs)) if flops else 0
    count, waited = len(args), len(after)

    def kernel(*refs):
        body(*refs[:count], *refs[count + waited :])

    specs = [pl.BlockSpec(memory_space=pltpu.VMEM)] * count + [pl.BlockSpec(memory_space=pl.ANY)] * waited
    return pl.pallas_call(
        kernel,
        out_shape=outs,
        in_specs=specs,
        scratch_shapes=scratch,
        compiler_params=pltpu.CompilerParams(vmem_limit_bytes=vmem * MIB),
        cost_estimate=pl.CostEstimate(flops=int(flops), bytes_accessed=int(moved), transcendentals=0),
    )(*args, *after)


def sds(shape, dtype):
    return jax.ShapeDtypeStruct(shape, dtype)


def column(row):
    blocks = [
        jnp.broadcast_to(row[:, i : i + LANES], (LANES, LANES)).T
        for i in range(0, row.shape[1], LANES)
    ]
    return blocks[0] if len(blocks) == 1 else jnp.concatenate(blocks, axis=0)


def hot_rows(row, width):
    ids = column(row)
    ids = jnp.concatenate([ids] * (width // LANES), axis=1)
    lane = lax.broadcasted_iota(jnp.int32, ids.shape, 1)
    return jnp.where(lane == ids, 1.0, 0.0).astype(BF)


def hot_columns(row, height, start=0):
    shape = (height, row.shape[1])
    at = lax.broadcasted_iota(jnp.int32, shape, 0)
    return jnp.where(at == row - start, 1.0, 0.0).astype(BF)


def pool_body(ids_ref, x_ref, keep_ref, send_ref):
    half = keep_ref.shape[0]
    core = lax.axis_index("fine") % 2
    ids = ids_ref[...]
    x = x_ref[...]
    step = min(256, half)
    for out_ref, base in ((send_ref, (1 - core) * half), (keep_ref, core * half)):
        for t in range(0, half, step):
            out_ref[t : t + step, :] = dot(hot_columns(ids, step, base + t), x)


def pick_body(part_ref, lists_ref, out_ref):
    half = part_ref.shape[0]
    core = lax.axis_index("fine") % 2
    out_ref[...] = dot(hot_rows(lists_ref[...] - core * half, half), part_ref[...]).astype(BF)


def side_body(own, other, out_ref):
    side = out_ref.shape[0]
    core = lax.axis_index("fine") % 2
    at = pl.ds(pl.multiple_of(core * side, side), side)
    out_ref[...] = own[at, :] + other[at, :]


def copy_body(x, out_ref):
    out_ref[...] = x[...]


def chip_body(keep, recv, part_ref, send_ref):
    total = keep[...] + recv[...]
    part_ref[...] = total
    send_ref[...] = total.astype(BF)


def across_body(part, recv, *out_refs):
    total = part[...] + recv[...].astype(F32)
    for ref in out_refs:
        ref[...] = total.astype(ref.dtype)


def core_order(half):
    core = lax.axis_index("fine") % 2
    at_own = pl.ds(pl.multiple_of(core * half, half), half)
    at_other = pl.ds(pl.multiple_of((1 - core) * half, half), half)
    return at_own, at_other


def gather_body(own_p, other_p, src_ref, w1_ref, b_ref, table, base, feats, token_ref):
    half, width = own_p.shape
    cells = 2 * half
    at_own, at_other = core_order(half)
    table[at_own, :] = own_p[...]
    table[at_other, :] = other_p[...]
    token_ref[...] = jnp.zeros_like(token_ref)
    base[...] = dot(table[...], w1_ref[0:width, :]) + b_ref[...].astype(F32)
    block = 512
    for k in range(K):
        for t in range(0, cells, block):
            at = k * cells + t
            hot = hot_rows(src_ref[k : k + 1, t : t + block], cells)
            feats[at : at + block, :] = dot(hot, table[...]).astype(BF)


def forward_body(base, near, own_halo, other_halo, src_ref, w1_ref, hid, slope, feats, token_ref, halo):
    token_ref[...] = jnp.zeros_like(token_ref)
    cells, width = base.shape
    side = own_halo.shape[0]
    core = lax.axis_index("fine") % 2
    halo[pl.ds(pl.multiple_of(core * side, PACK), side), :] = own_halo[...]
    halo[pl.ds(pl.multiple_of((1 - core) * side, PACK), side), :] = other_halo[...]
    for k in range(K):
        at = slice(k * cells, (k + 1) * cells)
        far = dot(hot_rows(src_ref[k : k + 1, :] - cells, 2 * side), halo[...])
        rows = (near[at, :].astype(F32) + far).astype(BF)
        feats[at, :] = rows
        pre = base[...] + dot(rows, w1_ref[width : 2 * width, :])
        sig = 0.5 * jnp.tanh(0.5 * pre) + 0.5
        hidden = pre * sig
        hid[...] = hidden if k == 0 else hid[...] + hidden
        slope[at, :] = sig + hidden * (1.0 - sig)


def split(x):
    high = x.astype(BF)
    return high, (x - high.astype(F32)).astype(BF)


def bias_rows(bias):
    high, low = (part.astype(F32) for part in split(bias))
    at = lax.broadcasted_iota(jnp.int32, (PACK, bias.shape[1]), 0)
    return jnp.where(at == 0, high, jnp.where(at == 1, low, 0.0)).astype(BF), high + low


def axis_bit(axis, bit):
    return lax.rem(lax.axis_index(axis) // (1 << bit), 2)


def emit(total_ref, bias, bit, keep_ref, send_ref, bias_ref):
    n = keep_ref.shape[0]
    if n == total_ref.shape[0]:
        sent = total_ref[...].astype(BF)
        keep_ref[...] = sent.astype(F32)
    else:
        side = axis_bit("coarse", bit)
        keep_ref[...] = total_ref[pl.ds(pl.multiple_of(side * n, n), n), :]
        sent = total_ref[pl.ds(pl.multiple_of((1 - side) * n, n), n), :].astype(BF)
    rows, bias = bias_rows(bias)
    send_ref[0:n, :] = sent
    send_ref[n : n + PACK, :] = rows
    bias_ref[...] = jnp.broadcast_to(bias, bias_ref.shape)


def backward_body(
    own_g, other_g, table, feats, hid, slope, wo_ref, wu_ref,
    act, ga_ref, gn_ref, keep_ref, send_ref, bias_ref,
    gsum, total,
):
    half, width = own_g.shape
    cells = 2 * half
    fine = lax.axis_index("fine")
    at_own, at_other = core_order(half)
    gsum[at_own, :] = own_g[...]
    gsum[at_other, :] = other_g[...]
    gn = dot_nt(gsum[...], wu_ref[...]).astype(BF)
    gn_ref[...] = gn
    grad = dot_nt(gn, wo_ref[...])
    ga = jnp.zeros((cells, width), F32)
    for k in range(K):
        at = slice(k * cells, (k + 1) * cells)
        part = (grad * slope[at, :]).astype(BF)
        act[at, :] = part
        ga = ga + part.astype(F32)
    ga_ref[...] = ga

    fines = lax.axis_size("fine")
    per = 4 * width // fines
    n = min(per, width)
    for index in range(fines):

        @pl.when(fine == index)
        def _():
            for r in range(0, per, n):
                which, first = divmod(index * per + r, width)
                cols = slice(first, first + n)
                if which == 0:
                    high, low = split(ga_ref[...])
                    left = table[:, cols]
                    out = dot_tn(left, high) + dot_tn(left, low)
                elif which == 1:
                    out = dot_tn(feats[:, cols], act[...])
                elif which == 2:
                    high, low = split(hid[:, cols])
                    out = dot_tn(high, gn_ref[...]) + dot_tn(low, gn_ref[...])
                else:
                    high, low = split(hid[...])
                    agg = dot(high, wo_ref[:, cols]) + dot(low, wo_ref[:, cols])
                    new = (table[:, cols].astype(F32) + agg).astype(BF)
                    out = dot_tn(new, gsum[...])
                total[r : r + n, :] = out

    emit(total, jnp.sum(ga_ref[...], axis=0, keepdims=True), 0, keep_ref, send_ref, bias_ref)


def received_bias(recv, n):
    return recv[n : n + 1, :].astype(F32) + recv[n + 1 : n + 2, :].astype(F32)


def stage_body(keep_in, recv, bias_in, keep_ref, send_ref, bias_ref, total, *, bit):
    n = keep_in.shape[0]
    total[...] = keep_in[...] + recv[0:n, :].astype(F32)
    emit(total, bias_in[0:1, :] + received_bias(recv, n), bit, keep_ref, send_ref, bias_ref)


def end_body(keep_in, recv, bias_in, out_ref):
    n = keep_in.shape[0]
    out_ref[0:n, :] = (keep_in[...] + recv[0:n, :].astype(F32)).astype(BF)
    out_ref[n : n + PACK, :] = bias_rows(bias_in[0:1, :] + received_bias(recv, n))[0]


def scatter(act, src_ref, first, count):
    cells = src_ref.shape[1]
    out = jnp.zeros((count, act.shape[1]), F32)
    for k in range(K):
        hot = hot_columns(src_ref[k : k + 1, :], count, first)
        out += dot(hot, act[k * cells : (k + 1) * cells, :])
    return out


def back_body(act, src_ref, w1_ref, out_ref, both):
    side, width = out_ref.shape
    rows = scatter(act, src_ref, src_ref.shape[1], 2 * side)
    both[...] = dot_nt(rows.astype(BF), w1_ref[width : 2 * width, :])
    core = lax.axis_index("fine") % 2
    out_ref[...] = both[pl.ds(pl.multiple_of((1 - core) * side, side), side), :].astype(BF)


def cell_grad_body(act, src_ref, ga_ref, gn_ref, w1_ref, out_ref, *, first):
    count, width = out_ref.shape
    step = min(512, count)
    for r in range(0, count, step):
        at = slice(first + r, first + r + step)
        rows = scatter(act, src_ref, first + r, step)
        out_ref[r : r + step, :] = (
            gn_ref[at, :].astype(F32)
            + dot_nt(ga_ref[at, :].astype(BF), w1_ref[0:width, :])
            + dot_nt(rows.astype(BF), w1_ref[width : 2 * width, :])
        )


def merge_body(own, other, *rest, bit):
    n = own.shape[0]
    out_ref = rest[-1]
    side = axis_bit("fine", bit)
    out_ref[pl.ds(pl.multiple_of(side * n, PACK), n), :] = own[...]
    out_ref[pl.ds(pl.multiple_of((1 - side) * n, PACK), n), :] = other[...]


def square_body(own, by_owner, by_chip, by_both, out_ref):
    size = out_ref.shape[0] // 2
    n = own.shape[0] - PACK
    half, chip = axis_bit("coarse", 0), axis_bit("fine", 1)
    for block, i, j in ((own, half, chip), (by_owner, 1 - half, chip), (by_chip, half, 1 - chip), (by_both, 1 - half, 1 - chip)):
        out_ref[pl.ds(pl.multiple_of(j * size + i * n, PACK), n), :] = block[0:n, :]
    for block, j in ((own, chip), (by_chip, 1 - chip)):
        out_ref[pl.ds(pl.multiple_of(j * size + 2 * n, PACK), PACK), :] = block[n:, :]


def weights_body(own, other, w1_ref, gb_ref, wo_ref, up_ref, *, per, edge_scale, cell_scale):
    width = own.shape[1]
    core = lax.axis_index("fine") % 2
    outs = ((w1_ref, 0, edge_scale), (w1_ref, width, edge_scale), (wo_ref, 0, edge_scale), (up_ref, 0, cell_scale))
    size = per + PACK
    n = min(per, width)
    for index in range(lax.axis_size("fine")):
        at = slice((index // 2) * size, (index // 2 + 1) * size)
        value = jnp.where(core == index % 2, own[at, :].astype(F32), other[at, :].astype(F32))
        if index == 0:
            gb_ref[...] = (value[per : per + 1] + value[per + 1 : per + 2]) * edge_scale
        for r in range(0, per, n):
            which, row = divmod(index * per + r, width)
            out_ref, start, scale = outs[which]
            out_ref[start + row : start + row + n, :] = value[r : r + n] * scale


def feats_body(*refs):
    *pool_refs, own_back, other_back, lists_ref, ids_ref, grad_ref, out_ref, token_ref, table = refs
    token_ref[...] = jnp.zeros_like(token_ref)
    cells = table.shape[0]
    nodes = grad_ref.shape[0]
    lists = lists_ref[...]
    core = lax.axis_index("fine") % 2
    side = own_back.shape[0]
    returned = jnp.concatenate([own_back[...], other_back[...]], axis=0)
    first, second = lists[:, :side], lists[:, side:]
    lists = jnp.where(core == 0, jnp.concatenate([second, first], axis=1), lists)
    step = pool_refs[0].shape[0]
    for i, pool_ref in enumerate(pool_refs):
        add = dot(hot_columns(lists, step, i * step), returned)
        table[i * step : (i + 1) * step, :] = (pool_ref[...] + add).astype(BF)
    block = 256
    for t in range(0, nodes, block):
        rows = dot(hot_rows(ids_ref[:, t : t + block], cells), table[...])
        out_ref[t : t + block, :] = (grad_ref[t : t + block, :].astype(F32) + rows).astype(BF)


def local(
    node_feats, grad_out, cluster_ids, halo_lists, edge_sources, w_edge_in, b_edge_in, w_edge_out, w_unpool,
):
    nodes, width = node_feats.shape
    cells = edge_sources.shape[0] // K
    half = cells // 2
    side = halo_lists.shape[0] // 2
    fines, coarses = lax.axis_size("fine"), lax.axis_size("coarse")
    fine_bits, coarse_bits = bits_of(fines), bits_of(coarses)
    ids = lax.rem(cluster_ids, cells).reshape(1, nodes)
    lists = halo_lists.reshape(1, 2 * side)
    src = edge_sources.reshape(cells, K).T
    bias = b_edge_in.reshape(1, width)

    def pool(x):
        keep, send = call(pool_body, (sds((half, width), F32),) * 2, (ids, x), 2 * nodes * cells * width)
        outs = (sds((half, width), F32), sds((half, width), BF))
        return call(chip_body, outs, (keep, swap(send, "fine", 0)), 0)

    def across(part, send, after=()):
        for bit in range(1, fine_bits):
            recv = swap(send, "fine", bit)
            last = bit == fine_bits - 1
            outs = (sds((half, width), BF),) if last else (sds((half, width), F32), sds((half, width), BF))
            part, send = (*call(across_body, outs, (part, recv), 0, after=after), None)[:2]
        return part

    part_p, send_p = pool(node_feats)
    part_g, send_g = pool(grad_out)
    own_p = across(part_p, send_p, after=(src, bias))
    other_p = swap(own_p, "fine", 0)
    picked = call(pick_body, (sds((2 * side, width), BF),), (own_p, lists), 0)[0]
    sent = call(side_body, (sds((side, width), BF),), (picked, swap(picked, "fine", 0)), 0)[0]
    own_halo = send_sides(sent)
    table, base, near, gather_token = call(
        gather_body,
        (
            sds((cells, width), BF), sds((cells, width), F32),
            sds((K * cells, width), BF), sds((8, LANES), F32),
        ),
        (own_p, other_p, src, w_edge_in, bias),
        0,
        vmem=32,
        after=(sent,),
    )
    own_halo = call(copy_body, (sds((side, width), BF),), (own_halo,), 0, after=(gather_token,))[0]
    other_halo = swap(own_halo, "fine", 0)
    hid, slope, feats, forward_token = call(
        forward_body,
        (
            sds((cells, width), F32), sds((K * cells, width), F32),
            sds((K * cells, width), BF), sds((8, LANES), F32),
        ),
        (base, near, own_halo, other_halo, src, w_edge_in),
        0,
        vmem=32,
        scratch=(pltpu.VMEM((2 * side, width), BF),),
    )
    own_g = across(part_g, send_g, after=(forward_token,))
    other_g = swap(own_g, "fine", 0)
    per = 4 * width // fines
    first = per // 2
    act, ga, gn, keep, send, bias_sum = call(
        backward_body,
        (
            sds((K * cells, width), BF), sds((cells, width), F32), sds((cells, width), BF),
            sds((first, width), F32), sds((first + PACK, width), BF), sds((8, width), F32),
        ),
        (own_g, other_g, table, feats, hid, slope, w_edge_out, w_unpool),
        2 * K * cells * width * width,
        vmem=32,
        scratch=(pltpu.VMEM((cells, width), BF), pltpu.VMEM((per, width), F32)),
    )

    back = call(
        back_body, (sds((side, width), BF),), (act, src, w_edge_in), 4 * K * side * cells * width,
        scratch=(pltpu.VMEM((2 * side, width), F32),),
    )[0]
    own_back = send_sides(back)
    other_back = swap(own_back, "fine", 0)
    cell_grads = [
        call(
            functools.partial(cell_grad_body, first=at),
            (sds((half, width), F32),),
            (act, src, ga, gn, w_edge_in),
            2 * K * half * cells * width,
        )[0]
        for at in (0, half)
    ]
    grad_feats, feats_token = call(
        feats_body,
        (sds((nodes, width), BF), sds((8, LANES), F32)),
        (*cell_grads, own_back, other_back, lists, ids, grad_out),
        2 * nodes * cells * width,
        vmem=24,
        scratch=(pltpu.VMEM((cells, width), BF),),
    )

    after = {1: (back,), 2: (cell_grads[0],)}
    for bit in range(1, coarse_bits):
        recv = swap(send, "coarse", bit - 1)
        keep, send, bias_sum = call(
            functools.partial(stage_body, bit=bit),
            (sds((first, width), F32), sds((first + PACK, width), BF), sds((8, width), F32)),
            (keep, recv, bias_sum),
            0,
            scratch=(pltpu.VMEM((first, width), F32),),
            after=after.get(bit, ()),
        )
    recv = swap(send, "coarse", coarse_bits - 1)
    part = call(
        end_body, (sds((first + PACK, width), BF),), (keep, recv, bias_sum), 0,
        after=(cell_grads[1], other_back),
    )[0]
    near = [swap(part, "coarse", 0), swap(part, "fine", 1), swap_both(part)]
    part = call(
        square_body, (sds((2 * (per + PACK), width), BF),), (part, *near), 0, after=(feats_token,)
    )[0]
    for bit in range(2, fine_bits):
        other = swap(part, "fine", bit)
        body = functools.partial(merge_body, bit=bit)
        part = call(body, (sds((2 * part.shape[0], width), BF),), (part, other), 0)[0]
    other = swap(part, "fine", 0)
    total_cells = cells * coarses
    scales = dict(edge_scale=float(total_cells * K) ** -0.5, cell_scale=float(total_cells) ** -0.5)
    grad_w1, grad_b, grad_wo, grad_up = call(
        functools.partial(weights_body, per=per, **scales),
        (
            sds((2 * width, width), F32), sds((1, width), F32), sds((width, width), F32), sds((width, width), F32),
        ),
        (part, other),
        0,
    )
    return grad_feats, grad_w1, grad_b.reshape(width), grad_wo, grad_up


def solution(mesh):
    both = ("coarse", "fine")
    return jax.shard_map(
        local,
        mesh=mesh,
        in_specs=(P(both, None), P(both, None), P(both), P("coarse"), P("coarse"), P(), P(), P(), P()),
        out_specs=(P(both, None), P(), P(), P(), P()),
        check_vma=False,
    )
```

```python
import functools

import jax
import jax.numpy as jnp
from jax import lax
from jax.experimental import pallas as pl
from jax.experimental.pallas import tpu as pltpu
from jax.sharding import PartitionSpec as P

K = 4
BF = jnp.bfloat16
F32 = jnp.float32
LANES = 128
PACK = 16
MIB = 1 << 20


def dot(a, b):
    return jnp.dot(a, b, preferred_element_type=F32)


def dot_nt(a, b):
    return lax.dot_general(a, b, (((1,), (1,)), ((), ())), preferred_element_type=F32)


def dot_tn(a, b):
    return lax.dot_general(a, b, (((0,), (0,)), ((), ())), preferred_element_type=F32)


def bits_of(count):
    assert count > 1 and count & (count - 1) == 0
    return count.bit_length() - 1


def swap(x, axis, bit):
    count = lax.axis_size(axis)
    return lax.ppermute(x, axis, [(i, i ^ (1 << bit)) for i in range(count)])


def swap_both(x):
    owners, fines = lax.axis_size("coarse"), lax.axis_size("fine")
    pairs = [(g * fines + f, (g ^ 1) * fines + (f ^ 2)) for g in range(owners) for f in range(fines)]
    return lax.ppermute(x, ("coarse", "fine"), pairs)


def send_sides(x, flip=0):
    owners, fines = lax.axis_size("coarse"), lax.axis_size("fine")
    pairs = [
        (g * fines + f, (g + 1 - 2 * (f % 2)) % owners * fines + (f ^ (2 * flip)))
        for g in range(owners)
        for f in range(fines)
    ]
    return lax.ppermute(x, ("coarse", "fine"), pairs)


def call(body, outs, args, flops, vmem=16, scratch=(), after=()):
    moved = sum(a.size * a.dtype.itemsize for a in (*args, *outs)) if flops else 0
    count, waited = len(args), len(after)

    def kernel(*refs):
        body(*refs[:count], *refs[count + waited :])

    specs = [pl.BlockSpec(memory_space=pltpu.VMEM)] * count + [pl.BlockSpec(memory_space=pl.ANY)] * waited
    return pl.pallas_call(
        kernel,
        out_shape=outs,
        in_specs=specs,
        scratch_shapes=scratch,
        compiler_params=pltpu.CompilerParams(vmem_limit_bytes=vmem * MIB),
        cost_estimate=pl.CostEstimate(flops=int(flops), bytes_accessed=int(moved), transcendentals=0),
    )(*args, *after)


def sds(shape, dtype):
    return jax.ShapeDtypeStruct(shape, dtype)


def column(row):
    blocks = [
        jnp.broadcast_to(row[:, i : i + LANES], (LANES, LANES)).T
        for i in range(0, row.shape[1], LANES)
    ]
    return blocks[0] if len(blocks) == 1 else jnp.concatenate(blocks, axis=0)


def hot_rows(row, width):
    ids = column(row)
    ids = jnp.concatenate([ids] * (width // LANES), axis=1)
    lane = lax.broadcasted_iota(jnp.int32, ids.shape, 1)
    return jnp.where(lane == ids, 1.0, 0.0).astype(BF)


def hot_columns(row, height, start=0):
    shape = (height, row.shape[1])
    at = lax.broadcasted_iota(jnp.int32, shape, 0)
    return jnp.where(at == row - start, 1.0, 0.0).astype(BF)


def pool_body(ids_ref, x_ref, keep_ref, send_ref):
    half = keep_ref.shape[0]
    core = lax.axis_index("fine") % 2
    ids = ids_ref[...]
    x = x_ref[...]
    step = min(256, half)
    for out_ref, base in ((send_ref, (1 - core) * half), (keep_ref, core * half)):
        for t in range(0, half, step):
            out_ref[t : t + step, :] = dot(hot_columns(ids, step, base + t), x)


def pick_body(part_ref, lists_ref, out_ref):
    half = part_ref.shape[0]
    core = lax.axis_index("fine") % 2
    out_ref[...] = dot(hot_rows(lists_ref[...] - core * half, half), part_ref[...]).astype(BF)


def side_body(own, other, out_ref):
    side = out_ref.shape[0]
    core = lax.axis_index("fine") % 2
    at = pl.ds(pl.multiple_of(core * side, side), side)
    out_ref[...] = own[at, :] + other[at, :]


def halo_sum_body(*refs):
    *parts, out_ref, slots = refs
    chip = lax.axis_index("fine") // 2
    for offset, part in enumerate(parts):
        slots[chip ^ offset] = part[...].astype(F32)
    total = slots[0]
    for i in range(1, len(parts)):
        total = total + slots[i]
    out_ref[...] = total.astype(BF)


def chip_body(keep, recv, part_ref, send_ref):
    total = keep[...] + recv[...]
    part_ref[...] = total
    send_ref[...] = total.astype(BF)


def across_body(part, recv, *out_refs):
    total = part[...] + recv[...].astype(F32)
    for ref in out_refs:
        ref[...] = total.astype(ref.dtype)


def core_order(half):
    core = lax.axis_index("fine") % 2
    at_own = pl.ds(pl.multiple_of(core * half, half), half)
    at_other = pl.ds(pl.multiple_of((1 - core) * half, half), half)
    return at_own, at_other


def extend_body(*refs):
    *others, own_p, own_halo, other_halo, w1_ref, b_ref, ext, base = refs
    half, width = own_p.shape
    cells = 2 * half
    side = own_halo.shape[0]
    core = lax.axis_index("fine") % 2
    ext[pl.ds(pl.multiple_of(core * half, half), half), :] = own_p[...]
    n = half // len(others)
    for i, other in enumerate(others):
        ext[pl.ds(pl.multiple_of((1 - core) * half + i * n, n), n), :] = other[...]
    ext[pl.ds(pl.multiple_of(cells + core * side, PACK), side), :] = own_halo[...]
    ext[pl.ds(pl.multiple_of(cells + (1 - core) * side, PACK), side), :] = other_halo[...]
    base[...] = dot(ext[0:cells, :], w1_ref[0:width, :]) + b_ref[...].astype(F32)


def forward_body(ext, base, src_ref, w1_ref, hid, slope, feats, token_ref, *, first):
    cells, width = base.shape
    rows = ext.shape[0]
    token_ref[...] = jnp.zeros_like(token_ref)
    block = 512
    for i in range(slope.shape[0] // cells):
        for t in range(0, cells, block):
            part = src_ref[first + i : first + i + 1, t : t + block]
            at = i * cells + t
            feats[at : at + block, :] = dot(hot_rows(part, rows), ext[...]).astype(BF)
        at = slice(i * cells, (i + 1) * cells)
        pre = base[...] + dot(feats[at, :], w1_ref[width : 2 * width, :])
        sig = 0.5 * jnp.tanh(0.5 * pre) + 0.5
        hidden = pre * sig
        hid[...] = hidden if i == 0 else hid[...] + hidden
        slope[at, :] = sig + hidden * (1.0 - sig)


def split(x):
    high = x.astype(BF)
    return high, (x - high.astype(F32)).astype(BF)


def bias_rows(bias):
    high, low = (part.astype(F32) for part in split(bias))
    at = lax.broadcasted_iota(jnp.int32, (PACK, bias.shape[1]), 0)
    return jnp.where(at == 0, high, jnp.where(at == 1, low, 0.0)).astype(BF), high + low


def axis_bit(axis, bit):
    return lax.rem(lax.axis_index(axis) // (1 << bit), 2)


def emit(total_ref, bias, bit, keep_ref, send_ref, bias_ref):
    n = keep_ref.shape[0]
    if n == total_ref.shape[0]:
        sent = total_ref[...].astype(BF)
        keep_ref[...] = sent.astype(F32)
    else:
        side = axis_bit("coarse", bit)
        keep_ref[...] = total_ref[pl.ds(pl.multiple_of(side * n, n), n), :]
        sent = total_ref[pl.ds(pl.multiple_of((1 - side) * n, n), n), :].astype(BF)
    rows, bias = bias_rows(bias)
    send_ref[0:n, :] = sent
    send_ref[n : n + PACK, :] = rows
    bias_ref[...] = jnp.broadcast_to(bias, bias_ref.shape)


def backward_body(
    own_g, other_g, ext, hid_1, slope_1, feats_1, hid_2, slope_2, feats_2, wo_ref, wu_ref,
    act, ga_ref, gn_ref, keep_ref, send_ref, bias_ref,
    gsum, total,
):
    half, width = own_g.shape
    cells = 2 * half
    fine = lax.axis_index("fine")
    at_own, at_other = core_order(half)
    gsum[at_own, :] = own_g[...]
    gsum[at_other, :] = other_g[...]
    gn = dot_nt(gsum[...], wu_ref[...]).astype(BF)
    gn_ref[...] = gn
    grad = dot_nt(gn, wo_ref[...])
    ga = jnp.zeros((cells, width), F32)
    for k in range(K):
        at = slice(k * cells, (k + 1) * cells)
        slope, here = (slope_1, k) if k < K // 2 else (slope_2, k - K // 2)
        part = (grad * slope[here * cells : (here + 1) * cells, :]).astype(BF)
        act[at, :] = part
        ga = ga + part.astype(F32)
    ga_ref[...] = ga

    fines = lax.axis_size("fine")
    per = 4 * width // fines
    n = min(per, width)
    for index in range(fines):

        @pl.when(fine == index)
        def _():
            for r in range(0, per, n):
                which, first = divmod(index * per + r, width)
                cols = slice(first, first + n)
                if which == 0:
                    high, low = split(ga_ref[...])
                    left = ext[0:cells, cols]
                    out = dot_tn(left, high) + dot_tn(left, low)
                elif which == 1:
                    n_1 = feats_1.shape[0]
                    out = dot_tn(feats_1[:, cols], act[0:n_1, :]) + dot_tn(feats_2[:, cols], act[n_1:, :])
                elif which == 2:
                    high, low = split(hid_1[:, cols] + hid_2[:, cols])
                    out = dot_tn(high, gn_ref[...]) + dot_tn(low, gn_ref[...])
                else:
                    high, low = split(hid_1[...] + hid_2[...])
                    agg = dot(high, wo_ref[:, cols]) + dot(low, wo_ref[:, cols])
                    new = (ext[0:cells, cols].astype(F32) + agg).astype(BF)
                    out = dot_tn(new, gsum[...])
                total[r : r + n, :] = out

    emit(total, jnp.sum(ga_ref[...], axis=0, keepdims=True), 0, keep_ref, send_ref, bias_ref)


def received_bias(recv, n):
    return recv[n : n + 1, :].astype(F32) + recv[n + 1 : n + 2, :].astype(F32)


def stage_body(keep_in, recv, bias_in, keep_ref, send_ref, bias_ref, total, *, bit):
    n = keep_in.shape[0]
    total[...] = keep_in[...] + recv[0:n, :].astype(F32)
    emit(total, bias_in[0:1, :] + received_bias(recv, n), bit, keep_ref, send_ref, bias_ref)


def end_body(keep_in, recv, bias_in, out_ref):
    n = keep_in.shape[0]
    out_ref[0:n, :] = (keep_in[...] + recv[0:n, :].astype(F32)).astype(BF)
    out_ref[n : n + PACK, :] = bias_rows(bias_in[0:1, :] + received_bias(recv, n))[0]


def scatter(act, src_ref, first, count):
    cells = src_ref.shape[1]
    out = jnp.zeros((count, act.shape[1]), F32)
    for k in range(K):
        hot = hot_columns(src_ref[k : k + 1, :], count, first)
        out += dot(hot, act[k * cells : (k + 1) * cells, :])
    return out


def back_body(act, src_ref, w1_ref, out_ref, both):
    side, width = out_ref.shape
    rows = scatter(act, src_ref, src_ref.shape[1], 2 * side)
    both[...] = dot_nt(rows.astype(BF), w1_ref[width : 2 * width, :])
    core = lax.axis_index("fine") % 2
    out_ref[...] = both[pl.ds(pl.multiple_of((1 - core) * side, side), side), :].astype(BF)


def cell_grad_body(act, src_ref, ga_ref, gn_ref, w1_ref, out_ref, *, first):
    count, width = out_ref.shape
    step = min(512, count)
    for r in range(0, count, step):
        at = slice(first + r, first + r + step)
        rows = scatter(act, src_ref, first + r, step)
        out_ref[r : r + step, :] = (
            gn_ref[at, :].astype(F32)
            + dot_nt(ga_ref[at, :].astype(BF), w1_ref[0:width, :])
            + dot_nt(rows.astype(BF), w1_ref[width : 2 * width, :])
        )


def merge_body(own, other, *rest, bit):
    n = own.shape[0]
    out_ref = rest[-1]
    side = axis_bit("fine", bit)
    out_ref[pl.ds(pl.multiple_of(side * n, PACK), n), :] = own[...]
    out_ref[pl.ds(pl.multiple_of((1 - side) * n, PACK), n), :] = other[...]


def square_body(own, by_owner, by_chip, by_both, out_ref):
    size = out_ref.shape[0] // 2
    n = own.shape[0] - PACK
    half, chip = axis_bit("coarse", 0), axis_bit("fine", 1)
    for block, i, j in ((own, half, chip), (by_owner, 1 - half, chip), (by_chip, half, 1 - chip), (by_both, 1 - half, 1 - chip)):
        out_ref[pl.ds(pl.multiple_of(j * size + i * n, PACK), n), :] = block[0:n, :]
    for block, j in ((own, chip), (by_chip, 1 - chip)):
        out_ref[pl.ds(pl.multiple_of(j * size + 2 * n, PACK), PACK), :] = block[n:, :]


def weights_body(own, other, w1_ref, gb_ref, wo_ref, up_ref, *, per, edge_scale, cell_scale):
    width = own.shape[1]
    core = lax.axis_index("fine") % 2
    outs = ((w1_ref, 0, edge_scale), (w1_ref, width, edge_scale), (wo_ref, 0, edge_scale), (up_ref, 0, cell_scale))
    size = per + PACK
    n = min(per, width)
    for index in range(lax.axis_size("fine")):
        at = slice((index // 2) * size, (index // 2 + 1) * size)
        value = jnp.where(core == index % 2, own[at, :].astype(F32), other[at, :].astype(F32))
        if index == 0:
            gb_ref[...] = (value[per : per + 1] + value[per + 1 : per + 2]) * edge_scale
        for r in range(0, per, n):
            which, row = divmod(index * per + r, width)
            out_ref, start, scale = outs[which]
            out_ref[start + row : start + row + n, :] = value[r : r + n] * scale


def feats_body(*refs):
    *pool_refs, own_back, other_back, lists_ref, ids_ref, grad_ref, out_ref, token_ref, table = refs
    token_ref[...] = jnp.zeros_like(token_ref)
    cells = table.shape[0]
    nodes = grad_ref.shape[0]
    lists = lists_ref[...]
    core = lax.axis_index("fine") % 2
    side = own_back.shape[0]
    returned = jnp.concatenate([own_back[...], other_back[...]], axis=0)
    first, second = lists[:, :side], lists[:, side:]
    lists = jnp.where(core == 0, jnp.concatenate([second, first], axis=1), lists)
    step = pool_refs[0].shape[0]
    for i, pool_ref in enumerate(pool_refs):
        add = dot(hot_columns(lists, step, i * step), returned)
        table[i * step : (i + 1) * step, :] = (pool_ref[...] + add).astype(BF)
    block = 256
    for t in range(0, nodes, block):
        rows = dot(hot_rows(ids_ref[:, t : t + block], cells), table[...])
        out_ref[t : t + block, :] = (grad_ref[t : t + block, :].astype(F32) + rows).astype(BF)


def local(
    node_feats, grad_out, cluster_ids, halo_lists, edge_sources, w_edge_in, b_edge_in, w_edge_out, w_unpool,
):
    nodes, width = node_feats.shape
    cells = edge_sources.shape[0] // K
    half = cells // 2
    side = halo_lists.shape[0] // 2
    rows = cells + 2 * side
    fines, coarses = lax.axis_size("fine"), lax.axis_size("coarse")
    fine_bits, coarse_bits = bits_of(fines), bits_of(coarses)
    ids = lax.rem(cluster_ids, cells).reshape(1, nodes)
    lists = halo_lists.reshape(1, 2 * side)
    src = edge_sources.reshape(cells, K).T
    bias = b_edge_in.reshape(1, width)

    def pool(x):
        keep, send = call(pool_body, (sds((half, width), F32),) * 2, (ids, x), 2 * nodes * cells * width)
        outs = (sds((half, width), F32), sds((half, width), BF))
        return call(chip_body, outs, (keep, swap(send, "fine", 0)), 0)

    def across(part, send, after=()):
        for bit in range(1, fine_bits):
            recv = swap(send, "fine", bit)
            last = bit == fine_bits - 1
            outs = (sds((half, width), BF),) if last else (sds((half, width), F32), sds((half, width), BF))
            part, send = (*call(across_body, outs, (part, recv), 0, after=after), None)[:2]
        return part

    part_p, send_p = pool(node_feats)
    part_g, send_g = pool(grad_out)
    picked = call(pick_body, (sds((2 * side, width), BF),), (send_p, lists), 0, after=(send_g,))[0]
    sent = call(side_body, (sds((side, width), BF),), (picked, swap(picked, "fine", 0)), 0)[0]
    own_halo = call(
        halo_sum_body, (sds((side, width), BF),), [send_sides(sent, d) for d in range(fines // 2)], 0,
        scratch=(pltpu.VMEM((fines // 2, side, width), F32),),
    )[0]
    own_p = across(part_p, send_p, after=(own_halo, src, bias))
    other_halo = swap(own_halo, "fine", 0)
    others = [swap(x, "fine", 0) for x in (own_p[: half // 2], own_p[half // 2 :])]
    ext, base = call(
        extend_body,
        (sds((rows, width), BF), sds((cells, width), F32)),
        (*others, own_p, own_halo, other_halo, w_edge_in, bias),
        0,
    )

    def forward(first, after=()):
        edges = K // 2 * cells
        return call(
            functools.partial(forward_body, first=first),
            (sds((cells, width), F32), sds((edges, width), F32), sds((edges, width), BF), sds((8, LANES), F32)),
            (ext, base, src, w_edge_in),
            0,
            vmem=32,
            after=after,
        )

    *front, front_token = forward(0)
    own_g = across(part_g, send_g, after=(front_token,))
    other_g = swap(own_g, "fine", 0)
    *rear, _ = forward(K // 2, after=(own_g,))
    per = 4 * width // fines
    first = per // 2
    act, ga, gn, keep, send, bias_sum = call(
        backward_body,
        (
            sds((K * cells, width), BF), sds((cells, width), F32), sds((cells, width), BF),
            sds((first, width), F32), sds((first + PACK, width), BF), sds((8, width), F32),
        ),
        (own_g, other_g, ext, *front, *rear, w_edge_out, w_unpool),
        2 * K * cells * width * width,
        vmem=32,
        scratch=(pltpu.VMEM((cells, width), BF), pltpu.VMEM((per, width), F32)),
    )

    back = call(
        back_body, (sds((side, width), BF),), (act, src, w_edge_in), 4 * K * side * cells * width,
        scratch=(pltpu.VMEM((2 * side, width), F32),),
    )[0]
    own_back = send_sides(back)
    other_back = swap(own_back, "fine", 0)
    cell_grads = [
        call(
            functools.partial(cell_grad_body, first=at),
            (sds((half, width), F32),),
            (act, src, ga, gn, w_edge_in),
            2 * K * half * cells * width,
        )[0]
        for at in (0, half)
    ]
    grad_feats, feats_token = call(
        feats_body,
        (sds((nodes, width), BF), sds((8, LANES), F32)),
        (*cell_grads, own_back, other_back, lists, ids, grad_out),
        2 * nodes * cells * width,
        vmem=24,
        scratch=(pltpu.VMEM((cells, width), BF),),
    )

    after = {1: (back,), 2: (cell_grads[0],)}
    for bit in range(1, coarse_bits):
        recv = swap(send, "coarse", bit - 1)
        keep, send, bias_sum = call(
            functools.partial(stage_body, bit=bit),
            (sds((first, width), F32), sds((first + PACK, width), BF), sds((8, width), F32)),
            (keep, recv, bias_sum),
            0,
            scratch=(pltpu.VMEM((first, width), F32),),
            after=after.get(bit, ()),
        )
    recv = swap(send, "coarse", coarse_bits - 1)
    part = call(
        end_body, (sds((first + PACK, width), BF),), (keep, recv, bias_sum), 0,
        after=(cell_grads[1], other_back),
    )[0]
    near = [swap(part, "coarse", 0), swap(part, "fine", 1), swap_both(part)]
    part = call(
        square_body, (sds((2 * (per + PACK), width), BF),), (part, *near), 0, after=(feats_token,)
    )[0]
    for bit in range(2, fine_bits):
        other = swap(part, "fine", bit)
        body = functools.partial(merge_body, bit=bit)
        part = call(body, (sds((2 * part.shape[0], width), BF),), (part, other), 0)[0]
    other = swap(part, "fine", 0)
    total_cells = cells * coarses
    scales = dict(edge_scale=float(total_cells * K) ** -0.5, cell_scale=float(total_cells) ** -0.5)
    grad_w1, grad_b, grad_wo, grad_up = call(
        functools.partial(weights_body, per=per, **scales),
        (
            sds((2 * width, width), F32), sds((1, width), F32), sds((width, width), F32), sds((width, width), F32),
        ),
        (part, other),
        0,
    )
    return grad_feats, grad_w1, grad_b.reshape(width), grad_wo, grad_up


def solution(mesh):
    both = ("coarse", "fine")
    return jax.shard_map(
        local,
        mesh=mesh,
        in_specs=(P(both, None), P(both, None), P(both), P("coarse"), P("coarse"), P(), P(), P(), P()),
        out_specs=(P(both, None), P(), P(), P(), P()),
        check_vma=False,
    )
```

```python
import functools

import jax
import jax.numpy as jnp
from jax import lax
from jax.experimental import pallas as pl
from jax.experimental.pallas import tpu as pltpu
from jax.sharding import PartitionSpec as P

K = 4
BF = jnp.bfloat16
F32 = jnp.float32
LANES = 128
PACK = 16
MIB = 1 << 20


def dot(a, b):
    return jnp.dot(a, b, preferred_element_type=F32)


def dot_nt(a, b):
    return lax.dot_general(a, b, (((1,), (1,)), ((), ())), preferred_element_type=F32)


def dot_tn(a, b):
    return lax.dot_general(a, b, (((0,), (0,)), ((), ())), preferred_element_type=F32)


def bits_of(count):
    assert count > 1 and count & (count - 1) == 0
    return count.bit_length() - 1


def swap(x, axis, bit):
    count = lax.axis_size(axis)
    return lax.ppermute(x, axis, [(i, i ^ (1 << bit)) for i in range(count)])


def swap_both(x):
    owners, fines = lax.axis_size("coarse"), lax.axis_size("fine")
    pairs = [(g * fines + f, (g ^ 1) * fines + (f ^ 2)) for g in range(owners) for f in range(fines)]
    return lax.ppermute(x, ("coarse", "fine"), pairs)


def send_sides(x, flip=0):
    owners, fines = lax.axis_size("coarse"), lax.axis_size("fine")
    pairs = [
        (g * fines + f, (g + 1 - 2 * (f % 2)) % owners * fines + (f ^ (2 * flip)))
        for g in range(owners)
        for f in range(fines)
    ]
    return lax.ppermute(x, ("coarse", "fine"), pairs)


def call(body, outs, args, flops, vmem=16, scratch=(), after=(), into=None, far=0):
    moved = sum(a.size * a.dtype.itemsize for a in (*args, *outs)) if flops else 0
    count = len(args)
    unseen = (*after, into) if into is not None else after
    waited = len(unseen)

    def kernel(*refs):
        body(*refs[:count], *refs[count + waited :])

    anywhere = pl.BlockSpec(memory_space=pl.ANY)
    in_vmem = pl.BlockSpec(memory_space=pltpu.VMEM)
    places = tuple([anywhere] * far + [in_vmem] * (len(outs) - far))
    return pl.pallas_call(
        kernel,
        out_shape=outs,
        in_specs=[in_vmem] * count + [anywhere] * waited,
        out_specs=places,
        scratch_shapes=scratch,
        input_output_aliases={} if into is None else {count + waited - 1: 0},
        compiler_params=pltpu.CompilerParams(vmem_limit_bytes=vmem * MIB),
        cost_estimate=pl.CostEstimate(flops=int(flops), bytes_accessed=int(moved), transcendentals=0),
    )(*args, *unseen)


def sds(shape, dtype):
    return jax.ShapeDtypeStruct(shape, dtype)


def column(row):
    blocks = [
        jnp.broadcast_to(row[:, i : i + LANES], (LANES, LANES)).T
        for i in range(0, row.shape[1], LANES)
    ]
    return blocks[0] if len(blocks) == 1 else jnp.concatenate(blocks, axis=0)


def hot_rows(row, width):
    ids = column(row)
    ids = jnp.concatenate([ids] * (width // LANES), axis=1)
    lane = lax.broadcasted_iota(jnp.int32, ids.shape, 1)
    return jnp.where(lane == ids, 1.0, 0.0).astype(BF)


def hot_columns(row, height, start=0):
    shape = (height, row.shape[1])
    at = lax.broadcasted_iota(jnp.int32, shape, 0)
    return jnp.where(at == row - start, 1.0, 0.0).astype(BF)


def source_body(src_ref, out_ref, mixed):
    per = LANES // K
    src = src_ref[...]
    at = lax.broadcasted_iota(jnp.int32, (LANES, LANES), 0)
    to = lax.broadcasted_iota(jnp.int32, (LANES, LANES), 1)
    order = jnp.where(to == (at % K) * per + at // K, 1.0, 0.0).astype(BF)
    high = lax.shift_right_logical(src, 6)
    low = (src - 64 * high).astype(F32).astype(BF)
    high = high.astype(F32).astype(BF)
    mixed[...] = (64.0 * dot(high, order) + dot(low, order)).astype(jnp.int32)
    count = mixed.shape[0] // K
    lane = lax.broadcasted_iota(jnp.int32, (count, LANES), 1) // per
    quarters = [mixed[pl.ds(j, count, stride=K), :] for j in range(K)]
    for k in range(K):
        rows = jnp.zeros((count, LANES), jnp.int32)
        for j in range(K):
            turned = quarters[j] if j == k else pltpu.roll(quarters[j], (j - k) % K * per, 1)
            rows = jnp.where(lane == j, turned, rows)
        for q in range(count):
            out_ref[k : k + 1, q * LANES : (q + 1) * LANES] = rows[q : q + 1, :]


def pool_body(ids_ref, x_ref, keep_ref, send_ref):
    half = keep_ref.shape[0]
    core = lax.axis_index("fine") % 2
    ids = ids_ref[...]
    x = x_ref[...]
    step = min(256, half)
    for out_ref, base in ((send_ref, (1 - core) * half), (keep_ref, core * half)):
        for t in range(0, half, step):
            out_ref[t : t + step, :] = dot(hot_columns(ids, step, base + t), x)


def pick_body(part_ref, lists_ref, out_ref):
    half = part_ref.shape[0]
    core = lax.axis_index("fine") % 2
    out_ref[...] = dot(hot_rows(lists_ref[...] - core * half, half), part_ref[...]).astype(BF)


def side_body(own, other, out_ref):
    side = out_ref.shape[0]
    core = lax.axis_index("fine") % 2
    at = pl.ds(pl.multiple_of(core * side, side), side)
    out_ref[...] = own[at, :] + other[at, :]


def halo_sum_body(*refs):
    *parts, out_ref, slots = refs
    chip = lax.axis_index("fine") // 2
    for offset, part in enumerate(parts):
        slots[chip ^ offset] = part[...].astype(F32)
    total = slots[0]
    for i in range(1, len(parts)):
        total = total + slots[i]
    out_ref[...] = total.astype(BF)


def chip_body(keep, recv, part_ref, send_ref):
    total = keep[...] + recv[...]
    part_ref[...] = total
    send_ref[...] = total.astype(BF)


def across_body(part, recv, *out_refs):
    total = part[...] + recv[...].astype(F32)
    for ref in out_refs:
        ref[...] = total.astype(ref.dtype)


def core_order(half):
    core = lax.axis_index("fine") % 2
    at_own = pl.ds(pl.multiple_of(core * half, half), half)
    at_other = pl.ds(pl.multiple_of((1 - core) * half, half), half)
    return at_own, at_other


def extend_body(*refs):
    *others, own_p, own_halo, other_halo, w1_ref, b_ref, ext, base = refs
    half, width = own_p.shape
    cells = 2 * half
    side = own_halo.shape[0]
    core = lax.axis_index("fine") % 2
    ext[pl.ds(pl.multiple_of(core * half, half), half), :] = own_p[...]
    n = half // len(others)
    for i, other in enumerate(others):
        ext[pl.ds(pl.multiple_of((1 - core) * half + i * n, n), n), :] = other[...]
    ext[pl.ds(pl.multiple_of(cells + core * side, PACK), side), :] = own_halo[...]
    ext[pl.ds(pl.multiple_of(cells + (1 - core) * side, PACK), side), :] = other_halo[...]
    base[...] = dot(ext[0:cells, :], w1_ref[0:width, :]) + b_ref[...].astype(F32)


def forward_body(ext, base, src_ref, w1_ref, hid, slope, feats, token_ref, *, first):
    cells, width = base.shape
    rows = ext.shape[0]
    token_ref[...] = jnp.zeros_like(token_ref)
    block = 512
    for i in range(slope.shape[0] // cells):
        for t in range(0, cells, block):
            part = src_ref[first + i : first + i + 1, t : t + block]
            at = i * cells + t
            feats[at : at + block, :] = dot(hot_rows(part, rows), ext[...]).astype(BF)
        at = slice(i * cells, (i + 1) * cells)
        pre = base[...] + dot(feats[at, :], w1_ref[width : 2 * width, :])
        sig = 0.5 * jnp.tanh(0.5 * pre) + 0.5
        hidden = pre * sig
        hid[...] = hidden if i == 0 else hid[...] + hidden
        slope[at, :] = sig + hidden * (1.0 - sig)


def split(x):
    high = x.astype(BF)
    return high, (x - high.astype(F32)).astype(BF)


def bias_rows(bias):
    high, low = (part.astype(F32) for part in split(bias))
    at = lax.broadcasted_iota(jnp.int32, (PACK, bias.shape[1]), 0)
    return jnp.where(at == 0, high, jnp.where(at == 1, low, 0.0)).astype(BF), high + low


def axis_bit(axis, bit):
    return lax.rem(lax.axis_index(axis) // (1 << bit), 2)


def emit(total_ref, bias, bit, keep_ref, send_ref, bias_ref):
    n = keep_ref.shape[0]
    if n == total_ref.shape[0]:
        sent = total_ref[...].astype(BF)
        keep_ref[...] = sent.astype(F32)
    else:
        side = axis_bit("coarse", bit)
        keep_ref[...] = total_ref[pl.ds(pl.multiple_of(side * n, n), n), :]
        sent = total_ref[pl.ds(pl.multiple_of((1 - side) * n, n), n), :].astype(BF)
    rows, bias = bias_rows(bias)
    send_ref[0:n, :] = sent
    send_ref[n : n + PACK, :] = rows
    bias_ref[...] = jnp.broadcast_to(bias, bias_ref.shape)


def backward_body(
    own_g, other_g, ext, hid_1, slope_1, feats_1, hid_2, slope_2, feats_2, wo_ref, wu_ref,
    act, ga_ref, gn_ref, keep_ref, send_ref, bias_ref,
    gsum, total,
):
    half, width = own_g.shape
    cells = 2 * half
    fine = lax.axis_index("fine")
    at_own, at_other = core_order(half)
    gsum[at_own, :] = own_g[...]
    gsum[at_other, :] = other_g[...]
    gn = dot_nt(gsum[...], wu_ref[...]).astype(BF)
    gn_ref[...] = gn
    grad = dot_nt(gn, wo_ref[...])
    ga = jnp.zeros((cells, width), F32)
    for k in range(K):
        at = slice(k * cells, (k + 1) * cells)
        slope, here = (slope_1, k) if k < K // 2 else (slope_2, k - K // 2)
        part = (grad * slope[here * cells : (here + 1) * cells, :]).astype(BF)
        act[at, :] = part
        ga = ga + part.astype(F32)
    ga_ref[...] = ga

    fines = lax.axis_size("fine")
    per = 4 * width // fines
    n = min(per, width)
    for index in range(fines):

        @pl.when(fine == index)
        def _():
            for r in range(0, per, n):
                which, first = divmod(index * per + r, width)
                cols = slice(first, first + n)
                if which == 0:
                    high, low = split(ga_ref[...])
                    left = ext[0:cells, cols]
                    out = dot_tn(left, high) + dot_tn(left, low)
                elif which == 1:
                    n_1 = feats_1.shape[0]
                    out = dot_tn(feats_1[:, cols], act[0:n_1, :]) + dot_tn(feats_2[:, cols], act[n_1:, :])
                elif which == 2:
                    high, low = split(hid_1[:, cols] + hid_2[:, cols])
                    out = dot_tn(high, gn_ref[...]) + dot_tn(low, gn_ref[...])
                else:
                    high, low = split(hid_1[...] + hid_2[...])
                    agg = dot(high, wo_ref[:, cols]) + dot(low, wo_ref[:, cols])
                    new = (ext[0:cells, cols].astype(F32) + agg).astype(BF)
                    out = dot_tn(new, gsum[...])
                total[r : r + n, :] = out

    emit(total, jnp.sum(ga_ref[...], axis=0, keepdims=True), 0, keep_ref, send_ref, bias_ref)


def received_bias(recv, n):
    return recv[n : n + 1, :].astype(F32) + recv[n + 1 : n + 2, :].astype(F32)


def stage_body(keep_in, recv, bias_in, keep_ref, send_ref, bias_ref, total, *, bit):
    n = keep_in.shape[0]
    total[...] = keep_in[...] + recv[0:n, :].astype(F32)
    emit(total, bias_in[0:1, :] + received_bias(recv, n), bit, keep_ref, send_ref, bias_ref)


def end_body(keep_in, recv, bias_in, out_ref):
    n = keep_in.shape[0]
    out_ref[0:n, :] = (keep_in[...] + recv[0:n, :].astype(F32)).astype(BF)
    out_ref[n : n + PACK, :] = bias_rows(bias_in[0:1, :] + received_bias(recv, n))[0]


def scatter(act, src_ref, first, count):
    cells = src_ref.shape[1]
    out = jnp.zeros((count, act.shape[1]), F32)
    for k in range(K):
        hot = hot_columns(src_ref[k : k + 1, :], count, first)
        out += dot(hot, act[k * cells : (k + 1) * cells, :])
    return out


def back_body(act, src_ref, w1_ref, out_ref, both):
    side, width = out_ref.shape
    rows = scatter(act, src_ref, src_ref.shape[1], 2 * side)
    both[...] = dot_nt(rows.astype(BF), w1_ref[width : 2 * width, :])
    core = lax.axis_index("fine") % 2
    out_ref[...] = both[pl.ds(pl.multiple_of((1 - core) * side, side), side), :].astype(BF)


def cell_grad_body(act, src_ref, ga_ref, gn_ref, w1_ref, out_ref, *, first):
    count, width = out_ref.shape
    step = min(512, count)
    for r in range(0, count, step):
        at = slice(first + r, first + r + step)
        rows = scatter(act, src_ref, first + r, step)
        out_ref[r : r + step, :] = (
            gn_ref[at, :].astype(F32)
            + dot_nt(ga_ref[at, :].astype(BF), w1_ref[0:width, :])
            + dot_nt(rows.astype(BF), w1_ref[width : 2 * width, :])
        )


def merge_body(own, other, *rest, bit):
    n = own.shape[0]
    out_ref = rest[-1]
    side = axis_bit("fine", bit)
    out_ref[pl.ds(pl.multiple_of(side * n, PACK), n), :] = own[...]
    out_ref[pl.ds(pl.multiple_of((1 - side) * n, PACK), n), :] = other[...]


def square_body(own, by_owner, by_chip, by_both, out_ref):
    size = out_ref.shape[0] // 2
    n = own.shape[0] - PACK
    half, chip = axis_bit("coarse", 0), axis_bit("fine", 1)
    for block, i, j in ((own, half, chip), (by_owner, 1 - half, chip), (by_chip, half, 1 - chip), (by_both, 1 - half, 1 - chip)):
        out_ref[pl.ds(pl.multiple_of(j * size + i * n, PACK), n), :] = block[0:n, :]
    for block, j in ((own, chip), (by_chip, 1 - chip)):
        out_ref[pl.ds(pl.multiple_of(j * size + 2 * n, PACK), PACK), :] = block[n:, :]


def weights_body(own, other, w1_ref, gb_ref, wo_ref, up_ref, *, per, edge_scale, cell_scale):
    width = own.shape[1]
    core = lax.axis_index("fine") % 2
    outs = ((w1_ref, 0, edge_scale), (w1_ref, width, edge_scale), (wo_ref, 0, edge_scale), (up_ref, 0, cell_scale))
    size = per + PACK
    n = min(per, width)
    for index in range(lax.axis_size("fine")):
        at = slice((index // 2) * size, (index // 2 + 1) * size)
        value = jnp.where(core == index % 2, own[at, :].astype(F32), other[at, :].astype(F32))
        if index == 0:
            gb_ref[...] = (value[per : per + 1] + value[per + 1 : per + 2]) * edge_scale
        for r in range(0, per, n):
            which, row = divmod(index * per + r, width)
            out_ref, start, scale = outs[which]
            out_ref[start + row : start + row + n, :] = value[r : r + n] * scale


def table_body(*refs):
    *pool_refs, own_back, other_back, lists_ref, table = refs
    lists = lists_ref[...]
    core = lax.axis_index("fine") % 2
    side = own_back.shape[0]
    returned = jnp.concatenate([own_back[...], other_back[...]], axis=0)
    first, second = lists[:, :side], lists[:, side:]
    lists = jnp.where(core == 0, jnp.concatenate([second, first], axis=1), lists)
    step = pool_refs[0].shape[0]
    for i, pool_ref in enumerate(pool_refs):
        add = dot(hot_columns(lists, step, i * step), returned)
        table[i * step : (i + 1) * step, :] = (pool_ref[...] + add).astype(BF)


def feats_body(table, ids_ref, grad_ref, *rest, first, count):
    out_hbm, token_ref, out, sem = rest[-4:]
    token_ref[...] = jnp.zeros_like(token_ref)
    cells = table.shape[0]
    block = 256
    for t in range(0, count, block):
        at = slice(first + t, first + t + block)
        rows = dot(hot_rows(ids_ref[:, at], cells), table[...])
        out[t : t + block, :] = (grad_ref[at, :].astype(F32) + rows).astype(BF)
    copy = pltpu.make_async_copy(out, out_hbm.at[first : first + count, :], sem)
    copy.start()
    copy.wait()


def local(
    node_feats, grad_out, cluster_ids, halo_lists, edge_sources, w_edge_in, b_edge_in, w_edge_out, w_unpool,
):
    nodes, width = node_feats.shape
    cells = edge_sources.shape[0] // K
    half = cells // 2
    side = halo_lists.shape[0] // 2
    rows = cells + 2 * side
    fines, coarses = lax.axis_size("fine"), lax.axis_size("coarse")
    fine_bits, coarse_bits = bits_of(fines), bits_of(coarses)
    ids = lax.rem(cluster_ids, cells).reshape(1, nodes)
    lists = halo_lists.reshape(1, 2 * side)
    flat = edge_sources.reshape(cells * K // LANES, LANES)
    src = call(
        source_body, (sds((K, cells), jnp.int32),), (flat,), 0, scratch=(pltpu.VMEM(flat.shape, jnp.int32),)
    )[0]
    bias = b_edge_in.reshape(1, width)

    def pool(x):
        keep, send = call(pool_body, (sds((half, width), F32),) * 2, (ids, x), 2 * nodes * cells * width)
        outs = (sds((half, width), F32), sds((half, width), BF))
        return call(chip_body, outs, (keep, swap(send, "fine", 0)), 0)

    def across(part, send, after=()):
        for bit in range(1, fine_bits):
            recv = swap(send, "fine", bit)
            last = bit == fine_bits - 1
            outs = (sds((half, width), BF),) if last else (sds((half, width), F32), sds((half, width), BF))
            part, send = (*call(across_body, outs, (part, recv), 0, after=after), None)[:2]
        return part

    part_p, send_p = pool(node_feats)
    part_g, send_g = pool(grad_out)
    picked = call(pick_body, (sds((2 * side, width), BF),), (send_p, lists), 0)[0]
    sent = call(side_body, (sds((side, width), BF),), (picked, swap(picked, "fine", 0)), 0)[0]
    own_halo = call(
        halo_sum_body, (sds((side, width), BF),), [send_sides(sent, d) for d in range(fines // 2)], 0,
        scratch=(pltpu.VMEM((fines // 2, side, width), F32),),
    )[0]
    own_p = across(part_p, send_p, after=(own_halo, src, bias))
    other_halo = swap(own_halo, "fine", 0)
    others = [swap(x, "fine", 0) for x in (own_p[: half // 2], own_p[half // 2 :])]
    ext, base = call(
        extend_body,
        (sds((rows, width), BF), sds((cells, width), F32)),
        (*others, own_p, own_halo, other_halo, w_edge_in, bias),
        0,
    )

    def forward(first, after=()):
        edges = K // 2 * cells
        return call(
            functools.partial(forward_body, first=first),
            (sds((cells, width), F32), sds((edges, width), F32), sds((edges, width), BF), sds((8, LANES), F32)),
            (ext, base, src, w_edge_in),
            0,
            vmem=32,
            after=after,
        )

    *front, front_token = forward(0)
    own_g = across(part_g, send_g, after=(front_token,))
    other_g = swap(own_g, "fine", 0)
    *rear, _ = forward(K // 2, after=(own_g,))
    per = 4 * width // fines
    first = per // 2
    act, ga, gn, keep, send, bias_sum = call(
        backward_body,
        (
            sds((K * cells, width), BF), sds((cells, width), F32), sds((cells, width), BF),
            sds((first, width), F32), sds((first + PACK, width), BF), sds((8, width), F32),
        ),
        (own_g, other_g, ext, *front, *rear, w_edge_out, w_unpool),
        2 * K * cells * width * width,
        vmem=32,
        scratch=(pltpu.VMEM((cells, width), BF), pltpu.VMEM((per, width), F32)),
    )

    back = call(
        back_body, (sds((side, width), BF),), (act, src, w_edge_in), 4 * K * side * cells * width,
        scratch=(pltpu.VMEM((2 * side, width), F32),),
    )[0]
    own_back = send_sides(back)
    other_back = swap(own_back, "fine", 0)
    cell_grads = [
        call(
            functools.partial(cell_grad_body, first=at),
            (sds((half, width), F32),),
            (act, src, ga, gn, w_edge_in),
            2 * K * half * cells * width,
        )[0]
        for at in (0, half)
    ]
    table = call(
        table_body, (sds((cells, width), BF),), (*cell_grads, own_back, other_back, lists), 0
    )[0]

    def feats(first, count, after=(), into=None):
        return call(
            functools.partial(feats_body, first=first, count=count),
            (sds((nodes, width), BF), sds((8, LANES), F32)),
            (table, ids, grad_out),
            2 * count * cells * width,
            vmem=24,
            scratch=(pltpu.VMEM((count, width), BF), pltpu.SemaphoreType.DMA(())),
            after=after,
            into=into,
            far=1,
        )

    after = {1: (back,), 2: (cell_grads[0],)}
    for bit in range(1, coarse_bits):
        recv = swap(send, "coarse", bit - 1)
        keep, send, bias_sum = call(
            functools.partial(stage_body, bit=bit),
            (sds((first, width), F32), sds((first + PACK, width), BF), sds((8, width), F32)),
            (keep, recv, bias_sum),
            0,
            scratch=(pltpu.VMEM((first, width), F32),),
            after=after.get(bit, ()),
        )
    recv = swap(send, "coarse", coarse_bits - 1)
    part = call(
        end_body, (sds((first + PACK, width), BF),), (keep, recv, bias_sum), 0,
        after=(cell_grads[1], other_back),
    )[0]
    front_rows = nodes // 2
    grad_feats, feats_token = feats(0, front_rows)
    near = [swap(part, "coarse", 0), swap(part, "fine", 1), swap_both(part)]
    part = call(
        square_body, (sds((2 * (per + PACK), width), BF),), (part, *near), 0, after=(feats_token,)
    )[0]
    for bit in range(2, fine_bits):
        other = swap(part, "fine", bit)
        body = functools.partial(merge_body, bit=bit)
        part = call(body, (sds((2 * part.shape[0], width), BF),), (part, other), 0)[0]
    other = swap(part, "fine", 0)
    grad_feats, feats_token = feats(front_rows, nodes - front_rows, after=(part,), into=grad_feats)
    total_cells = cells * coarses
    scales = dict(edge_scale=float(total_cells * K) ** -0.5, cell_scale=float(total_cells) ** -0.5)
    grad_w1, grad_b, grad_wo, grad_up = call(
        functools.partial(weights_body, per=per, **scales),
        (
            sds((2 * width, width), F32), sds((1, width), F32), sds((width, width), F32), sds((width, width), F32),
        ),
        (part, other),
        0,
        after=(feats_token,),
    )
    return grad_feats, grad_w1, grad_b.reshape(width), grad_wo, grad_up


def solution(mesh):
    both = ("coarse", "fine")
    return jax.shard_map(
        local,
        mesh=mesh,
        in_specs=(P(both, None), P(both, None), P(both), P("coarse"), P("coarse"), P(), P(), P(), P()),
        out_specs=(P(both, None), P(), P(), P(), P()),
        check_vma=False,
    )
```

```python
import functools

import jax
import jax.numpy as jnp
from jax import lax
from jax.experimental import pallas as pl
from jax.experimental.pallas import tpu as pltpu
from jax.sharding import PartitionSpec as P

K = 4
EARLY = 3
BF = jnp.bfloat16
F32 = jnp.float32
LANES = 128
PACK = 16
MIB = 1 << 20
AHEAD = 10**9


def dot(a, b):
    return jnp.dot(a, b, preferred_element_type=F32)


def dot_nt(a, b):
    return lax.dot_general(a, b, (((1,), (1,)), ((), ())), preferred_element_type=F32)


def dot_tn(a, b):
    return lax.dot_general(a, b, (((0,), (0,)), ((), ())), preferred_element_type=F32)


def bits_of(count):
    assert count > 1 and count & (count - 1) == 0
    return count.bit_length() - 1


def swap(x, axis, bit):
    count = lax.axis_size(axis)
    return lax.ppermute(x, axis, [(i, i ^ (1 << bit)) for i in range(count)])


def swap_both(x):
    owners, fines = lax.axis_size("coarse"), lax.axis_size("fine")
    pairs = [(g * fines + f, (g ^ 1) * fines + (f ^ 2)) for g in range(owners) for f in range(fines)]
    return lax.ppermute(x, ("coarse", "fine"), pairs)


def send_sides(x, flip=0):
    owners, fines = lax.axis_size("coarse"), lax.axis_size("fine")
    pairs = [
        (g * fines + f, (g + 1 - 2 * (f % 2)) % owners * fines + (f ^ (2 * flip)))
        for g in range(owners)
        for f in range(fines)
    ]
    return lax.ppermute(x, ("coarse", "fine"), pairs)


def call(body, outs, args, flops, vmem=16, scratch=(), after=(), into=None, far=0):
    moved = sum(a.size * a.dtype.itemsize for a in (*args, *outs)) if flops else 0
    count = len(args)
    unseen = (*after, into) if into is not None else after
    waited = len(unseen)

    def kernel(*refs):
        body(*refs[:count], *refs[count + waited :])

    anywhere = pl.BlockSpec(memory_space=pl.ANY)
    in_vmem = pl.BlockSpec(memory_space=pltpu.VMEM)
    places = tuple([anywhere] * far + [in_vmem] * (len(outs) - far))
    return pl.pallas_call(
        kernel,
        out_shape=outs,
        in_specs=[in_vmem] * count + [anywhere] * waited,
        out_specs=places,
        scratch_shapes=scratch,
        input_output_aliases={} if into is None else {count + waited - 1: 0},
        compiler_params=pltpu.CompilerParams(vmem_limit_bytes=vmem * MIB),
        cost_estimate=pl.CostEstimate(flops=int(flops), bytes_accessed=int(moved), transcendentals=0),
    )(*args, *unseen)


def sds(shape, dtype):
    return jax.ShapeDtypeStruct(shape, dtype)


def column(row):
    blocks = [
        jnp.broadcast_to(row[:, i : i + LANES], (LANES, LANES)).T
        for i in range(0, row.shape[1], LANES)
    ]
    return blocks[0] if len(blocks) == 1 else jnp.concatenate(blocks, axis=0)


def hot_rows(row, width):
    ids = column(row)
    ids = jnp.concatenate([ids] * (width // LANES), axis=1)
    lane = lax.broadcasted_iota(jnp.int32, ids.shape, 1)
    return jnp.where(lane == ids, 1.0, 0.0).astype(BF)


def hot_columns(row, height, start=0):
    shape = (height, row.shape[1])
    at = lax.broadcasted_iota(jnp.int32, shape, 0)
    return jnp.where(at == row - start, 1.0, 0.0).astype(BF)


def local_body(ids_ref, out_ref, *, cells):
    out_ref[...] = lax.rem(ids_ref[...], cells)


def source_body(src_ref, out_ref, mixed):
    per = LANES // K
    src = src_ref[...]
    at = lax.broadcasted_iota(jnp.int32, (LANES, LANES), 0)
    to = lax.broadcasted_iota(jnp.int32, (LANES, LANES), 1)
    order = jnp.where(to == (at % K) * per + at // K, 1.0, 0.0).astype(BF)
    high = lax.shift_right_logical(src, 6)
    low = (src - 64 * high).astype(F32).astype(BF)
    high = high.astype(F32).astype(BF)
    mixed[...] = (64.0 * dot(high, order) + dot(low, order)).astype(jnp.int32)
    count = mixed.shape[0] // K
    lane = lax.broadcasted_iota(jnp.int32, (count, LANES), 1) // per
    quarters = [mixed[pl.ds(j, count, stride=K), :] for j in range(K)]
    for k in range(K):
        rows = jnp.zeros((count, LANES), jnp.int32)
        for j in range(K):
            turned = quarters[j] if j == k else pltpu.roll(quarters[j], (j - k) % K * per, 1)
            rows = jnp.where(lane == j, turned, rows)
        for q in range(count):
            out_ref[k : k + 1, q * LANES : (q + 1) * LANES] = rows[q : q + 1, :]


def pool_body(ids_ref, x_ref, keep_ref, send_ref):
    half = keep_ref.shape[0]
    core = lax.axis_index("fine") % 2
    ids = ids_ref[...]
    x = x_ref[...]
    step = min(256, half)
    for out_ref, base in ((send_ref, (1 - core) * half), (keep_ref, core * half)):
        for t in range(0, half, step):
            out_ref[t : t + step, :] = dot(hot_columns(ids, step, base + t), x)


def pick_body(part_ref, lists_ref, out_ref):
    half = part_ref.shape[0]
    core = lax.axis_index("fine") % 2
    out_ref[...] = dot(hot_rows(lists_ref[...] - core * half, half), part_ref[...]).astype(BF)


def side_body(own, other, out_ref):
    side = out_ref.shape[0]
    core = lax.axis_index("fine") % 2
    at = pl.ds(pl.multiple_of(core * side, side), side)
    out_ref[...] = own[at, :] + other[at, :]


def halo_sum_body(*refs):
    *parts, out_ref, slots = refs
    chip = lax.axis_index("fine") // 2
    for offset, part in enumerate(parts):
        slots[chip ^ offset] = part[...].astype(F32)
    total = slots[0]
    for i in range(1, len(parts)):
        total = total + slots[i]
    out_ref[...] = total.astype(BF)


def chip_body(keep, recv, part_ref, send_ref):
    total = keep[...] + recv[...]
    part_ref[...] = total
    send_ref[...] = total.astype(BF)


def across_body(part, recv, *out_refs):
    total = part[...] + recv[...].astype(F32)
    for ref in out_refs:
        ref[...] = total.astype(ref.dtype)


def core_order(half):
    core = lax.axis_index("fine") % 2
    at_own = pl.ds(pl.multiple_of(core * half, half), half)
    at_other = pl.ds(pl.multiple_of((1 - core) * half, half), half)
    return at_own, at_other


def near_body(own_p, src_ref, near):
    half = own_p.shape[0]
    cells = 2 * half
    core = lax.axis_index("fine") % 2
    block = 512
    for k in range(K):
        for t in range(0, cells, block):
            hot = hot_rows(src_ref[k : k + 1, t : t + block] - core * half, half)
            near[k * cells + t : k * cells + t + block, :] = dot(hot, own_p[...]).astype(BF)


def extend_body(*refs):
    *others, own_p, own_halo, other_halo, w1_ref, b_ref, table, far, base = refs
    half, width = own_p.shape
    side = own_halo.shape[0]
    core = lax.axis_index("fine") % 2
    n = half // len(others)
    for i, other in enumerate(others):
        far[i * n : (i + 1) * n, :] = other[...]
    far[pl.ds(pl.multiple_of(half + core * side, PACK), side), :] = own_halo[...]
    far[pl.ds(pl.multiple_of(half + (1 - core) * side, PACK), side), :] = other_halo[...]
    at_own, at_other = core_order(half)
    table[at_own, :] = own_p[...]
    table[at_other, :] = far[0:half, :]
    base[...] = dot(table[...], w1_ref[0:width, :]) + b_ref[...].astype(F32)


def forward_body(base, far, near, src_ref, w1_ref, hid, slope, feats, token_ref, *, first):
    cells, width = base.shape
    half = cells // 2
    core = lax.axis_index("fine") % 2
    token_ref[...] = jnp.zeros_like(token_ref)
    block = 512
    for i in range(slope.shape[0] // cells):
        for t in range(0, cells, block):
            src = src_ref[first + i : first + i + 1, t : t + block]
            mine = jnp.logical_and(src >= core * half, src < (core + 1) * half)
            place = jnp.where(src >= cells, src - half, src - (1 - core) * half)
            picked = dot(hot_rows(jnp.where(mine, -1, place), far.shape[0]), far[...])
            here = slice((first + i) * cells + t, (first + i) * cells + t + block)
            feats[i * cells + t : i * cells + t + block, :] = (picked + near[here, :].astype(F32)).astype(BF)
        at = slice(i * cells, (i + 1) * cells)
        pre = base[...] + dot(feats[at, :], w1_ref[width : 2 * width, :])
        sig = 0.5 * jnp.tanh(0.5 * pre) + 0.5
        hidden = pre * sig
        hid[...] = hidden if i == 0 else hid[...] + hidden
        slope[at, :] = sig + hidden * (1.0 - sig)


def split(x):
    high = x.astype(BF)
    return high, (x - high.astype(F32)).astype(BF)


def bias_rows(bias):
    high, low = (part.astype(F32) for part in split(bias))
    at = lax.broadcasted_iota(jnp.int32, (PACK, bias.shape[1]), 0)
    return jnp.where(at == 0, high, jnp.where(at == 1, low, 0.0)).astype(BF), high + low


def axis_bit(axis, bit):
    return lax.rem(lax.axis_index(axis) // (1 << bit), 2)


def emit(total_ref, bias, bit, keep_ref, send_ref, bias_ref):
    n = keep_ref.shape[0]
    if n == total_ref.shape[0]:
        sent = total_ref[...].astype(BF)
        keep_ref[...] = sent.astype(F32)
    else:
        side = axis_bit("coarse", bit)
        keep_ref[...] = total_ref[pl.ds(pl.multiple_of(side * n, n), n), :]
        sent = total_ref[pl.ds(pl.multiple_of((1 - side) * n, n), n), :].astype(BF)
    rows, bias = bias_rows(bias)
    send_ref[0:n, :] = sent
    send_ref[n : n + PACK, :] = rows
    bias_ref[...] = jnp.broadcast_to(bias, bias_ref.shape)


def backward_body(
    own_g, other_g, table, hid_1, slope_1, feats_1, hid_2, slope_2, feats_2, wo_ref, wu_ref,
    act, ga_ref, gn_ref, keep_ref, send_ref, bias_ref,
    gsum, total,
):
    half, width = own_g.shape
    cells = 2 * half
    fine = lax.axis_index("fine")
    at_own, at_other = core_order(half)
    gsum[at_own, :] = own_g[...]
    gsum[at_other, :] = other_g[...]
    gn = dot_nt(gsum[...], wu_ref[...]).astype(BF)
    gn_ref[...] = gn
    grad = dot_nt(gn, wo_ref[...])
    ga = jnp.zeros((cells, width), F32)
    for k in range(K):
        at = slice(k * cells, (k + 1) * cells)
        slope, here = (slope_1, k) if k < EARLY else (slope_2, k - EARLY)
        part = (grad * slope[here * cells : (here + 1) * cells, :]).astype(BF)
        act[at, :] = part
        ga = ga + part.astype(F32)
    ga_ref[...] = ga

    fines = lax.axis_size("fine")
    per = 4 * width // fines
    n = min(per, width)
    for index in range(fines):

        @pl.when(fine == index)
        def _():
            for r in range(0, per, n):
                which, first = divmod(index * per + r, width)
                cols = slice(first, first + n)
                if which == 0:
                    high, low = split(ga_ref[...])
                    left = table[:, cols]
                    out = dot_tn(left, high) + dot_tn(left, low)
                elif which == 1:
                    n_1 = feats_1.shape[0]
                    out = dot_tn(feats_1[:, cols], act[0:n_1, :]) + dot_tn(feats_2[:, cols], act[n_1:, :])
                elif which == 2:
                    high, low = split(hid_1[:, cols] + hid_2[:, cols])
                    out = dot_tn(high, gn_ref[...]) + dot_tn(low, gn_ref[...])
                else:
                    high, low = split(hid_1[...] + hid_2[...])
                    agg = dot(high, wo_ref[:, cols]) + dot(low, wo_ref[:, cols])
                    new = (table[:, cols].astype(F32) + agg).astype(BF)
                    out = dot_tn(new, gsum[...])
                total[r : r + n, :] = out

    emit(total, jnp.sum(ga_ref[...], axis=0, keepdims=True), 0, keep_ref, send_ref, bias_ref)


def received_bias(recv, n):
    return recv[n : n + 1, :].astype(F32) + recv[n + 1 : n + 2, :].astype(F32)


def stage_body(keep_in, recv, bias_in, keep_ref, send_ref, bias_ref, total, *, bit):
    n = keep_in.shape[0]
    total[...] = keep_in[...] + recv[0:n, :].astype(F32)
    emit(total, bias_in[0:1, :] + received_bias(recv, n), bit, keep_ref, send_ref, bias_ref)


def end_body(keep_in, recv, bias_in, out_ref):
    n = keep_in.shape[0]
    out_ref[0:n, :] = (keep_in[...] + recv[0:n, :].astype(F32)).astype(BF)
    out_ref[n : n + PACK, :] = bias_rows(bias_in[0:1, :] + received_bias(recv, n))[0]


def scatter(act, src_ref, first, count):
    cells = src_ref.shape[1]
    out = jnp.zeros((count, act.shape[1]), F32)
    for k in range(K):
        hot = hot_columns(src_ref[k : k + 1, :], count, first)
        out += dot(hot, act[k * cells : (k + 1) * cells, :])
    return out


def back_body(act, src_ref, w1_ref, out_ref, both):
    side, width = out_ref.shape
    rows = scatter(act, src_ref, src_ref.shape[1], 2 * side)
    both[...] = dot_nt(rows.astype(BF), w1_ref[width : 2 * width, :])
    core = lax.axis_index("fine") % 2
    out_ref[...] = both[pl.ds(pl.multiple_of((1 - core) * side, side), side), :].astype(BF)


def cell_grad_body(act, src_ref, ga_ref, gn_ref, w1_ref, out_ref, *, first):
    count, width = out_ref.shape
    step = min(512, count)
    for r in range(0, count, step):
        at = slice(first + r, first + r + step)
        rows = scatter(act, src_ref, first + r, step)
        out_ref[r : r + step, :] = (
            gn_ref[at, :].astype(F32)
            + dot_nt(ga_ref[at, :].astype(BF), w1_ref[0:width, :])
            + dot_nt(rows.astype(BF), w1_ref[width : 2 * width, :])
        )


def merge_body(own, other, *rest, bit):
    n = own.shape[0]
    out_ref = rest[-1]
    side = axis_bit("fine", bit)
    out_ref[pl.ds(pl.multiple_of(side * n, PACK), n), :] = own[...]
    out_ref[pl.ds(pl.multiple_of((1 - side) * n, PACK), n), :] = other[...]


def square_body(own, by_owner, by_chip, by_both, out_ref):
    size = out_ref.shape[0] // 2
    n = own.shape[0] - PACK
    half, chip = axis_bit("coarse", 0), axis_bit("fine", 1)
    for block, i, j in ((own, half, chip), (by_owner, 1 - half, chip), (by_chip, half, 1 - chip), (by_both, 1 - half, 1 - chip)):
        out_ref[pl.ds(pl.multiple_of(j * size + i * n, PACK), n), :] = block[0:n, :]
    for block, j in ((own, chip), (by_chip, 1 - chip)):
        out_ref[pl.ds(pl.multiple_of(j * size + 2 * n, PACK), PACK), :] = block[n:, :]


def weights_body(own, other, w1_ref, gb_ref, wo_ref, up_ref, *, per, edge_scale, cell_scale):
    width = own.shape[1]
    core = lax.axis_index("fine") % 2
    outs = ((w1_ref, 0, edge_scale), (w1_ref, width, edge_scale), (wo_ref, 0, edge_scale), (up_ref, 0, cell_scale))
    size = per + PACK
    n = min(per, width)
    for index in range(lax.axis_size("fine")):
        at = slice((index // 2) * size, (index // 2 + 1) * size)
        value = jnp.where(core == index % 2, own[at, :].astype(F32), other[at, :].astype(F32))
        if index == 0:
            gb_ref[...] = (value[per : per + 1] + value[per + 1 : per + 2]) * edge_scale
        for r in range(0, per, n):
            which, row = divmod(index * per + r, width)
            out_ref, start, scale = outs[which]
            out_ref[start + row : start + row + n, :] = value[r : r + n] * scale


def table_body(*refs):
    *pool_refs, own_back, other_back, lists_ref, table = refs
    lists = lists_ref[...]
    core = lax.axis_index("fine") % 2
    side = own_back.shape[0]
    returned = jnp.concatenate([own_back[...], other_back[...]], axis=0)
    first, second = lists[:, :side], lists[:, side:]
    lists = jnp.where(core == 0, jnp.concatenate([second, first], axis=1), lists)
    step = pool_refs[0].shape[0]
    for i, pool_ref in enumerate(pool_refs):
        add = dot(hot_columns(lists, step, i * step), returned)
        table[i * step : (i + 1) * step, :] = (pool_ref[...] + add).astype(BF)


def feats_body(table, ids_ref, grad_ref, *rest, first, count):
    out_hbm, token_ref, out, sem = rest[-4:]
    token_ref[...] = jnp.zeros_like(token_ref)
    cells = table.shape[0]
    block = 256
    for t in range(0, count, block):
        at = slice(first + t, first + t + block)
        rows = dot(hot_rows(ids_ref[:, at], cells), table[...])
        out[t : t + block, :] = (grad_ref[at, :].astype(F32) + rows).astype(BF)
    copy = pltpu.make_async_copy(out, out_hbm.at[first : first + count, :], sem)
    copy.start()
    copy.wait()


def local(
    node_feats, grad_out, cluster_ids, halo_lists, edge_sources, w_edge_in, b_edge_in, w_edge_out, w_unpool,
):
    nodes, width = node_feats.shape
    cells = edge_sources.shape[0] // K
    half = cells // 2
    side = halo_lists.shape[0] // 2
    fines, coarses = lax.axis_size("fine"), lax.axis_size("coarse")
    fine_bits, coarse_bits = bits_of(fines), bits_of(coarses)
    ids = call(
        functools.partial(local_body, cells=cells), (sds((1, nodes), jnp.int32),), (cluster_ids.reshape(1, nodes),), AHEAD
    )[0]
    lists = halo_lists.reshape(1, 2 * side)
    flat = edge_sources.reshape(cells * K // LANES, LANES)
    src = call(
        source_body, (sds((K, cells), jnp.int32),), (flat,), 0, scratch=(pltpu.VMEM(flat.shape, jnp.int32),)
    )[0]
    bias = b_edge_in.reshape(1, width)

    def pool(x):
        keep, send = call(pool_body, (sds((half, width), F32),) * 2, (ids, x), 2 * nodes * cells * width)
        outs = (sds((half, width), F32), sds((half, width), BF))
        return call(chip_body, outs, (keep, swap(send, "fine", 0)), 0)

    def across(part, send, after=()):
        for bit in range(1, fine_bits):
            recv = swap(send, "fine", bit)
            last = bit == fine_bits - 1
            outs = (sds((half, width), BF),) if last else (sds((half, width), F32), sds((half, width), BF))
            part, send = (*call(across_body, outs, (part, recv), 0, after=after), None)[:2]
        return part

    part_p, send_p = pool(node_feats)
    part_g, send_g = pool(grad_out)
    picked = call(pick_body, (sds((2 * side, width), BF),), (send_p, lists), 0)[0]
    sent = call(side_body, (sds((side, width), BF),), (picked, swap(picked, "fine", 0)), 0)[0]
    own_halo = call(
        halo_sum_body, (sds((side, width), BF),), [send_sides(sent, d) for d in range(fines // 2)], 0,
        scratch=(pltpu.VMEM((fines // 2, side, width), F32),),
    )[0]
    own_p = across(part_p, send_p, after=(own_halo, src, bias))
    other_halo = swap(own_halo, "fine", 0)
    others = [swap(x, "fine", 0) for x in (own_p[: half // 2], own_p[half // 2 :])]
    near = call(near_body, (sds((K * cells, width), BF),), (own_p, src), 0, vmem=24)[0]
    table, far, base = call(
        extend_body,
        (sds((cells, width), BF), sds((half + 2 * side, width), BF), sds((cells, width), F32)),
        (*others, own_p, own_halo, other_halo, w_edge_in, bias),
        0,
    )

    def forward(first, count, after=()):
        edges = count * cells
        return call(
            functools.partial(forward_body, first=first),
            (sds((cells, width), F32), sds((edges, width), F32), sds((edges, width), BF), sds((8, LANES), F32)),
            (base, far, near, src, w_edge_in),
            0,
            vmem=32,
            after=after,
        )

    *front, front_token = forward(0, EARLY)
    own_g = across(part_g, send_g, after=(front_token,))
    other_g = swap(own_g, "fine", 0)
    *rear, _ = forward(EARLY, K - EARLY, after=(own_g,))
    per = 4 * width // fines
    first = per // 2
    act, ga, gn, keep, send, bias_sum = call(
        backward_body,
        (
            sds((K * cells, width), BF), sds((cells, width), F32), sds((cells, width), BF),
            sds((first, width), F32), sds((first + PACK, width), BF), sds((8, width), F32),
        ),
        (own_g, other_g, table, *front, *rear, w_edge_out, w_unpool),
        2 * K * cells * width * width,
        vmem=32,
        scratch=(pltpu.VMEM((cells, width), BF), pltpu.VMEM((per, width), F32)),
    )

    back = call(
        back_body, (sds((side, width), BF),), (act, src, w_edge_in), 4 * K * side * cells * width,
        scratch=(pltpu.VMEM((2 * side, width), F32),),
    )[0]
    own_back = send_sides(back)
    other_back = swap(own_back, "fine", 0)
    cell_grads = [
        call(
            functools.partial(cell_grad_body, first=at),
            (sds((half, width), F32),),
            (act, src, ga, gn, w_edge_in),
            2 * K * half * cells * width,
        )[0]
        for at in (0, half)
    ]
    table = call(
        table_body, (sds((cells, width), BF),), (*cell_grads, own_back, other_back, lists), 0
    )[0]

    def feats(first, count, after=(), into=None):
        return call(
            functools.partial(feats_body, first=first, count=count),
            (sds((nodes, width), BF), sds((8, LANES), F32)),
            (table, ids, grad_out),
            2 * count * cells * width,
            vmem=24,
            scratch=(pltpu.VMEM((count, width), BF), pltpu.SemaphoreType.DMA(())),
            after=after,
            into=into,
            far=1,
        )

    after = {1: (back,), 2: (cell_grads[0],)}
    for bit in range(1, coarse_bits):
        recv = swap(send, "coarse", bit - 1)
        keep, send, bias_sum = call(
            functools.partial(stage_body, bit=bit),
            (sds((first, width), F32), sds((first + PACK, width), BF), sds((8, width), F32)),
            (keep, recv, bias_sum),
            0,
            scratch=(pltpu.VMEM((first, width), F32),),
            after=after.get(bit, ()),
        )
    recv = swap(send, "coarse", coarse_bits - 1)
    part = call(
        end_body, (sds((first + PACK, width), BF),), (keep, recv, bias_sum), 0,
        after=(cell_grads[1], other_back),
    )[0]
    front_rows = nodes // 2
    grad_feats, feats_token = feats(0, front_rows)
    near = [swap(part, "coarse", 0), swap(part, "fine", 1), swap_both(part)]
    part = call(
        square_body, (sds((2 * (per + PACK), width), BF),), (part, *near), 0, after=(feats_token,)
    )[0]
    for bit in range(2, fine_bits):
        other = swap(part, "fine", bit)
        body = functools.partial(merge_body, bit=bit)
        part = call(body, (sds((2 * part.shape[0], width), BF),), (part, other), 0)[0]
    other = swap(part, "fine", 0)
    grad_feats, feats_token = feats(front_rows, nodes - front_rows, after=(part,), into=grad_feats)
    total_cells = cells * coarses
    scales = dict(edge_scale=float(total_cells * K) ** -0.5, cell_scale=float(total_cells) ** -0.5)
    grad_w1, grad_b, grad_wo, grad_up = call(
        functools.partial(weights_body, per=per, **scales),
        (
            sds((2 * width, width), F32), sds((1, width), F32), sds((width, width), F32), sds((width, width), F32),
        ),
        (part, other),
        0,
        after=(feats_token,),
    )
    return grad_feats, grad_w1, grad_b.reshape(width), grad_wo, grad_up


def solution(mesh):
    both = ("coarse", "fine")
    return jax.shard_map(
        local,
        mesh=mesh,
        in_specs=(P(both, None), P(both, None), P(both), P("coarse"), P("coarse"), P(), P(), P(), P()),
        out_specs=(P(both, None), P(), P(), P(), P()),
        check_vma=False,
    )
```

```python
import functools

import jax
import jax.numpy as jnp
from jax import lax
from jax.experimental import pallas as pl
from jax.experimental.pallas import tpu as pltpu
from jax.sharding import PartitionSpec as P

K = 4
EARLY = 2
BF = jnp.bfloat16
F32 = jnp.float32
LANES = 128
PACK = 16
MIB = 1 << 20
AHEAD = 10**9


def dot(a, b):
    return jnp.dot(a, b, preferred_element_type=F32)


def dot_nt(a, b):
    return lax.dot_general(a, b, (((1,), (1,)), ((), ())), preferred_element_type=F32)


def dot_tn(a, b):
    return lax.dot_general(a, b, (((0,), (0,)), ((), ())), preferred_element_type=F32)


def bits_of(count):
    assert count > 1 and count & (count - 1) == 0
    return count.bit_length() - 1


def swap(x, axis, bit):
    count = lax.axis_size(axis)
    return lax.ppermute(x, axis, [(i, i ^ (1 << bit)) for i in range(count)])


def swap_both(x):
    owners, fines = lax.axis_size("coarse"), lax.axis_size("fine")
    pairs = [(g * fines + f, (g ^ 1) * fines + (f ^ 2)) for g in range(owners) for f in range(fines)]
    return lax.ppermute(x, ("coarse", "fine"), pairs)


def send_sides(x, flip=0):
    owners, fines = lax.axis_size("coarse"), lax.axis_size("fine")
    pairs = [
        (g * fines + f, (g + 1 - 2 * (f % 2)) % owners * fines + (f ^ (2 * flip)))
        for g in range(owners)
        for f in range(fines)
    ]
    return lax.ppermute(x, ("coarse", "fine"), pairs)


def call(body, outs, args, flops, vmem=16, scratch=(), after=(), into=None, far=0):
    moved = sum(a.size * a.dtype.itemsize for a in (*args, *outs)) if flops else 0
    count = len(args)
    unseen = (*after, into) if into is not None else after
    waited = len(unseen)

    def kernel(*refs):
        body(*refs[:count], *refs[count + waited :])

    anywhere = pl.BlockSpec(memory_space=pl.ANY)
    in_vmem = pl.BlockSpec(memory_space=pltpu.VMEM)
    places = tuple([anywhere] * far + [in_vmem] * (len(outs) - far))
    return pl.pallas_call(
        kernel,
        out_shape=outs,
        in_specs=[in_vmem] * count + [anywhere] * waited,
        out_specs=places,
        scratch_shapes=scratch,
        input_output_aliases={} if into is None else {count + waited - 1: 0},
        compiler_params=pltpu.CompilerParams(vmem_limit_bytes=vmem * MIB),
        cost_estimate=pl.CostEstimate(flops=int(flops), bytes_accessed=int(moved), transcendentals=0),
    )(*args, *unseen)


def sds(shape, dtype):
    return jax.ShapeDtypeStruct(shape, dtype)


def column(row):
    blocks = [
        jnp.broadcast_to(row[:, i : i + LANES], (LANES, LANES)).T
        for i in range(0, row.shape[1], LANES)
    ]
    return blocks[0] if len(blocks) == 1 else jnp.concatenate(blocks, axis=0)


def hot_rows(row, width):
    ids = column(row)
    ids = jnp.concatenate([ids] * (width // LANES), axis=1)
    lane = lax.broadcasted_iota(jnp.int32, ids.shape, 1)
    return jnp.where(lane == ids, 1.0, 0.0).astype(BF)


def hot_columns(row, height, start=0):
    shape = (height, row.shape[1])
    at = lax.broadcasted_iota(jnp.int32, shape, 0)
    return jnp.where(at == row - start, 1.0, 0.0).astype(BF)


def local_body(ids_ref, out_ref, *, cells):
    out_ref[...] = lax.rem(ids_ref[...], cells)


def source_body(src_ref, out_ref, mixed):
    per = LANES // K
    src = src_ref[...]
    at = lax.broadcasted_iota(jnp.int32, (LANES, LANES), 0)
    to = lax.broadcasted_iota(jnp.int32, (LANES, LANES), 1)
    order = jnp.where(to == (at % K) * per + at // K, 1.0, 0.0).astype(BF)
    high = lax.shift_right_logical(src, 6)
    low = (src - 64 * high).astype(F32).astype(BF)
    high = high.astype(F32).astype(BF)
    mixed[...] = (64.0 * dot(high, order) + dot(low, order)).astype(jnp.int32)
    count = mixed.shape[0] // K
    lane = lax.broadcasted_iota(jnp.int32, (count, LANES), 1) // per
    quarters = [mixed[pl.ds(j, count, stride=K), :] for j in range(K)]
    for k in range(K):
        rows = jnp.zeros((count, LANES), jnp.int32)
        for j in range(K):
            turned = quarters[j] if j == k else pltpu.roll(quarters[j], (j - k) % K * per, 1)
            rows = jnp.where(lane == j, turned, rows)
        for q in range(count):
            out_ref[k : k + 1, q * LANES : (q + 1) * LANES] = rows[q : q + 1, :]


def pool_body(ids_ref, x_ref, keep_ref, *send_refs):
    half = keep_ref.shape[0]
    n = half // len(send_refs)
    core = lax.axis_index("fine") % 2
    ids = ids_ref[...]
    x = x_ref[...]
    core_rows = (1 - core) * half
    for i, ref in enumerate(send_refs):
        step = min(256, n)
        for t in range(0, n, step):
            ref[t : t + step, :] = dot(hot_columns(ids, step, core_rows + i * n + t), x)
    step = min(256, half)
    for t in range(0, half, step):
        keep_ref[t : t + step, :] = dot(hot_columns(ids, step, core * half + t), x)


def pick_body(part_ref, lists_ref, out_ref):
    half = part_ref.shape[0]
    core = lax.axis_index("fine") % 2
    out_ref[...] = dot(hot_rows(lists_ref[...] - core * half, half), part_ref[...]).astype(BF)


def side_body(own, other, out_ref):
    side = out_ref.shape[0]
    core = lax.axis_index("fine") % 2
    at = pl.ds(pl.multiple_of(core * side, side), side)
    out_ref[...] = own[at, :] + other[at, :]


def halo_sum_body(*refs):
    *parts, out_ref, slots = refs
    chip = lax.axis_index("fine") // 2
    for offset, part in enumerate(parts):
        slots[chip ^ offset] = part[...].astype(F32)
    total = slots[0]
    for i in range(1, len(parts)):
        total = total + slots[i]
    out_ref[...] = total.astype(BF)


def chip_body(keep, *refs):
    *recvs, part_ref, send_ref = refs
    n = keep.shape[0] // len(recvs)
    for i, recv in enumerate(recvs):
        at = slice(i * n, (i + 1) * n)
        total = keep[at, :] + recv[...]
        part_ref[at, :] = total
        send_ref[at, :] = total.astype(BF)


def across_body(part, recv, *out_refs):
    total = part[...] + recv[...].astype(F32)
    for ref in out_refs:
        ref[...] = total.astype(ref.dtype)


def core_order(half):
    core = lax.axis_index("fine") % 2
    at_own = pl.ds(pl.multiple_of(core * half, half), half)
    at_other = pl.ds(pl.multiple_of((1 - core) * half, half), half)
    return at_own, at_other


def near_body(own_p, src_ref, near):
    half = own_p.shape[0]
    cells = 2 * half
    core = lax.axis_index("fine") % 2
    block = 512
    for k in range(K):
        for t in range(0, cells, block):
            hot = hot_rows(src_ref[k : k + 1, t : t + block] - core * half, half)
            near[k * cells + t : k * cells + t + block, :] = dot(hot, own_p[...]).astype(BF)


def extend_body(*refs):
    *others, own_p, own_halo, other_halo, w1_ref, b_ref, table, far, base = refs
    half, width = own_p.shape
    side = own_halo.shape[0]
    core = lax.axis_index("fine") % 2
    n = half // len(others)
    for i, other in enumerate(others):
        far[i * n : (i + 1) * n, :] = other[...]
    far[pl.ds(pl.multiple_of(half + core * side, PACK), side), :] = own_halo[...]
    far[pl.ds(pl.multiple_of(half + (1 - core) * side, PACK), side), :] = other_halo[...]
    at_own, at_other = core_order(half)
    table[at_own, :] = own_p[...]
    table[at_other, :] = far[0:half, :]
    base[...] = dot(table[...], w1_ref[0:width, :]) + b_ref[...].astype(F32)


def forward_body(base, far, near, src_ref, w1_ref, hid, slope, feats, *tokens, first):
    cells, width = base.shape
    half = cells // 2
    core = lax.axis_index("fine") % 2
    for ref in tokens:
        ref[...] = jnp.zeros_like(ref)
    block = 512
    for i in range(slope.shape[0] // cells):
        for t in range(0, cells, block):
            src = src_ref[first + i : first + i + 1, t : t + block]
            mine = jnp.logical_and(src >= core * half, src < (core + 1) * half)
            place = jnp.where(src >= cells, src - half, src - (1 - core) * half)
            picked = dot(hot_rows(jnp.where(mine, -1, place), far.shape[0]), far[...])
            here = slice((first + i) * cells + t, (first + i) * cells + t + block)
            feats[i * cells + t : i * cells + t + block, :] = (picked + near[here, :].astype(F32)).astype(BF)
        at = slice(i * cells, (i + 1) * cells)
        pre = base[...] + dot(feats[at, :], w1_ref[width : 2 * width, :])
        sig = 0.5 * jnp.tanh(0.5 * pre) + 0.5
        hidden = pre * sig
        hid[...] = hidden if i == 0 else hid[...] + hidden
        slope[at, :] = sig + hidden * (1.0 - sig)


def split(x):
    high = x.astype(BF)
    return high, (x - high.astype(F32)).astype(BF)


def bias_rows(bias):
    high, low = (part.astype(F32) for part in split(bias))
    at = lax.broadcasted_iota(jnp.int32, (PACK, bias.shape[1]), 0)
    return jnp.where(at == 0, high, jnp.where(at == 1, low, 0.0)).astype(BF), high + low


def axis_bit(axis, bit):
    return lax.rem(lax.axis_index(axis) // (1 << bit), 2)


def emit(total_ref, bias, bit, keep_ref, send_ref, bias_ref):
    n = keep_ref.shape[0]
    if n == total_ref.shape[0]:
        sent = total_ref[...].astype(BF)
        keep_ref[...] = sent.astype(F32)
    else:
        side = axis_bit("coarse", bit)
        keep_ref[...] = total_ref[pl.ds(pl.multiple_of(side * n, n), n), :]
        sent = total_ref[pl.ds(pl.multiple_of((1 - side) * n, n), n), :].astype(BF)
    rows, bias = bias_rows(bias)
    send_ref[0:n, :] = sent
    send_ref[n : n + PACK, :] = rows
    bias_ref[...] = jnp.broadcast_to(bias, bias_ref.shape)


def backward_body(
    own_g, other_g, table, hid_1, slope_1, feats_1, hid_2, slope_2, feats_2, wo_ref, wu_ref,
    act, ga_ref, gn_ref, keep_ref, send_ref, bias_ref,
    gsum, total,
):
    half, width = own_g.shape
    cells = 2 * half
    fine = lax.axis_index("fine")
    at_own, at_other = core_order(half)
    gsum[at_own, :] = own_g[...]
    gsum[at_other, :] = other_g[...]
    gn = dot_nt(gsum[...], wu_ref[...]).astype(BF)
    gn_ref[...] = gn
    grad = dot_nt(gn, wo_ref[...])
    ga = jnp.zeros((cells, width), F32)
    for k in range(K):
        at = slice(k * cells, (k + 1) * cells)
        slope, here = (slope_1, k) if k < EARLY else (slope_2, k - EARLY)
        part = (grad * slope[here * cells : (here + 1) * cells, :]).astype(BF)
        act[at, :] = part
        ga = ga + part.astype(F32)
    ga_ref[...] = ga

    fines = lax.axis_size("fine")
    per = 4 * width // fines
    n = min(per, width)
    for index in range(fines):

        @pl.when(fine == index)
        def _():
            for r in range(0, per, n):
                which, first = divmod(index * per + r, width)
                cols = slice(first, first + n)
                if which == 0:
                    high, low = split(ga_ref[...])
                    left = table[:, cols]
                    out = dot_tn(left, high) + dot_tn(left, low)
                elif which == 1:
                    n_1 = feats_1.shape[0]
                    out = dot_tn(feats_1[:, cols], act[0:n_1, :]) + dot_tn(feats_2[:, cols], act[n_1:, :])
                elif which == 2:
                    high, low = split(hid_1[:, cols] + hid_2[:, cols])
                    out = dot_tn(high, gn_ref[...]) + dot_tn(low, gn_ref[...])
                else:
                    high, low = split(hid_1[...] + hid_2[...])
                    agg = dot(high, wo_ref[:, cols]) + dot(low, wo_ref[:, cols])
                    new = (table[:, cols].astype(F32) + agg).astype(BF)
                    out = dot_tn(new, gsum[...])
                total[r : r + n, :] = out

    emit(total, jnp.sum(ga_ref[...], axis=0, keepdims=True), 0, keep_ref, send_ref, bias_ref)


def received_bias(recv, n):
    return recv[n : n + 1, :].astype(F32) + recv[n + 1 : n + 2, :].astype(F32)


def stage_body(keep_in, recv, bias_in, keep_ref, send_ref, bias_ref, total, *, bit):
    n = keep_in.shape[0]
    total[...] = keep_in[...] + recv[0:n, :].astype(F32)
    emit(total, bias_in[0:1, :] + received_bias(recv, n), bit, keep_ref, send_ref, bias_ref)


def end_body(keep_in, recv, bias_in, out_ref):
    n = keep_in.shape[0]
    out_ref[0:n, :] = (keep_in[...] + recv[0:n, :].astype(F32)).astype(BF)
    out_ref[n : n + PACK, :] = bias_rows(bias_in[0:1, :] + received_bias(recv, n))[0]


def scatter(act, src_ref, first, count):
    cells = src_ref.shape[1]
    out = jnp.zeros((count, act.shape[1]), F32)
    for k in range(K):
        hot = hot_columns(src_ref[k : k + 1, :], count, first)
        out += dot(hot, act[k * cells : (k + 1) * cells, :])
    return out


def back_body(act, src_ref, w1_ref, out_ref, both):
    side, width = out_ref.shape
    rows = scatter(act, src_ref, src_ref.shape[1], 2 * side)
    both[...] = dot_nt(rows.astype(BF), w1_ref[width : 2 * width, :])
    core = lax.axis_index("fine") % 2
    out_ref[...] = both[pl.ds(pl.multiple_of((1 - core) * side, side), side), :].astype(BF)


def cell_grad_body(act, src_ref, ga_ref, gn_ref, w1_ref, out_ref, *, first):
    count, width = out_ref.shape
    step = min(512, count)
    for r in range(0, count, step):
        at = slice(first + r, first + r + step)
        rows = scatter(act, src_ref, first + r, step)
        out_ref[r : r + step, :] = (
            gn_ref[at, :].astype(F32)
            + dot_nt(ga_ref[at, :].astype(BF), w1_ref[0:width, :])
            + dot_nt(rows.astype(BF), w1_ref[width : 2 * width, :])
        )


def merge_body(own, other, *rest, bit):
    n = own.shape[0]
    out_ref = rest[-1]
    side = axis_bit("fine", bit)
    out_ref[pl.ds(pl.multiple_of(side * n, PACK), n), :] = own[...]
    out_ref[pl.ds(pl.multiple_of((1 - side) * n, PACK), n), :] = other[...]


def square_body(own, by_owner, by_chip, by_both, out_ref):
    size = out_ref.shape[0] // 2
    n = own.shape[0] - PACK
    half, chip = axis_bit("coarse", 0), axis_bit("fine", 1)
    for block, i, j in ((own, half, chip), (by_owner, 1 - half, chip), (by_chip, half, 1 - chip), (by_both, 1 - half, 1 - chip)):
        out_ref[pl.ds(pl.multiple_of(j * size + i * n, PACK), n), :] = block[0:n, :]
    for block, j in ((own, chip), (by_chip, 1 - chip)):
        out_ref[pl.ds(pl.multiple_of(j * size + 2 * n, PACK), PACK), :] = block[n:, :]


def weights_body(own, other, w1_ref, gb_ref, wo_ref, up_ref, *, per, edge_scale, cell_scale):
    width = own.shape[1]
    core = lax.axis_index("fine") % 2
    outs = ((w1_ref, 0, edge_scale), (w1_ref, width, edge_scale), (wo_ref, 0, edge_scale), (up_ref, 0, cell_scale))
    size = per + PACK
    n = min(per, width)
    for index in range(lax.axis_size("fine")):
        at = slice((index // 2) * size, (index // 2 + 1) * size)
        value = jnp.where(core == index % 2, own[at, :].astype(F32), other[at, :].astype(F32))
        if index == 0:
            gb_ref[...] = (value[per : per + 1] + value[per + 1 : per + 2]) * edge_scale
        for r in range(0, per, n):
            which, row = divmod(index * per + r, width)
            out_ref, start, scale = outs[which]
            out_ref[start + row : start + row + n, :] = value[r : r + n] * scale


def table_body(*refs):
    *pool_refs, own_back, other_back, lists_ref, table = refs
    lists = lists_ref[...]
    core = lax.axis_index("fine") % 2
    side = own_back.shape[0]
    returned = jnp.concatenate([own_back[...], other_back[...]], axis=0)
    first, second = lists[:, :side], lists[:, side:]
    lists = jnp.where(core == 0, jnp.concatenate([second, first], axis=1), lists)
    step = pool_refs[0].shape[0]
    for i, pool_ref in enumerate(pool_refs):
        add = dot(hot_columns(lists, step, i * step), returned)
        table[i * step : (i + 1) * step, :] = (pool_ref[...] + add).astype(BF)


def feats_body(table, ids_ref, grad_ref, *rest, first, count):
    out_hbm, token_ref, out, sem = rest[-4:]
    token_ref[...] = jnp.zeros_like(token_ref)
    cells = table.shape[0]
    block = 256
    for t in range(0, count, block):
        at = slice(first + t, first + t + block)
        rows = dot(hot_rows(ids_ref[:, at], cells), table[...])
        out[t : t + block, :] = (grad_ref[at, :].astype(F32) + rows).astype(BF)
    copy = pltpu.make_async_copy(out, out_hbm.at[first : first + count, :], sem)
    copy.start()
    copy.wait()


def local(
    node_feats, grad_out, cluster_ids, halo_lists, edge_sources, w_edge_in, b_edge_in, w_edge_out, w_unpool,
):
    nodes, width = node_feats.shape
    cells = edge_sources.shape[0] // K
    half = cells // 2
    side = halo_lists.shape[0] // 2
    fines, coarses = lax.axis_size("fine"), lax.axis_size("coarse")
    fine_bits, coarse_bits = bits_of(fines), bits_of(coarses)
    ids = call(
        functools.partial(local_body, cells=cells), (sds((1, nodes), jnp.int32),), (cluster_ids.reshape(1, nodes),), AHEAD
    )[0]
    lists = halo_lists.reshape(1, 2 * side)
    flat = edge_sources.reshape(cells * K // LANES, LANES)
    src = call(
        source_body, (sds((K, cells), jnp.int32),), (flat,), 0, scratch=(pltpu.VMEM(flat.shape, jnp.int32),)
    )[0]
    bias = b_edge_in.reshape(1, width)

    def pool(x, pieces):
        outs = (sds((half, width), F32),) + (sds((half // pieces, width), F32),) * pieces
        keep, *sends = call(pool_body, outs, (ids, x), 2 * nodes * cells * width)
        outs = (sds((half, width), F32), sds((half, width), BF))
        return call(chip_body, outs, (keep, *[swap(send, "fine", 0) for send in sends]), 0)

    def across(part, send, after=()):
        for bit in range(1, fine_bits):
            recv = swap(send, "fine", bit)
            last = bit == fine_bits - 1
            outs = (sds((half, width), BF),) if last else (sds((half, width), F32), sds((half, width), BF))
            part, send = (*call(across_body, outs, (part, recv), 0, after=after), None)[:2]
        return part

    part_p, send_p = pool(node_feats, 1)
    part_g, send_g = pool(grad_out, 4)
    picked = call(pick_body, (sds((2 * side, width), BF),), (send_p, lists), 0)[0]
    sent = call(side_body, (sds((side, width), BF),), (picked, swap(picked, "fine", 0)), 0)[0]
    own_halo = call(
        halo_sum_body, (sds((side, width), BF),), [send_sides(sent, d) for d in range(fines // 2)], 0,
        scratch=(pltpu.VMEM((fines // 2, side, width), F32),),
    )[0]
    own_p = across(part_p, send_p, after=(own_halo, src, bias))
    other_halo = swap(own_halo, "fine", 0)
    others = [swap(x, "fine", 0) for x in (own_p[: half // 2], own_p[half // 2 :])]
    near = call(near_body, (sds((K * cells, width), BF),), (own_p, src), 0, vmem=24)[0]
    table, far, base = call(
        extend_body,
        (sds((cells, width), BF), sds((half + 2 * side, width), BF), sds((cells, width), F32)),
        (*others, own_p, own_halo, other_halo, w_edge_in, bias),
        0,
    )

    def forward(first, count, after=(), tokens=()):
        edges = count * cells
        return call(
            functools.partial(forward_body, first=first),
            (sds((cells, width), F32), sds((edges, width), F32), sds((edges, width), BF), *tokens),
            (base, far, near, src, w_edge_in),
            0,
            vmem=32,
            after=after,
        )

    *front, front_token = forward(0, EARLY, tokens=(sds((8, LANES), F32),))
    own_g = across(part_g, send_g, after=(front_token,))
    other_g = swap(own_g, "fine", 0)
    rear = forward(EARLY, K - EARLY, after=(own_g,))
    per = 4 * width // fines
    first = per // 2
    act, ga, gn, keep, send, bias_sum = call(
        backward_body,
        (
            sds((K * cells, width), BF), sds((cells, width), F32), sds((cells, width), BF),
            sds((first, width), F32), sds((first + PACK, width), BF), sds((8, width), F32),
        ),
        (own_g, other_g, table, *front, *rear, w_edge_out, w_unpool),
        2 * K * cells * width * width,
        vmem=32,
        scratch=(pltpu.VMEM((cells, width), BF), pltpu.VMEM((per, width), F32)),
    )

    back = call(
        back_body, (sds((side, width), BF),), (act, src, w_edge_in), 4 * K * side * cells * width,
        scratch=(pltpu.VMEM((2 * side, width), F32),),
    )[0]
    own_back = send_sides(back)
    other_back = swap(own_back, "fine", 0)
    cell_grads = [
        call(
            functools.partial(cell_grad_body, first=at),
            (sds((half, width), F32),),
            (act, src, ga, gn, w_edge_in),
            2 * K * half * cells * width,
        )[0]
        for at in (0, half)
    ]
    table = call(
        table_body, (sds((cells, width), BF),), (*cell_grads, own_back, other_back, lists), 0
    )[0]

    def feats(first, count, after=(), into=None):
        return call(
            functools.partial(feats_body, first=first, count=count),
            (sds((nodes, width), BF), sds((8, LANES), F32)),
            (table, ids, grad_out),
            2 * count * cells * width,
            vmem=24,
            scratch=(pltpu.VMEM((count, width), BF), pltpu.SemaphoreType.DMA(())),
            after=after,
            into=into,
            far=1,
        )

    after = {1: (back,), 2: (cell_grads[0],)}
    for bit in range(1, coarse_bits):
        recv = swap(send, "coarse", bit - 1)
        keep, send, bias_sum = call(
            functools.partial(stage_body, bit=bit),
            (sds((first, width), F32), sds((first + PACK, width), BF), sds((8, width), F32)),
            (keep, recv, bias_sum),
            0,
            scratch=(pltpu.VMEM((first, width), F32),),
            after=after.get(bit, ()),
        )
    recv = swap(send, "coarse", coarse_bits - 1)
    front_rows = nodes // 4
    grad_feats, feats_token = feats(0, front_rows)
    part = call(
        end_body, (sds((first + PACK, width), BF),), (keep, recv, bias_sum), 0,
        after=(feats_token,),
    )[0]
    grad_feats, feats_token = feats(front_rows, nodes - front_rows, after=(part,), into=grad_feats)
    near = [swap(part, "coarse", 0), swap(part, "fine", 1), swap_both(part)]
    part = call(
        square_body, (sds((2 * (per + PACK), width), BF),), (part, *near), 0, after=(feats_token,)
    )[0]
    for bit in range(2, fine_bits):
        other = swap(part, "fine", bit)
        body = functools.partial(merge_body, bit=bit)
        part = call(body, (sds((2 * part.shape[0], width), BF),), (part, other), 0)[0]
    other = swap(part, "fine", 0)
    total_cells = cells * coarses
    scales = dict(edge_scale=float(total_cells * K) ** -0.5, cell_scale=float(total_cells) ** -0.5)
    grad_w1, grad_b, grad_wo, grad_up = call(
        functools.partial(weights_body, per=per, **scales),
        (
            sds((2 * width, width), F32), sds((1, width), F32), sds((width, width), F32), sds((width, width), F32),
        ),
        (part, other),
        0,
    )
    return grad_feats, grad_w1, grad_b.reshape(width), grad_wo, grad_up


def solution(mesh):
    both = ("coarse", "fine")
    return jax.shard_map(
        local,
        mesh=mesh,
        in_specs=(P(both, None), P(both, None), P(both), P("coarse"), P("coarse"), P(), P(), P(), P()),
        out_specs=(P(both, None), P(), P(), P(), P()),
        check_vma=False,
    )
```

```python
import functools

import jax
import jax.numpy as jnp
from jax import lax
from jax.experimental import pallas as pl
from jax.experimental.pallas import tpu as pltpu
from jax.sharding import PartitionSpec as P

K = 4
EARLY = 2
BF = jnp.bfloat16
F32 = jnp.float32
LANES = 128
PACK = 16
MIB = 1 << 20
AHEAD = 10**9


def dot(a, b):
    return jnp.dot(a, b, preferred_element_type=F32)


def dot_nt(a, b):
    return lax.dot_general(a, b, (((1,), (1,)), ((), ())), preferred_element_type=F32)


def dot_tn(a, b):
    return lax.dot_general(a, b, (((0,), (0,)), ((), ())), preferred_element_type=F32)


def bits_of(count):
    assert count > 1 and count & (count - 1) == 0
    return count.bit_length() - 1


def swap(x, axis, bit):
    count = lax.axis_size(axis)
    return lax.ppermute(x, axis, [(i, i ^ (1 << bit)) for i in range(count)])


def swap_both(x):
    owners, fines = lax.axis_size("coarse"), lax.axis_size("fine")
    pairs = [(g * fines + f, (g ^ 1) * fines + (f ^ 2)) for g in range(owners) for f in range(fines)]
    return lax.ppermute(x, ("coarse", "fine"), pairs)


def send_sides(x, flip=0):
    owners, fines = lax.axis_size("coarse"), lax.axis_size("fine")
    pairs = [
        (g * fines + f, (g + 1 - 2 * (f % 2)) % owners * fines + (f ^ (2 * flip)))
        for g in range(owners)
        for f in range(fines)
    ]
    return lax.ppermute(x, ("coarse", "fine"), pairs)


def call(body, outs, args, flops, vmem=16, scratch=(), after=(), into=None, far=0):
    moved = sum(a.size * a.dtype.itemsize for a in (*args, *outs)) if flops else 0
    count = len(args)
    unseen = (*after, into) if into is not None else after
    waited = len(unseen)

    def kernel(*refs):
        body(*refs[:count], *refs[count + waited :])

    anywhere = pl.BlockSpec(memory_space=pl.ANY)
    in_vmem = pl.BlockSpec(memory_space=pltpu.VMEM)
    places = tuple([anywhere] * far + [in_vmem] * (len(outs) - far))
    return pl.pallas_call(
        kernel,
        out_shape=outs,
        in_specs=[in_vmem] * count + [anywhere] * waited,
        out_specs=places,
        scratch_shapes=scratch,
        input_output_aliases={} if into is None else {count + waited - 1: 0},
        compiler_params=pltpu.CompilerParams(vmem_limit_bytes=vmem * MIB),
        cost_estimate=pl.CostEstimate(flops=int(flops), bytes_accessed=int(moved), transcendentals=0),
    )(*args, *unseen)


def sds(shape, dtype):
    return jax.ShapeDtypeStruct(shape, dtype)


def column(row):
    blocks = [
        jnp.broadcast_to(row[:, i : i + LANES], (LANES, LANES)).T
        for i in range(0, row.shape[1], LANES)
    ]
    return blocks[0] if len(blocks) == 1 else jnp.concatenate(blocks, axis=0)


def hot_rows(row, width):
    ids = column(row)
    ids = jnp.concatenate([ids] * (width // LANES), axis=1)
    lane = lax.broadcasted_iota(jnp.int32, ids.shape, 1)
    return jnp.where(lane == ids, 1.0, 0.0).astype(BF)


def hot_columns(row, height, start=0):
    shape = (height, row.shape[1])
    at = lax.broadcasted_iota(jnp.int32, shape, 0)
    return jnp.where(at == row - start, 1.0, 0.0).astype(BF)


def local_body(ids_ref, out_ref, *, cells):
    out_ref[...] = lax.rem(ids_ref[...], cells)


def source_body(src_ref, out_ref, mixed):
    per = LANES // K
    src = src_ref[...]
    at = lax.broadcasted_iota(jnp.int32, (LANES, LANES), 0)
    to = lax.broadcasted_iota(jnp.int32, (LANES, LANES), 1)
    order = jnp.where(to == (at % K) * per + at // K, 1.0, 0.0).astype(BF)
    high = lax.shift_right_logical(src, 6)
    low = (src - 64 * high).astype(F32).astype(BF)
    high = high.astype(F32).astype(BF)
    mixed[...] = (64.0 * dot(high, order) + dot(low, order)).astype(jnp.int32)
    count = mixed.shape[0] // K
    lane = lax.broadcasted_iota(jnp.int32, (count, LANES), 1) // per
    quarters = [mixed[pl.ds(j, count, stride=K), :] for j in range(K)]
    for k in range(K):
        rows = jnp.zeros((count, LANES), jnp.int32)
        for j in range(K):
            turned = quarters[j] if j == k else pltpu.roll(quarters[j], (j - k) % K * per, 1)
            rows = jnp.where(lane == j, turned, rows)
        for q in range(count):
            out_ref[k : k + 1, q * LANES : (q + 1) * LANES] = rows[q : q + 1, :]


def pool_body(ids_ref, x_ref, out_ref, *, other):
    half = out_ref.shape[0]
    core = lax.axis_index("fine") % 2
    first = ((1 - core) if other else core) * half
    ids = ids_ref[...] - first
    step = min(256, half)
    for t in range(0, half, step):
        out_ref[t : t + step, :] = dot(hot_columns(ids, step, t), x_ref[...])


def pick_body(part_ref, lists_ref, out_ref):
    half = part_ref.shape[0]
    core = lax.axis_index("fine") % 2
    out_ref[...] = dot(hot_rows(lists_ref[...] - core * half, half), part_ref[...]).astype(BF)


def side_body(own, other, out_ref):
    side = out_ref.shape[0]
    core = lax.axis_index("fine") % 2
    at = pl.ds(pl.multiple_of(core * side, side), side)
    out_ref[...] = own[at, :] + other[at, :]


def halo_sum_body(*refs):
    *parts, out_ref, slots = refs
    chip = lax.axis_index("fine") // 2
    for offset, part in enumerate(parts):
        slots[chip ^ offset] = part[...].astype(F32)
    total = slots[0]
    for i in range(1, len(parts)):
        total = total + slots[i]
    out_ref[...] = total.astype(BF)


def chip_body(keep, recv, part_ref, send_ref):
    total = keep[...] + recv[...]
    part_ref[...] = total
    send_ref[...] = total.astype(BF)


def across_body(part, recv, *out_refs):
    total = part[...] + recv[...].astype(F32)
    for ref in out_refs:
        ref[...] = total.astype(ref.dtype)


def core_order(half):
    core = lax.axis_index("fine") % 2
    at_own = pl.ds(pl.multiple_of(core * half, half), half)
    at_other = pl.ds(pl.multiple_of((1 - core) * half, half), half)
    return at_own, at_other


def near_body(own_p, src_ref, near):
    half = own_p.shape[0]
    cells = 2 * half
    core = lax.axis_index("fine") % 2
    block = 512
    for k in range(K):
        for t in range(0, cells, block):
            hot = hot_rows(src_ref[k : k + 1, t : t + block] - core * half, half)
            near[k * cells + t : k * cells + t + block, :] = dot(hot, own_p[...]).astype(BF)


def extend_body(*refs):
    *others, own_p, own_halo, other_halo, w1_ref, b_ref, table, far, base = refs
    half, width = own_p.shape
    side = own_halo.shape[0]
    core = lax.axis_index("fine") % 2
    n = half // len(others)
    for i, other in enumerate(others):
        far[i * n : (i + 1) * n, :] = other[...]
    far[pl.ds(pl.multiple_of(half + core * side, PACK), side), :] = own_halo[...]
    far[pl.ds(pl.multiple_of(half + (1 - core) * side, PACK), side), :] = other_halo[...]
    at_own, at_other = core_order(half)
    table[at_own, :] = own_p[...]
    table[at_other, :] = far[0:half, :]
    base[...] = dot(table[...], w1_ref[0:width, :]) + b_ref[...].astype(F32)


def forward_body(base, far, near, src_ref, w1_ref, hid, slope, feats, *tokens, first):
    cells, width = base.shape
    half = cells // 2
    core = lax.axis_index("fine") % 2
    for ref in tokens:
        ref[...] = jnp.zeros_like(ref)
    block = 512
    for i in range(slope.shape[0] // cells):
        for t in range(0, cells, block):
            src = src_ref[first + i : first + i + 1, t : t + block]
            mine = jnp.logical_and(src >= core * half, src < (core + 1) * half)
            place = jnp.where(src >= cells, src - half, src - (1 - core) * half)
            picked = dot(hot_rows(jnp.where(mine, -1, place), far.shape[0]), far[...])
            here = slice((first + i) * cells + t, (first + i) * cells + t + block)
            feats[i * cells + t : i * cells + t + block, :] = (picked + near[here, :].astype(F32)).astype(BF)
        at = slice(i * cells, (i + 1) * cells)
        pre = base[...] + dot(feats[at, :], w1_ref[width : 2 * width, :])
        sig = 0.5 * jnp.tanh(0.5 * pre) + 0.5
        hidden = pre * sig
        hid[...] = hidden if i == 0 else hid[...] + hidden
        slope[at, :] = sig + hidden * (1.0 - sig)


def split(x):
    high = x.astype(BF)
    return high, (x - high.astype(F32)).astype(BF)


def bias_rows(bias):
    high, low = (part.astype(F32) for part in split(bias))
    at = lax.broadcasted_iota(jnp.int32, (PACK, bias.shape[1]), 0)
    return jnp.where(at == 0, high, jnp.where(at == 1, low, 0.0)).astype(BF), high + low


def axis_bit(axis, bit):
    return lax.rem(lax.axis_index(axis) // (1 << bit), 2)


def emit(total_ref, bias, bit, keep_ref, send_ref, bias_ref):
    n = keep_ref.shape[0]
    if n == total_ref.shape[0]:
        sent = total_ref[...].astype(BF)
        keep_ref[...] = sent.astype(F32)
    else:
        side = axis_bit("coarse", bit)
        keep_ref[...] = total_ref[pl.ds(pl.multiple_of(side * n, n), n), :]
        sent = total_ref[pl.ds(pl.multiple_of((1 - side) * n, n), n), :].astype(BF)
    rows, bias = bias_rows(bias)
    send_ref[0:n, :] = sent
    send_ref[n : n + PACK, :] = rows
    bias_ref[...] = jnp.broadcast_to(bias, bias_ref.shape)


def backward_body(
    own_g, other_g, table, hid_1, slope_1, feats_1, hid_2, slope_2, feats_2, wo_ref, wu_ref,
    act, ga_ref, gn_ref, keep_ref, send_ref, bias_ref,
    gsum, total,
):
    half, width = own_g.shape
    cells = 2 * half
    fine = lax.axis_index("fine")
    at_own, at_other = core_order(half)
    gsum[at_own, :] = own_g[...]
    gsum[at_other, :] = other_g[...]
    gn = dot_nt(gsum[...], wu_ref[...]).astype(BF)
    gn_ref[...] = gn
    grad = dot_nt(gn, wo_ref[...])
    ga = jnp.zeros((cells, width), F32)
    for k in range(K):
        at = slice(k * cells, (k + 1) * cells)
        slope, here = (slope_1, k) if k < EARLY else (slope_2, k - EARLY)
        part = (grad * slope[here * cells : (here + 1) * cells, :]).astype(BF)
        act[at, :] = part
        ga = ga + part.astype(F32)
    ga_ref[...] = ga

    fines = lax.axis_size("fine")
    per = 4 * width // fines
    n = min(per, width)
    for index in range(fines):

        @pl.when(fine == index)
        def _():
            for r in range(0, per, n):
                which, first = divmod(index * per + r, width)
                cols = slice(first, first + n)
                if which == 0:
                    high, low = split(ga_ref[...])
                    left = table[:, cols]
                    out = dot_tn(left, high) + dot_tn(left, low)
                elif which == 1:
                    n_1 = feats_1.shape[0]
                    out = dot_tn(feats_1[:, cols], act[0:n_1, :]) + dot_tn(feats_2[:, cols], act[n_1:, :])
                elif which == 2:
                    high, low = split(hid_1[:, cols] + hid_2[:, cols])
                    out = dot_tn(high, gn_ref[...]) + dot_tn(low, gn_ref[...])
                else:
                    high, low = split(hid_1[...] + hid_2[...])
                    agg = dot(high, wo_ref[:, cols]) + dot(low, wo_ref[:, cols])
                    new = (table[:, cols].astype(F32) + agg).astype(BF)
                    out = dot_tn(new, gsum[...])
                total[r : r + n, :] = out

    emit(total, jnp.sum(ga_ref[...], axis=0, keepdims=True), 0, keep_ref, send_ref, bias_ref)


def received_bias(recv, n):
    return recv[n : n + 1, :].astype(F32) + recv[n + 1 : n + 2, :].astype(F32)


def stage_body(keep_in, recv, bias_in, keep_ref, send_ref, bias_ref, total, *, bit):
    n = keep_in.shape[0]
    total[...] = keep_in[...] + recv[0:n, :].astype(F32)
    emit(total, bias_in[0:1, :] + received_bias(recv, n), bit, keep_ref, send_ref, bias_ref)


def end_body(keep_in, recv, bias_in, out_ref):
    n = keep_in.shape[0]
    out_ref[0:n, :] = (keep_in[...] + recv[0:n, :].astype(F32)).astype(BF)
    out_ref[n : n + PACK, :] = bias_rows(bias_in[0:1, :] + received_bias(recv, n))[0]


def scatter(act, src_ref, first, count):
    cells = src_ref.shape[1]
    out = jnp.zeros((count, act.shape[1]), F32)
    for k in range(K):
        hot = hot_columns(src_ref[k : k + 1, :], count, first)
        out += dot(hot, act[k * cells : (k + 1) * cells, :])
    return out


def back_body(act, src_ref, w1_ref, out_ref, both):
    side, width = out_ref.shape
    rows = scatter(act, src_ref, src_ref.shape[1], 2 * side)
    both[...] = dot_nt(rows.astype(BF), w1_ref[width : 2 * width, :])
    core = lax.axis_index("fine") % 2
    out_ref[...] = both[pl.ds(pl.multiple_of((1 - core) * side, side), side), :].astype(BF)


def cell_grad_body(act, src_ref, ga_ref, gn_ref, w1_ref, out_ref, *, first):
    count, width = out_ref.shape
    step = min(512, count)
    for r in range(0, count, step):
        at = slice(first + r, first + r + step)
        rows = scatter(act, src_ref, first + r, step)
        out_ref[r : r + step, :] = (
            gn_ref[at, :].astype(F32)
            + dot_nt(ga_ref[at, :].astype(BF), w1_ref[0:width, :])
            + dot_nt(rows.astype(BF), w1_ref[width : 2 * width, :])
        )


def merge_body(own, other, *rest, bit):
    n = own.shape[0]
    out_ref = rest[-1]
    side = axis_bit("fine", bit)
    out_ref[pl.ds(pl.multiple_of(side * n, PACK), n), :] = own[...]
    out_ref[pl.ds(pl.multiple_of((1 - side) * n, PACK), n), :] = other[...]


def square_body(own, by_owner, by_chip, by_both, out_ref):
    size = out_ref.shape[0] // 2
    n = own.shape[0] - PACK
    half, chip = axis_bit("coarse", 0), axis_bit("fine", 1)
    for block, i, j in ((own, half, chip), (by_owner, 1 - half, chip), (by_chip, half, 1 - chip), (by_both, 1 - half, 1 - chip)):
        out_ref[pl.ds(pl.multiple_of(j * size + i * n, PACK), n), :] = block[0:n, :]
    for block, j in ((own, chip), (by_chip, 1 - chip)):
        out_ref[pl.ds(pl.multiple_of(j * size + 2 * n, PACK), PACK), :] = block[n:, :]


def weights_body(own, other, w1_ref, gb_ref, wo_ref, up_ref, *, per, edge_scale, cell_scale):
    width = own.shape[1]
    core = lax.axis_index("fine") % 2
    outs = ((w1_ref, 0, edge_scale), (w1_ref, width, edge_scale), (wo_ref, 0, edge_scale), (up_ref, 0, cell_scale))
    size = per + PACK
    n = min(per, width)
    for index in range(lax.axis_size("fine")):
        at = slice((index // 2) * size, (index // 2 + 1) * size)
        value = jnp.where(core == index % 2, own[at, :].astype(F32), other[at, :].astype(F32))
        if index == 0:
            gb_ref[...] = (value[per : per + 1] + value[per + 1 : per + 2]) * edge_scale
        for r in range(0, per, n):
            which, row = divmod(index * per + r, width)
            out_ref, start, scale = outs[which]
            out_ref[start + row : start + row + n, :] = value[r : r + n] * scale


def table_body(*refs):
    *pool_refs, own_back, other_back, lists_ref, table = refs
    lists = lists_ref[...]
    core = lax.axis_index("fine") % 2
    side = own_back.shape[0]
    returned = jnp.concatenate([own_back[...], other_back[...]], axis=0)
    first, second = lists[:, :side], lists[:, side:]
    lists = jnp.where(core == 0, jnp.concatenate([second, first], axis=1), lists)
    step = pool_refs[0].shape[0]
    for i, pool_ref in enumerate(pool_refs):
        add = dot(hot_columns(lists, step, i * step), returned)
        table[i * step : (i + 1) * step, :] = (pool_ref[...] + add).astype(BF)


def feats_body(table, ids_ref, grad_ref, *rest, first, count):
    out_hbm, token_ref, out, sem = rest[-4:]
    token_ref[...] = jnp.zeros_like(token_ref)
    cells = table.shape[0]
    block = 256
    for t in range(0, count, block):
        at = slice(first + t, first + t + block)
        rows = dot(hot_rows(ids_ref[:, at], cells), table[...])
        out[t : t + block, :] = (grad_ref[at, :].astype(F32) + rows).astype(BF)
    copy = pltpu.make_async_copy(out, out_hbm.at[first : first + count, :], sem)
    copy.start()
    copy.wait()


def local(
    node_feats, grad_out, cluster_ids, halo_lists, edge_sources, w_edge_in, b_edge_in, w_edge_out, w_unpool,
):
    nodes, width = node_feats.shape
    cells = edge_sources.shape[0] // K
    half = cells // 2
    side = halo_lists.shape[0] // 2
    fines, coarses = lax.axis_size("fine"), lax.axis_size("coarse")
    fine_bits, coarse_bits = bits_of(fines), bits_of(coarses)
    ids = call(
        functools.partial(local_body, cells=cells), (sds((1, nodes), jnp.int32),), (cluster_ids.reshape(1, nodes),), AHEAD
    )[0]
    lists = halo_lists.reshape(1, 2 * side)
    flat = edge_sources.reshape(cells * K // LANES, LANES)
    src = call(
        source_body, (sds((K, cells), jnp.int32),), (flat,), 0, scratch=(pltpu.VMEM(flat.shape, jnp.int32),)
    )[0]
    bias = b_edge_in.reshape(1, width)

    def half_sums(x, other, after=()):
        body = functools.partial(pool_body, other=other)
        return call(body, (sds((half, width), F32),), (ids, x), nodes * cells * width, after=after)[0]

    def chip_sums(keep, recv, after=()):
        outs = (sds((half, width), F32), sds((half, width), BF))
        return call(chip_body, outs, (keep, recv), 0, after=after)

    def across(part, send, after=()):
        for bit in range(1, fine_bits):
            recv = swap(send, "fine", bit)
            last = bit == fine_bits - 1
            outs = (sds((half, width), BF),) if last else (sds((half, width), F32), sds((half, width), BF))
            part, send = (*call(across_body, outs, (part, recv), 0, after=after), None)[:2]
        return part

    recv_p = swap(half_sums(node_feats, True), "fine", 0)
    recv_g = swap(half_sums(grad_out, True), "fine", 0)
    part_p, send_p = chip_sums(half_sums(node_feats, False), recv_p)
    picked = call(pick_body, (sds((2 * side, width), BF),), (send_p, lists), 0)[0]
    sent = call(side_body, (sds((side, width), BF),), (picked, swap(picked, "fine", 0)), 0)[0]
    part_g, send_g = chip_sums(half_sums(grad_out, False, after=(send_p,)), recv_g)
    own_halo = call(
        halo_sum_body, (sds((side, width), BF),), [send_sides(sent, d) for d in range(fines // 2)], 0,
        scratch=(pltpu.VMEM((fines // 2, side, width), F32),),
    )[0]
    own_p = across(part_p, send_p, after=(own_halo, src, bias))
    other_halo = swap(own_halo, "fine", 0)
    others = [swap(x, "fine", 0) for x in (own_p[: half // 2], own_p[half // 2 :])]
    near = call(near_body, (sds((K * cells, width), BF),), (own_p, src), 0, vmem=24)[0]
    table, far, base = call(
        extend_body,
        (sds((cells, width), BF), sds((half + 2 * side, width), BF), sds((cells, width), F32)),
        (*others, own_p, own_halo, other_halo, w_edge_in, bias),
        0,
    )

    def forward(first, count, after=(), tokens=()):
        edges = count * cells
        return call(
            functools.partial(forward_body, first=first),
            (sds((cells, width), F32), sds((edges, width), F32), sds((edges, width), BF), *tokens),
            (base, far, near, src, w_edge_in),
            0,
            vmem=32,
            after=after,
        )

    *front, front_token = forward(0, EARLY, tokens=(sds((8, LANES), F32),))
    own_g = across(part_g, send_g, after=(front_token,))
    other_g = swap(own_g, "fine", 0)
    rear = forward(EARLY, K - EARLY, after=(own_g,))
    per = 4 * width // fines
    first = per // 2
    act, ga, gn, keep, send, bias_sum = call(
        backward_body,
        (
            sds((K * cells, width), BF), sds((cells, width), F32), sds((cells, width), BF),
            sds((first, width), F32), sds((first + PACK, width), BF), sds((8, width), F32),
        ),
        (own_g, other_g, table, *front, *rear, w_edge_out, w_unpool),
        2 * K * cells * width * width,
        vmem=32,
        scratch=(pltpu.VMEM((cells, width), BF), pltpu.VMEM((per, width), F32)),
    )

    back = call(
        back_body, (sds((side, width), BF),), (act, src, w_edge_in), 4 * K * side * cells * width,
        scratch=(pltpu.VMEM((2 * side, width), F32),),
    )[0]
    own_back = send_sides(back)
    other_back = swap(own_back, "fine", 0)
    cell_grads = [
        call(
            functools.partial(cell_grad_body, first=at),
            (sds((half, width), F32),),
            (act, src, ga, gn, w_edge_in),
            2 * K * half * cells * width,
        )[0]
        for at in (0, half)
    ]
    table = call(
        table_body, (sds((cells, width), BF),), (*cell_grads, own_back, other_back, lists), 0
    )[0]

    def feats(first, count, after=(), into=None):
        return call(
            functools.partial(feats_body, first=first, count=count),
            (sds((nodes, width), BF), sds((8, LANES), F32)),
            (table, ids, grad_out),
            2 * count * cells * width,
            vmem=24,
            scratch=(pltpu.VMEM((count, width), BF), pltpu.SemaphoreType.DMA(())),
            after=after,
            into=into,
            far=1,
        )

    after = {1: (back,), 2: (cell_grads[0],)}
    for bit in range(1, coarse_bits):
        recv = swap(send, "coarse", bit - 1)
        keep, send, bias_sum = call(
            functools.partial(stage_body, bit=bit),
            (sds((first, width), F32), sds((first + PACK, width), BF), sds((8, width), F32)),
            (keep, recv, bias_sum),
            0,
            scratch=(pltpu.VMEM((first, width), F32),),
            after=after.get(bit, ()),
        )
    recv = swap(send, "coarse", coarse_bits - 1)
    front_rows = nodes // 4
    grad_feats, feats_token = feats(0, front_rows)
    part = call(
        end_body, (sds((first + PACK, width), BF),), (keep, recv, bias_sum), 0,
        after=(feats_token,),
    )[0]
    grad_feats, feats_token = feats(front_rows, nodes - front_rows, after=(part,), into=grad_feats)
    near = [swap(part, "coarse", 0), swap(part, "fine", 1), swap_both(part)]
    part = call(
        square_body, (sds((2 * (per + PACK), width), BF),), (part, *near), 0, after=(feats_token,)
    )[0]
    for bit in range(2, fine_bits):
        other = swap(part, "fine", bit)
        body = functools.partial(merge_body, bit=bit)
        part = call(body, (sds((2 * part.shape[0], width), BF),), (part, other), 0)[0]
    other = swap(part, "fine", 0)
    total_cells = cells * coarses
    scales = dict(edge_scale=float(total_cells * K) ** -0.5, cell_scale=float(total_cells) ** -0.5)
    grad_w1, grad_b, grad_wo, grad_up = call(
        functools.partial(weights_body, per=per, **scales),
        (
            sds((2 * width, width), F32), sds((1, width), F32), sds((width, width), F32), sds((width, width), F32),
        ),
        (part, other),
        0,
    )
    return grad_feats, grad_w1, grad_b.reshape(width), grad_wo, grad_up


def solution(mesh):
    both = ("coarse", "fine")
    return jax.shard_map(
        local,
        mesh=mesh,
        in_specs=(P(both, None), P(both, None), P(both), P("coarse"), P("coarse"), P(), P(), P(), P()),
        out_specs=(P(both, None), P(), P(), P(), P()),
        check_vma=False,
    )
```

```python
import functools

import jax
import jax.numpy as jnp
from jax import lax
from jax.experimental import pallas as pl
from jax.experimental.pallas import tpu as pltpu
from jax.sharding import PartitionSpec as P

K = 4
EARLY = 2
BF = jnp.bfloat16
F32 = jnp.float32
LANES = 128
PACK = 16
MIB = 1 << 20
AHEAD = 10**9


def dot(a, b):
    return jnp.dot(a, b, preferred_element_type=F32)


def dot_nt(a, b):
    return lax.dot_general(a, b, (((1,), (1,)), ((), ())), preferred_element_type=F32)


def dot_tn(a, b):
    return lax.dot_general(a, b, (((0,), (0,)), ((), ())), preferred_element_type=F32)


def bits_of(count):
    assert count > 1 and count & (count - 1) == 0
    return count.bit_length() - 1


def swap(x, axis, bit):
    count = lax.axis_size(axis)
    return lax.ppermute(x, axis, [(i, i ^ (1 << bit)) for i in range(count)])


def swap_owners(x):
    return lax.ppermute(x, "coarse", [(i, i ^ 3) for i in range(lax.axis_size("coarse"))])


def swap_both(x):
    owners, fines = lax.axis_size("coarse"), lax.axis_size("fine")
    pairs = [(g * fines + f, (g ^ 1) * fines + (f ^ 2)) for g in range(owners) for f in range(fines)]
    return lax.ppermute(x, ("coarse", "fine"), pairs)


def send_sides(x, flip=0):
    owners, fines = lax.axis_size("coarse"), lax.axis_size("fine")
    pairs = [
        (g * fines + f, (g + 1 - 2 * (f % 2)) % owners * fines + (f ^ (2 * flip)))
        for g in range(owners)
        for f in range(fines)
    ]
    return lax.ppermute(x, ("coarse", "fine"), pairs)


def call(body, outs, args, flops, vmem=16, scratch=(), after=(), into=None, far=0):
    moved = sum(a.size * a.dtype.itemsize for a in (*args, *outs)) if flops else 0
    count = len(args)
    unseen = (*after, into) if into is not None else after
    waited = len(unseen)

    def kernel(*refs):
        body(*refs[:count], *refs[count + waited :])

    anywhere = pl.BlockSpec(memory_space=pl.ANY)
    in_vmem = pl.BlockSpec(memory_space=pltpu.VMEM)
    places = tuple([anywhere] * far + [in_vmem] * (len(outs) - far))
    return pl.pallas_call(
        kernel,
        out_shape=outs,
        in_specs=[in_vmem] * count + [anywhere] * waited,
        out_specs=places,
        scratch_shapes=scratch,
        input_output_aliases={} if into is None else {count + waited - 1: 0},
        compiler_params=pltpu.CompilerParams(vmem_limit_bytes=vmem * MIB),
        cost_estimate=pl.CostEstimate(flops=int(flops), bytes_accessed=int(moved), transcendentals=0),
    )(*args, *unseen)


def sds(shape, dtype):
    return jax.ShapeDtypeStruct(shape, dtype)


def column(row):
    blocks = [
        jnp.broadcast_to(row[:, i : i + LANES], (LANES, LANES)).T
        for i in range(0, row.shape[1], LANES)
    ]
    return blocks[0] if len(blocks) == 1 else jnp.concatenate(blocks, axis=0)


def hot_rows(row, width):
    ids = column(row)
    ids = jnp.concatenate([ids] * (width // LANES), axis=1)
    lane = lax.broadcasted_iota(jnp.int32, ids.shape, 1)
    return jnp.where(lane == ids, 1.0, 0.0).astype(BF)


def hot_columns(row, height, start=0):
    shape = (height, row.shape[1])
    at = lax.broadcasted_iota(jnp.int32, shape, 0)
    return jnp.where(at == row - start, 1.0, 0.0).astype(BF)


def local_body(ids_ref, out_ref, *, cells):
    out_ref[...] = lax.rem(ids_ref[...], cells)


def source_body(src_ref, out_ref, mixed):
    per = LANES // K
    src = src_ref[...]
    at = lax.broadcasted_iota(jnp.int32, (LANES, LANES), 0)
    to = lax.broadcasted_iota(jnp.int32, (LANES, LANES), 1)
    order = jnp.where(to == (at % K) * per + at // K, 1.0, 0.0).astype(BF)
    high = lax.shift_right_logical(src, 6)
    low = (src - 64 * high).astype(F32).astype(BF)
    high = high.astype(F32).astype(BF)
    mixed[...] = (64.0 * dot(high, order) + dot(low, order)).astype(jnp.int32)
    count = mixed.shape[0] // K
    lane = lax.broadcasted_iota(jnp.int32, (count, LANES), 1) // per
    quarters = [mixed[pl.ds(j, count, stride=K), :] for j in range(K)]
    for k in range(K):
        rows = jnp.zeros((count, LANES), jnp.int32)
        for j in range(K):
            turned = quarters[j] if j == k else pltpu.roll(quarters[j], (j - k) % K * per, 1)
            rows = jnp.where(lane == j, turned, rows)
        for q in range(count):
            out_ref[k : k + 1, q * LANES : (q + 1) * LANES] = rows[q : q + 1, :]


def pool_body(ids_ref, x_ref, out_ref, *, other):
    half = out_ref.shape[0]
    core = lax.axis_index("fine") % 2
    first = ((1 - core) if other else core) * half
    ids = ids_ref[...] - first
    step = min(256, half)
    for t in range(0, half, step):
        out_ref[t : t + step, :] = dot(hot_columns(ids, step, t), x_ref[...])


def pick_body(part_ref, lists_ref, out_ref):
    half = part_ref.shape[0]
    core = lax.axis_index("fine") % 2
    out_ref[...] = dot(hot_rows(lists_ref[...] - core * half, half), part_ref[...]).astype(BF)


def side_body(own, other, out_ref):
    side = out_ref.shape[0]
    core = lax.axis_index("fine") % 2
    at = pl.ds(pl.multiple_of(core * side, side), side)
    out_ref[...] = own[at, :] + other[at, :]


def halo_sum_body(*refs):
    *parts, out_ref, slots = refs
    chip = lax.axis_index("fine") // 2
    for offset, part in enumerate(parts):
        slots[chip ^ offset] = part[...].astype(F32)
    total = slots[0]
    for i in range(1, len(parts)):
        total = total + slots[i]
    out_ref[...] = total.astype(BF)


def chip_body(keep, recv, part_ref, send_ref):
    total = keep[...] + recv[...]
    part_ref[...] = total
    send_ref[...] = total.astype(BF)


def across_body(part, recv, *out_refs):
    total = part[...] + recv[...].astype(F32)
    for ref in out_refs:
        ref[...] = total.astype(ref.dtype)


def core_order(half):
    core = lax.axis_index("fine") % 2
    at_own = pl.ds(pl.multiple_of(core * half, half), half)
    at_other = pl.ds(pl.multiple_of((1 - core) * half, half), half)
    return at_own, at_other


def near_body(own_p, src_ref, near):
    half = own_p.shape[0]
    cells = 2 * half
    core = lax.axis_index("fine") % 2
    block = 512
    for k in range(K):
        for t in range(0, cells, block):
            hot = hot_rows(src_ref[k : k + 1, t : t + block] - core * half, half)
            near[k * cells + t : k * cells + t + block, :] = dot(hot, own_p[...]).astype(BF)


def extend_body(*refs):
    *others, own_p, own_halo, other_halo, w1_ref, b_ref, table, far, base = refs
    half, width = own_p.shape
    side = own_halo.shape[0]
    core = lax.axis_index("fine") % 2
    n = half // len(others)
    for i, other in enumerate(others):
        far[i * n : (i + 1) * n, :] = other[...]
    far[pl.ds(pl.multiple_of(half + core * side, PACK), side), :] = own_halo[...]
    far[pl.ds(pl.multiple_of(half + (1 - core) * side, PACK), side), :] = other_halo[...]
    at_own, at_other = core_order(half)
    table[at_own, :] = own_p[...]
    table[at_other, :] = far[0:half, :]
    base[...] = dot(table[...], w1_ref[0:width, :]) + b_ref[...].astype(F32)


def forward_body(base, far, near, src_ref, w1_ref, hid, slope, feats, *tokens, first):
    cells, width = base.shape
    half = cells // 2
    core = lax.axis_index("fine") % 2
    for ref in tokens:
        ref[...] = jnp.zeros_like(ref)
    block = 512
    for i in range(slope.shape[0] // cells):
        for t in range(0, cells, block):
            src = src_ref[first + i : first + i + 1, t : t + block]
            mine = jnp.logical_and(src >= core * half, src < (core + 1) * half)
            place = jnp.where(src >= cells, src - half, src - (1 - core) * half)
            picked = dot(hot_rows(jnp.where(mine, -1, place), far.shape[0]), far[...])
            here = slice((first + i) * cells + t, (first + i) * cells + t + block)
            feats[i * cells + t : i * cells + t + block, :] = (picked + near[here, :].astype(F32)).astype(BF)
        at = slice(i * cells, (i + 1) * cells)
        pre = base[...] + dot(feats[at, :], w1_ref[width : 2 * width, :])
        sig = 0.5 * jnp.tanh(0.5 * pre) + 0.5
        hidden = pre * sig
        hid[...] = hidden if i == 0 else hid[...] + hidden
        slope[at, :] = sig + hidden * (1.0 - sig)


def split(x):
    high = x.astype(BF)
    return high, (x - high.astype(F32)).astype(BF)


def bias_rows(bias):
    high, low = (part.astype(F32) for part in split(bias))
    at = lax.broadcasted_iota(jnp.int32, (PACK, bias.shape[1]), 0)
    return jnp.where(at == 0, high, jnp.where(at == 1, low, 0.0)).astype(BF), high + low


def axis_bit(axis, bit):
    return lax.rem(lax.axis_index(axis) // (1 << bit), 2)


def emit(total, bias, keep_ref, send_ref, bias_ref):
    n = keep_ref.shape[0]
    sent = total.astype(BF)
    keep_ref[...] = sent.astype(F32)
    rows, bias = bias_rows(bias)
    send_ref[0:n, :] = sent
    send_ref[n : n + PACK, :] = rows
    bias_ref[...] = jnp.broadcast_to(bias, bias_ref.shape)


def backward_body(
    own_g, other_g, table, hid_1, slope_1, feats_1, hid_2, slope_2, feats_2, wo_ref, wu_ref,
    act, ga_ref, gn_ref, mine_ref, by_one, by_two, by_both,
    gsum, total,
):
    half, width = own_g.shape
    cells = 2 * half
    fine = lax.axis_index("fine")
    at_own, at_other = core_order(half)
    gsum[at_own, :] = own_g[...]
    gsum[at_other, :] = other_g[...]
    gn = dot_nt(gsum[...], wu_ref[...]).astype(BF)
    gn_ref[...] = gn
    grad = dot_nt(gn, wo_ref[...])
    ga = jnp.zeros((cells, width), F32)
    for k in range(K):
        at = slice(k * cells, (k + 1) * cells)
        slope, here = (slope_1, k) if k < EARLY else (slope_2, k - EARLY)
        part = (grad * slope[here * cells : (here + 1) * cells, :]).astype(BF)
        act[at, :] = part
        ga = ga + part.astype(F32)
    ga_ref[...] = ga

    fines = lax.axis_size("fine")
    per = 4 * width // fines
    n = min(per, width)
    for index in range(fines):

        @pl.when(fine == index)
        def _():
            for r in range(0, per, n):
                which, first = divmod(index * per + r, width)
                cols = slice(first, first + n)
                if which == 0:
                    high, low = split(ga_ref[...])
                    left = table[:, cols]
                    out = dot_tn(left, high) + dot_tn(left, low)
                elif which == 1:
                    n_1 = feats_1.shape[0]
                    out = dot_tn(feats_1[:, cols], act[0:n_1, :]) + dot_tn(feats_2[:, cols], act[n_1:, :])
                elif which == 2:
                    high, low = split(hid_1[:, cols] + hid_2[:, cols])
                    out = dot_tn(high, gn_ref[...]) + dot_tn(low, gn_ref[...])
                else:
                    high, low = split(hid_1[...] + hid_2[...])
                    agg = dot(high, wo_ref[:, cols]) + dot(low, wo_ref[:, cols])
                    new = (table[:, cols].astype(F32) + agg).astype(BF)
                    out = dot_tn(new, gsum[...])
                total[r : r + n, :] = out

    rows = bias_rows(jnp.sum(ga_ref[...], axis=0, keepdims=True))[0]
    half = axis_bit("coarse", 0)
    n = per // 2
    for ref, at in ((mine_ref, half), (by_one, 1 - half), (by_two, half), (by_both, 1 - half)):
        ref[0:n, :] = total[pl.ds(pl.multiple_of(at * n, n), n), :].astype(BF)
        ref[n : n + PACK, :] = rows


def square_sum_body(own, by_both, by_two, by_one, keep_ref, send_ref, bias_ref, slots):
    n = keep_ref.shape[0]
    me = lax.rem(lax.axis_index("coarse"), 4)
    for i, ref in enumerate((own, by_one, by_two, by_both)):
        slots[me ^ i] = ref[...].astype(F32)
    total = slots[0] + slots[1] + slots[2] + slots[3]
    emit(total[0:n], total[n : n + 1] + total[n + 1 : n + 2], keep_ref, send_ref, bias_ref)


def received_bias(recv, n):
    return recv[n : n + 1, :].astype(F32) + recv[n + 1 : n + 2, :].astype(F32)


def stage_body(keep_in, recv, bias_in, keep_ref, send_ref, bias_ref):
    n = keep_in.shape[0]
    total = keep_in[...] + recv[0:n, :].astype(F32)
    emit(total, bias_in[0:1, :] + received_bias(recv, n), keep_ref, send_ref, bias_ref)


def end_body(keep_in, recv, bias_in, out_ref):
    n = keep_in.shape[0]
    out_ref[0:n, :] = (keep_in[...] + recv[0:n, :].astype(F32)).astype(BF)
    out_ref[n : n + PACK, :] = bias_rows(bias_in[0:1, :] + received_bias(recv, n))[0]


def scatter(act, src_ref, first, count):
    cells = src_ref.shape[1]
    out = jnp.zeros((count, act.shape[1]), F32)
    for k in range(K):
        hot = hot_columns(src_ref[k : k + 1, :], count, first)
        out += dot(hot, act[k * cells : (k + 1) * cells, :])
    return out


def back_body(act, src_ref, w1_ref, out_ref, both):
    side, width = out_ref.shape
    rows = scatter(act, src_ref, src_ref.shape[1], 2 * side)
    both[...] = dot_nt(rows.astype(BF), w1_ref[width : 2 * width, :])
    core = lax.axis_index("fine") % 2
    out_ref[...] = both[pl.ds(pl.multiple_of((1 - core) * side, side), side), :].astype(BF)


def cell_grad_body(act, src_ref, ga_ref, gn_ref, w1_ref, out_ref, *, first):
    count, width = out_ref.shape
    step = min(512, count)
    for r in range(0, count, step):
        at = slice(first + r, first + r + step)
        rows = scatter(act, src_ref, first + r, step)
        out_ref[r : r + step, :] = (
            gn_ref[at, :].astype(F32)
            + dot_nt(ga_ref[at, :].astype(BF), w1_ref[0:width, :])
            + dot_nt(rows.astype(BF), w1_ref[width : 2 * width, :])
        )


def merge_body(own, other, *rest, bit):
    n = own.shape[0]
    out_ref = rest[-1]
    side = axis_bit("fine", bit)
    out_ref[pl.ds(pl.multiple_of(side * n, PACK), n), :] = own[...]
    out_ref[pl.ds(pl.multiple_of((1 - side) * n, PACK), n), :] = other[...]


def square_body(own, by_owner, by_chip, by_both, out_ref):
    size = out_ref.shape[0] // 2
    n = own.shape[0] - PACK
    half, chip = axis_bit("coarse", 0), axis_bit("fine", 1)
    for block, i, j in ((own, half, chip), (by_owner, 1 - half, chip), (by_chip, half, 1 - chip), (by_both, 1 - half, 1 - chip)):
        out_ref[pl.ds(pl.multiple_of(j * size + i * n, PACK), n), :] = block[0:n, :]
    for block, j in ((own, chip), (by_chip, 1 - chip)):
        out_ref[pl.ds(pl.multiple_of(j * size + 2 * n, PACK), PACK), :] = block[n:, :]


def weights_body(own, other, w1_ref, gb_ref, wo_ref, up_ref, *, per, edge_scale, cell_scale):
    width = own.shape[1]
    core = lax.axis_index("fine") % 2
    outs = ((w1_ref, 0, edge_scale), (w1_ref, width, edge_scale), (wo_ref, 0, edge_scale), (up_ref, 0, cell_scale))
    size = per + PACK
    n = min(per, width)
    for index in range(lax.axis_size("fine")):
        at = slice((index // 2) * size, (index // 2 + 1) * size)
        value = jnp.where(core == index % 2, own[at, :].astype(F32), other[at, :].astype(F32))
        if index == 0:
            gb_ref[...] = (value[per : per + 1] + value[per + 1 : per + 2]) * edge_scale
        for r in range(0, per, n):
            which, row = divmod(index * per + r, width)
            out_ref, start, scale = outs[which]
            out_ref[start + row : start + row + n, :] = value[r : r + n] * scale


def table_body(*refs):
    *pool_refs, own_back, other_back, lists_ref, table = refs
    lists = lists_ref[...]
    core = lax.axis_index("fine") % 2
    side = own_back.shape[0]
    returned = jnp.concatenate([own_back[...], other_back[...]], axis=0)
    first, second = lists[:, :side], lists[:, side:]
    lists = jnp.where(core == 0, jnp.concatenate([second, first], axis=1), lists)
    step = pool_refs[0].shape[0]
    for i, pool_ref in enumerate(pool_refs):
        add = dot(hot_columns(lists, step, i * step), returned)
        table[i * step : (i + 1) * step, :] = (pool_ref[...] + add).astype(BF)


def feats_body(table, ids_ref, grad_ref, *rest, first, count):
    out_hbm, token_ref, out, sem = rest[-4:]
    token_ref[...] = jnp.zeros_like(token_ref)
    cells = table.shape[0]
    block = 256
    for t in range(0, count, block):
        at = slice(first + t, first + t + block)
        rows = dot(hot_rows(ids_ref[:, at], cells), table[...])
        out[t : t + block, :] = (grad_ref[at, :].astype(F32) + rows).astype(BF)
    copy = pltpu.make_async_copy(out, out_hbm.at[first : first + count, :], sem)
    copy.start()
    copy.wait()


def local(
    node_feats, grad_out, cluster_ids, halo_lists, edge_sources, w_edge_in, b_edge_in, w_edge_out, w_unpool,
):
    nodes, width = node_feats.shape
    cells = edge_sources.shape[0] // K
    half = cells // 2
    side = halo_lists.shape[0] // 2
    fines, coarses = lax.axis_size("fine"), lax.axis_size("coarse")
    fine_bits, coarse_bits = bits_of(fines), bits_of(coarses)
    ids = call(
        functools.partial(local_body, cells=cells), (sds((1, nodes), jnp.int32),), (cluster_ids.reshape(1, nodes),), AHEAD
    )[0]
    lists = halo_lists.reshape(1, 2 * side)
    flat = edge_sources.reshape(cells * K // LANES, LANES)
    src = call(
        source_body, (sds((K, cells), jnp.int32),), (flat,), 0, scratch=(pltpu.VMEM(flat.shape, jnp.int32),)
    )[0]
    bias = b_edge_in.reshape(1, width)

    def half_sums(x, other, after=()):
        body = functools.partial(pool_body, other=other)
        return call(body, (sds((half, width), F32),), (ids, x), nodes * cells * width, after=after)[0]

    def chip_sums(keep, recv, after=()):
        outs = (sds((half, width), F32), sds((half, width), BF))
        return call(chip_body, outs, (keep, recv), 0, after=after)

    def across(part, send, after=()):
        for bit in range(1, fine_bits):
            recv = swap(send, "fine", bit)
            last = bit == fine_bits - 1
            outs = (sds((half, width), BF),) if last else (sds((half, width), F32), sds((half, width), BF))
            part, send = (*call(across_body, outs, (part, recv), 0, after=after), None)[:2]
        return part

    recv_p = swap(half_sums(node_feats, True), "fine", 0)
    recv_g = swap(half_sums(grad_out, True), "fine", 0)
    part_p, send_p = chip_sums(half_sums(node_feats, False), recv_p)
    picked = call(pick_body, (sds((2 * side, width), BF),), (send_p, lists), 0)[0]
    sent = call(side_body, (sds((side, width), BF),), (picked, swap(picked, "fine", 0)), 0)[0]
    part_g, send_g = chip_sums(half_sums(grad_out, False, after=(send_p,)), recv_g)
    own_halo = call(
        halo_sum_body, (sds((side, width), BF),), [send_sides(sent, d) for d in range(fines // 2)], 0,
        scratch=(pltpu.VMEM((fines // 2, side, width), F32),),
    )[0]
    own_p = across(part_p, send_p, after=(own_halo, src, bias))
    other_halo = swap(own_halo, "fine", 0)
    others = [swap(x, "fine", 0) for x in (own_p[: half // 2], own_p[half // 2 :])]
    near = call(near_body, (sds((K * cells, width), BF),), (own_p, src), 0, vmem=24)[0]
    table, far, base = call(
        extend_body,
        (sds((cells, width), BF), sds((half + 2 * side, width), BF), sds((cells, width), F32)),
        (*others, own_p, own_halo, other_halo, w_edge_in, bias),
        0,
    )

    def forward(first, count, after=(), tokens=()):
        edges = count * cells
        return call(
            functools.partial(forward_body, first=first),
            (sds((cells, width), F32), sds((edges, width), F32), sds((edges, width), BF), *tokens),
            (base, far, near, src, w_edge_in),
            0,
            vmem=32,
            after=after,
        )

    *front, front_token = forward(0, EARLY, tokens=(sds((8, LANES), F32),))
    own_g = across(part_g, send_g, after=(front_token,))
    other_g = swap(own_g, "fine", 0)
    rear = forward(EARLY, K - EARLY, after=(own_g,))
    per = 4 * width // fines
    first = per // 2
    message = sds((first + PACK, width), BF)
    act, ga, gn, mine, *sends = call(
        backward_body,
        (
            sds((K * cells, width), BF), sds((cells, width), F32), sds((cells, width), BF),
            message, message, message, message,
        ),
        (own_g, other_g, table, *front, *rear, w_edge_out, w_unpool),
        2 * K * cells * width * width,
        vmem=32,
        scratch=(pltpu.VMEM((cells, width), BF), pltpu.VMEM((per, width), F32)),
    )

    back = call(
        back_body, (sds((side, width), BF),), (act, src, w_edge_in), 0,
        scratch=(pltpu.VMEM((2 * side, width), F32),),
    )[0]
    own_back = send_sides(back)
    cell_grads = [
        call(
            functools.partial(cell_grad_body, first=at),
            (sds((half, width), F32),),
            (act, src, ga, gn, w_edge_in),
            0,
        )[0]
        for at in (0, half)
    ]
    recvs = swap_owners(sends[2]), swap(sends[1], "coarse", 1), swap(sends[0], "coarse", 0)
    outs = (sds((first, width), F32), message, sds((8, width), F32))
    keep, send, bias_sum = call(
        square_sum_body, outs, (mine, *recvs), 0, after=(own_back, cell_grads[1]),
        scratch=(pltpu.VMEM((4, first + PACK, width), F32),),
    )
    other_back = swap(own_back, "fine", 0)
    table = call(
        table_body, (sds((cells, width), BF),), (*cell_grads, own_back, other_back, lists), 0
    )[0]

    def feats(first, count, after=(), into=None):
        return call(
            functools.partial(feats_body, first=first, count=count),
            (sds((nodes, width), BF), sds((8, LANES), F32)),
            (table, ids, grad_out),
            2 * count * cells * width,
            vmem=24,
            scratch=(pltpu.VMEM((count, width), BF), pltpu.SemaphoreType.DMA(())),
            after=after,
            into=into,
            far=1,
        )

    for bit in range(2, coarse_bits - 1):
        recv = swap(send, "coarse", bit)
        keep, send, bias_sum = call(stage_body, outs, (keep, recv, bias_sum), 0)
    recv = swap(send, "coarse", coarse_bits - 1)
    part = call(end_body, (message,), (keep, recv, bias_sum), 0, after=(other_back, cell_grads[0]))[0]
    front_rows = nodes // 8 * 5
    grad_feats, feats_token = feats(0, front_rows)
    near = [swap(part, "coarse", 0), swap(part, "fine", 1), swap_both(part)]
    part = call(
        square_body, (sds((2 * (per + PACK), width), BF),), (part, *near), 0, after=(feats_token,)
    )[0]
    for bit in range(2, fine_bits):
        other = swap(part, "fine", bit)
        body = functools.partial(merge_body, bit=bit)
        part = call(body, (sds((2 * part.shape[0], width), BF),), (part, other), 0)[0]
    other = swap(part, "fine", 0)
    grad_feats, feats_token = feats(front_rows, nodes - front_rows, after=(part,), into=grad_feats)
    total_cells = cells * coarses
    scales = dict(edge_scale=float(total_cells * K) ** -0.5, cell_scale=float(total_cells) ** -0.5)
    grad_w1, grad_b, grad_wo, grad_up = call(
        functools.partial(weights_body, per=per, **scales),
        (
            sds((2 * width, width), F32), sds((1, width), F32), sds((width, width), F32), sds((width, width), F32),
        ),
        (part, other),
        0,
        after=(feats_token,),
    )
    return grad_feats, grad_w1, grad_b.reshape(width), grad_wo, grad_up


def solution(mesh):
    both = ("coarse", "fine")
    return jax.shard_map(
        local,
        mesh=mesh,
        in_specs=(P(both, None), P(both, None), P(both), P("coarse"), P("coarse"), P(), P(), P(), P()),
        out_specs=(P(both, None), P(), P(), P(), P()),
        check_vma=False,
    )
```

```python
import functools

import jax
import jax.numpy as jnp
from jax import lax
from jax.experimental import pallas as pl
from jax.experimental.pallas import tpu as pltpu
from jax.sharding import PartitionSpec as P

K = 4
EARLY = 3
BF = jnp.bfloat16
F32 = jnp.float32
LANES = 128
PACK = 16
MIB = 1 << 20
AHEAD = 10**9


def dot(a, b):
    return jnp.dot(a, b, preferred_element_type=F32)


def dot_nt(a, b):
    return lax.dot_general(a, b, (((1,), (1,)), ((), ())), preferred_element_type=F32)


def dot_tn(a, b):
    return lax.dot_general(a, b, (((0,), (0,)), ((), ())), preferred_element_type=F32)


def bits_of(count):
    assert count > 1 and count & (count - 1) == 0
    return count.bit_length() - 1


def swap(x, axis, bit):
    count = lax.axis_size(axis)
    return lax.ppermute(x, axis, [(i, i ^ (1 << bit)) for i in range(count)])


def swap_owners(x):
    return lax.ppermute(x, "coarse", [(i, i ^ 3) for i in range(lax.axis_size("coarse"))])


def swap_both(x):
    owners, fines = lax.axis_size("coarse"), lax.axis_size("fine")
    pairs = [(g * fines + f, (g ^ 1) * fines + (f ^ 2)) for g in range(owners) for f in range(fines)]
    return lax.ppermute(x, ("coarse", "fine"), pairs)


def send_sides(x, flip=0):
    owners, fines = lax.axis_size("coarse"), lax.axis_size("fine")
    pairs = [
        (g * fines + f, (g + 1 - 2 * (f % 2)) % owners * fines + (f ^ (2 * flip)))
        for g in range(owners)
        for f in range(fines)
    ]
    return lax.ppermute(x, ("coarse", "fine"), pairs)


def call(body, outs, args, flops, vmem=16, scratch=(), after=(), into=None, far=0):
    moved = sum(a.size * a.dtype.itemsize for a in (*args, *outs)) if flops else 0
    count = len(args)
    unseen = (*after, into) if into is not None else after
    waited = len(unseen)

    def kernel(*refs):
        body(*refs[:count], *refs[count + waited :])

    anywhere = pl.BlockSpec(memory_space=pl.ANY)
    in_vmem = pl.BlockSpec(memory_space=pltpu.VMEM)
    places = tuple([anywhere] * far + [in_vmem] * (len(outs) - far))
    return pl.pallas_call(
        kernel,
        out_shape=outs,
        in_specs=[in_vmem] * count + [anywhere] * waited,
        out_specs=places,
        scratch_shapes=scratch,
        input_output_aliases={} if into is None else {count + waited - 1: 0},
        compiler_params=pltpu.CompilerParams(vmem_limit_bytes=vmem * MIB),
        cost_estimate=pl.CostEstimate(flops=int(flops), bytes_accessed=int(moved), transcendentals=0),
    )(*args, *unseen)


def sds(shape, dtype):
    return jax.ShapeDtypeStruct(shape, dtype)


def column(row):
    blocks = [
        jnp.broadcast_to(row[:, i : i + LANES], (LANES, LANES)).T
        for i in range(0, row.shape[1], LANES)
    ]
    return blocks[0] if len(blocks) == 1 else jnp.concatenate(blocks, axis=0)


def hot_rows(row, width):
    ids = column(row)
    ids = jnp.concatenate([ids] * (width // LANES), axis=1)
    lane = lax.broadcasted_iota(jnp.int32, ids.shape, 1)
    return jnp.where(lane == ids, 1.0, 0.0).astype(BF)


def hot_columns(row, height, start=0):
    shape = (height, row.shape[1])
    at = lax.broadcasted_iota(jnp.int32, shape, 0)
    return jnp.where(at == row - start, 1.0, 0.0).astype(BF)


def local_body(ids_ref, out_ref, *, cells):
    out_ref[...] = lax.rem(ids_ref[...], cells)


def source_body(src_ref, out_ref, mixed):
    per = LANES // K
    src = src_ref[...]
    at = lax.broadcasted_iota(jnp.int32, (LANES, LANES), 0)
    to = lax.broadcasted_iota(jnp.int32, (LANES, LANES), 1)
    order = jnp.where(to == (at % K) * per + at // K, 1.0, 0.0).astype(BF)
    high = lax.shift_right_logical(src, 6)
    low = (src - 64 * high).astype(F32).astype(BF)
    high = high.astype(F32).astype(BF)
    mixed[...] = (64.0 * dot(high, order) + dot(low, order)).astype(jnp.int32)
    count = mixed.shape[0] // K
    lane = lax.broadcasted_iota(jnp.int32, (count, LANES), 1) // per
    quarters = [mixed[pl.ds(j, count, stride=K), :] for j in range(K)]
    for k in range(K):
        rows = jnp.zeros((count, LANES), jnp.int32)
        for j in range(K):
            turned = quarters[j] if j == k else pltpu.roll(quarters[j], (j - k) % K * per, 1)
            rows = jnp.where(lane == j, turned, rows)
        for q in range(count):
            out_ref[k : k + 1, q * LANES : (q + 1) * LANES] = rows[q : q + 1, :]


def pool_body(ids_ref, x_ref, out_ref, *, other):
    half = out_ref.shape[0]
    core = lax.axis_index("fine") % 2
    first = ((1 - core) if other else core) * half
    ids = ids_ref[...] - first
    step = min(256, half)
    for t in range(0, half, step):
        out_ref[t : t + step, :] = dot(hot_columns(ids, step, t), x_ref[...])


def pick_body(part_ref, lists_ref, out_ref):
    half = part_ref.shape[0]
    core = lax.axis_index("fine") % 2
    out_ref[...] = dot(hot_rows(lists_ref[...] - core * half, half), part_ref[...]).astype(BF)


def side_body(own, other, out_ref):
    side = out_ref.shape[0]
    core = lax.axis_index("fine") % 2
    at = pl.ds(pl.multiple_of(core * side, side), side)
    out_ref[...] = own[at, :] + other[at, :]


def halo_sum_body(*refs):
    *parts, out_ref, slots = refs
    chip = lax.axis_index("fine") // 2
    for offset, part in enumerate(parts):
        slots[chip ^ offset] = part[...].astype(F32)
    total = slots[0]
    for i in range(1, len(parts)):
        total = total + slots[i]
    out_ref[...] = total.astype(BF)


def chip_body(keep, recv, part_ref, send_ref):
    total = keep[...] + recv[...]
    part_ref[...] = total
    send_ref[...] = total.astype(BF)


def across_body(part, recv, *out_refs):
    total = part[...] + recv[...].astype(F32)
    for ref in out_refs:
        ref[...] = total.astype(ref.dtype)


def core_order(half):
    core = lax.axis_index("fine") % 2
    at_own = pl.ds(pl.multiple_of(core * half, half), half)
    at_other = pl.ds(pl.multiple_of((1 - core) * half, half), half)
    return at_own, at_other


def near_body(own_p, src_ref, near):
    half = own_p.shape[0]
    cells = 2 * half
    core = lax.axis_index("fine") % 2
    block = 512
    for k in range(K):
        for t in range(0, cells, block):
            hot = hot_rows(src_ref[k : k + 1, t : t + block] - core * half, half)
            near[k * cells + t : k * cells + t + block, :] = dot(hot, own_p[...]).astype(BF)


def extend_body(*refs):
    *others, own_p, own_halo, other_halo, w1_ref, b_ref, table, far, base = refs
    half, width = own_p.shape
    side = own_halo.shape[0]
    core = lax.axis_index("fine") % 2
    n = half // len(others)
    for i, other in enumerate(others):
        far[i * n : (i + 1) * n, :] = other[...]
    far[pl.ds(pl.multiple_of(half + core * side, PACK), side), :] = own_halo[...]
    far[pl.ds(pl.multiple_of(half + (1 - core) * side, PACK), side), :] = other_halo[...]
    at_own, at_other = core_order(half)
    table[at_own, :] = own_p[...]
    table[at_other, :] = far[0:half, :]
    base[...] = dot(table[...], w1_ref[0:width, :]) + b_ref[...].astype(F32)


def forward_body(base, far, near, src_ref, w1_ref, hid, slope, feats, *tokens, first):
    cells, width = base.shape
    half = cells // 2
    core = lax.axis_index("fine") % 2
    for ref in tokens:
        ref[...] = jnp.zeros_like(ref)
    block = 512
    for i in range(slope.shape[0] // cells):
        for t in range(0, cells, block):
            src = src_ref[first + i : first + i + 1, t : t + block]
            mine = jnp.logical_and(src >= core * half, src < (core + 1) * half)
            place = jnp.where(src >= cells, src - half, src - (1 - core) * half)
            picked = dot(hot_rows(jnp.where(mine, -1, place), far.shape[0]), far[...])
            here = slice((first + i) * cells + t, (first + i) * cells + t + block)
            feats[i * cells + t : i * cells + t + block, :] = (picked + near[here, :].astype(F32)).astype(BF)
        at = slice(i * cells, (i + 1) * cells)
        pre = base[...] + dot(feats[at, :], w1_ref[width : 2 * width, :])
        sig = 0.5 * jnp.tanh(0.5 * pre) + 0.5
        hidden = pre * sig
        hid[...] = hidden if i == 0 else hid[...] + hidden
        slope[at, :] = sig + hidden * (1.0 - sig)


def split(x):
    high = x.astype(BF)
    return high, (x - high.astype(F32)).astype(BF)


def bias_rows(bias):
    high, low = (part.astype(F32) for part in split(bias))
    at = lax.broadcasted_iota(jnp.int32, (PACK, bias.shape[1]), 0)
    return jnp.where(at == 0, high, jnp.where(at == 1, low, 0.0)).astype(BF), high + low


def axis_bit(axis, bit):
    return lax.rem(lax.axis_index(axis) // (1 << bit), 2)


def emit(total, bias, keep_ref, send_ref, bias_ref):
    n = keep_ref.shape[0]
    sent = total.astype(BF)
    keep_ref[...] = sent.astype(F32)
    rows, bias = bias_rows(bias)
    send_ref[0:n, :] = sent
    send_ref[n : n + PACK, :] = rows
    bias_ref[...] = jnp.broadcast_to(bias, bias_ref.shape)


def backward_body(
    own_g, other_g, table, hid_1, slope_1, feats_1, hid_2, slope_2, feats_2, wo_ref, wu_ref,
    act, ga_ref, gn_ref, mine_ref, by_one, by_two, by_both,
    gsum, total,
):
    half, width = own_g.shape
    cells = 2 * half
    fine = lax.axis_index("fine")
    at_own, at_other = core_order(half)
    gsum[at_own, :] = own_g[...]
    gsum[at_other, :] = other_g[...]
    gn = dot_nt(gsum[...], wu_ref[...]).astype(BF)
    gn_ref[...] = gn
    grad = dot_nt(gn, wo_ref[...])
    ga = jnp.zeros((cells, width), F32)
    for k in range(K):
        at = slice(k * cells, (k + 1) * cells)
        slope, here = (slope_1, k) if k < EARLY else (slope_2, k - EARLY)
        part = (grad * slope[here * cells : (here + 1) * cells, :]).astype(BF)
        act[at, :] = part
        ga = ga + part.astype(F32)
    ga_ref[...] = ga

    fines = lax.axis_size("fine")
    per = 4 * width // fines
    n = min(per, width)
    for index in range(fines):

        @pl.when(fine == index)
        def _():
            for r in range(0, per, n):
                which, first = divmod(index * per + r, width)
                cols = slice(first, first + n)
                if which == 0:
                    high, low = split(ga_ref[...])
                    left = table[:, cols]
                    out = dot_tn(left, high) + dot_tn(left, low)
                elif which == 1:
                    n_1 = feats_1.shape[0]
                    out = dot_tn(feats_1[:, cols], act[0:n_1, :]) + dot_tn(feats_2[:, cols], act[n_1:, :])
                elif which == 2:
                    high, low = split(hid_1[:, cols] + hid_2[:, cols])
                    out = dot_tn(high, gn_ref[...]) + dot_tn(low, gn_ref[...])
                else:
                    high, low = split(hid_1[...] + hid_2[...])
                    agg = dot(high, wo_ref[:, cols]) + dot(low, wo_ref[:, cols])
                    new = (table[:, cols].astype(F32) + agg).astype(BF)
                    out = dot_tn(new, gsum[...])
                total[r : r + n, :] = out

    rows = bias_rows(jnp.sum(ga_ref[...], axis=0, keepdims=True))[0]
    half = axis_bit("coarse", 0)
    n = per // 2
    for ref, at in ((mine_ref, half), (by_one, 1 - half), (by_two, half), (by_both, 1 - half)):
        ref[0:n, :] = total[pl.ds(pl.multiple_of(at * n, n), n), :].astype(BF)
        ref[n : n + PACK, :] = rows


def square_sum_body(own, by_both, by_two, by_one, keep_ref, send_ref, bias_ref, slots):
    n = keep_ref.shape[0]
    me = lax.rem(lax.axis_index("coarse"), 4)
    for i, ref in enumerate((own, by_one, by_two, by_both)):
        slots[me ^ i] = ref[...].astype(F32)
    total = slots[0] + slots[1] + slots[2] + slots[3]
    emit(total[0:n], total[n : n + 1] + total[n + 1 : n + 2], keep_ref, send_ref, bias_ref)


def received_bias(recv, n):
    return recv[n : n + 1, :].astype(F32) + recv[n + 1 : n + 2, :].astype(F32)


def stage_body(keep_in, recv, bias_in, keep_ref, send_ref, bias_ref):
    n = keep_in.shape[0]
    total = keep_in[...] + recv[0:n, :].astype(F32)
    emit(total, bias_in[0:1, :] + received_bias(recv, n), keep_ref, send_ref, bias_ref)


def end_body(keep_in, recv, bias_in, out_ref):
    n = keep_in.shape[0]
    out_ref[0:n, :] = (keep_in[...] + recv[0:n, :].astype(F32)).astype(BF)
    out_ref[n : n + PACK, :] = bias_rows(bias_in[0:1, :] + received_bias(recv, n))[0]


def scatter(act, src_ref, first, count):
    cells = src_ref.shape[1]
    out = jnp.zeros((count, act.shape[1]), F32)
    for k in range(K):
        hot = hot_columns(src_ref[k : k + 1, :], count, first)
        out += dot(hot, act[k * cells : (k + 1) * cells, :])
    return out


def back_body(act, src_ref, w1_ref, out_ref):
    side, width = out_ref.shape
    core = lax.axis_index("fine") % 2
    rows = scatter(act, src_ref, src_ref.shape[1] + (1 - core) * side, side)
    out_ref[...] = dot_nt(rows.astype(BF), w1_ref[width : 2 * width, :]).astype(BF)


def cell_grad_body(act, src_ref, ga_ref, gn_ref, w1_ref, out_ref, *, first):
    count, width = out_ref.shape
    step = min(512, count)
    for r in range(0, count, step):
        at = slice(first + r, first + r + step)
        rows = scatter(act, src_ref, first + r, step)
        out_ref[r : r + step, :] = (
            gn_ref[at, :].astype(F32)
            + dot_nt(ga_ref[at, :].astype(BF), w1_ref[0:width, :])
            + dot_nt(rows.astype(BF), w1_ref[width : 2 * width, :])
        )


def merge_body(own, other, *rest, bit):
    n = own.shape[0]
    out_ref = rest[-1]
    side = axis_bit("fine", bit)
    out_ref[pl.ds(pl.multiple_of(side * n, PACK), n), :] = own[...]
    out_ref[pl.ds(pl.multiple_of((1 - side) * n, PACK), n), :] = other[...]


def square_body(own, by_owner, by_chip, by_both, out_ref):
    size = out_ref.shape[0] // 2
    n = own.shape[0] - PACK
    half, chip = axis_bit("coarse", 0), axis_bit("fine", 1)
    for block, i, j in ((own, half, chip), (by_owner, 1 - half, chip), (by_chip, half, 1 - chip), (by_both, 1 - half, 1 - chip)):
        out_ref[pl.ds(pl.multiple_of(j * size + i * n, PACK), n), :] = block[0:n, :]
    for block, j in ((own, chip), (by_chip, 1 - chip)):
        out_ref[pl.ds(pl.multiple_of(j * size + 2 * n, PACK), PACK), :] = block[n:, :]


def weights_body(own, other, w1_ref, gb_ref, wo_ref, up_ref, *, per, edge_scale, cell_scale):
    width = own.shape[1]
    core = lax.axis_index("fine") % 2
    outs = ((w1_ref, 0, edge_scale), (w1_ref, width, edge_scale), (wo_ref, 0, edge_scale), (up_ref, 0, cell_scale))
    size = per + PACK
    n = min(per, width)
    for index in range(lax.axis_size("fine")):
        at = slice((index // 2) * size, (index // 2 + 1) * size)
        value = jnp.where(core == index % 2, own[at, :].astype(F32), other[at, :].astype(F32))
        if index == 0:
            gb_ref[...] = (value[per : per + 1] + value[per + 1 : per + 2]) * edge_scale
        for r in range(0, per, n):
            which, row = divmod(index * per + r, width)
            out_ref, start, scale = outs[which]
            out_ref[start + row : start + row + n, :] = value[r : r + n] * scale


def table_body(*refs):
    *pool_refs, own_back, other_back, lists_ref, table = refs
    lists = lists_ref[...]
    core = lax.axis_index("fine") % 2
    side = own_back.shape[0]
    returned = jnp.concatenate([own_back[...], other_back[...]], axis=0)
    first, second = lists[:, :side], lists[:, side:]
    lists = jnp.where(core == 0, jnp.concatenate([second, first], axis=1), lists)
    step = pool_refs[0].shape[0]
    for i, pool_ref in enumerate(pool_refs):
        add = dot(hot_columns(lists, step, i * step), returned)
        table[i * step : (i + 1) * step, :] = (pool_ref[...] + add).astype(BF)


def feats_body(table, ids_ref, grad_ref, out_hbm, token_ref, out, sems):
    token_ref[...] = jnp.zeros_like(token_ref)
    cells = table.shape[0]
    block = out.shape[0] // sems.shape[0]
    stores = []
    for i in range(sems.shape[0]):
        at = slice(i * block, (i + 1) * block)
        rows = dot(hot_rows(ids_ref[:, at], cells), table[...])
        out[at, :] = (grad_ref[at, :].astype(F32) + rows).astype(BF)
        stores.append(pltpu.make_async_copy(out.at[at, :], out_hbm.at[at, :], sems.at[i]))
        stores[-1].start()
    for store in stores:
        store.wait()


def local(
    node_feats, grad_out, cluster_ids, halo_lists, edge_sources, w_edge_in, b_edge_in, w_edge_out, w_unpool,
):
    nodes, width = node_feats.shape
    cells = edge_sources.shape[0] // K
    half = cells // 2
    side = halo_lists.shape[0] // 2
    fines, coarses = lax.axis_size("fine"), lax.axis_size("coarse")
    fine_bits, coarse_bits = bits_of(fines), bits_of(coarses)
    ids = call(
        functools.partial(local_body, cells=cells), (sds((1, nodes), jnp.int32),), (cluster_ids.reshape(1, nodes),), AHEAD
    )[0]
    lists = halo_lists.reshape(1, 2 * side)
    flat = edge_sources.reshape(cells * K // LANES, LANES)
    src = call(
        source_body, (sds((K, cells), jnp.int32),), (flat,), 0, scratch=(pltpu.VMEM(flat.shape, jnp.int32),)
    )[0]
    bias = b_edge_in.reshape(1, width)

    def half_sums(x, other, after=()):
        body = functools.partial(pool_body, other=other)
        return call(body, (sds((half, width), F32),), (ids, x), nodes * cells * width, after=after)[0]

    def chip_sums(keep, recv, after=()):
        outs = (sds((half, width), F32), sds((half, width), BF))
        return call(chip_body, outs, (keep, recv), 0, after=after)

    def across(part, send, after=()):
        for bit in range(1, fine_bits):
            recv = swap(send, "fine", bit)
            last = bit == fine_bits - 1
            outs = (sds((half, width), BF),) if last else (sds((half, width), F32), sds((half, width), BF))
            part, send = (*call(across_body, outs, (part, recv), 0, after=after), None)[:2]
        return part

    recv_p = swap(half_sums(node_feats, True), "fine", 0)
    recv_g = swap(half_sums(grad_out, True), "fine", 0)
    part_p, send_p = chip_sums(half_sums(node_feats, False), recv_p)
    picked = call(pick_body, (sds((2 * side, width), BF),), (send_p, lists), 0)[0]
    sent = call(side_body, (sds((side, width), BF),), (picked, swap(picked, "fine", 0)), 0)[0]
    part_g, send_g = chip_sums(half_sums(grad_out, False, after=(send_p,)), recv_g)
    own_halo = call(
        halo_sum_body, (sds((side, width), BF),), [send_sides(sent, d) for d in range(fines // 2)], 0,
        scratch=(pltpu.VMEM((fines // 2, side, width), F32),),
    )[0]
    own_p = across(part_p, send_p, after=(own_halo, src, bias))
    other_halo = swap(own_halo, "fine", 0)
    others = [swap(x, "fine", 0) for x in (own_p[: half // 2], own_p[half // 2 :])]
    near = call(near_body, (sds((K * cells, width), BF),), (own_p, src), 0, vmem=24)[0]
    table, far, base = call(
        extend_body,
        (sds((cells, width), BF), sds((half + 2 * side, width), BF), sds((cells, width), F32)),
        (*others, own_p, own_halo, other_halo, w_edge_in, bias),
        0,
    )

    def forward(first, count, after=(), tokens=()):
        edges = count * cells
        return call(
            functools.partial(forward_body, first=first),
            (sds((cells, width), F32), sds((edges, width), F32), sds((edges, width), BF), *tokens),
            (base, far, near, src, w_edge_in),
            0,
            vmem=32,
            after=after,
        )

    *front, front_token = forward(0, EARLY, tokens=(sds((8, LANES), F32),))
    own_g = across(part_g, send_g, after=(front_token,))
    other_g = swap(own_g, "fine", 0)
    rear = forward(EARLY, K - EARLY, after=(own_g,))
    per = 4 * width // fines
    first = per // 2
    message = sds((first + PACK, width), BF)
    act, ga, gn, mine, *sends = call(
        backward_body,
        (
            sds((K * cells, width), BF), sds((cells, width), F32), sds((cells, width), BF),
            message, message, message, message,
        ),
        (own_g, other_g, table, *front, *rear, w_edge_out, w_unpool),
        2 * K * cells * width * width,
        vmem=32,
        scratch=(pltpu.VMEM((cells, width), BF), pltpu.VMEM((per, width), F32)),
    )

    back = call(
        back_body, (sds((side, width), BF),), (act, src, w_edge_in), 0
    )[0]
    own_back = send_sides(back)
    cell_grads = [
        call(
            functools.partial(cell_grad_body, first=at),
            (sds((half, width), F32),),
            (act, src, ga, gn, w_edge_in),
            0,
        )[0]
        for at in (0, half)
    ]
    recvs = swap_owners(sends[2]), swap(sends[1], "coarse", 1), swap(sends[0], "coarse", 0)
    outs = (sds((first, width), F32), message, sds((8, width), F32))
    keep, send, bias_sum = call(
        square_sum_body, outs, (mine, *recvs), 0, after=(own_back, cell_grads[1]),
        scratch=(pltpu.VMEM((4, first + PACK, width), F32),),
    )
    other_back = swap(own_back, "fine", 0)
    table = call(
        table_body, (sds((cells, width), BF),), (*cell_grads, own_back, other_back, lists), 0
    )[0]

    for bit in range(2, coarse_bits - 1):
        recv = swap(send, "coarse", bit)
        keep, send, bias_sum = call(stage_body, outs, (keep, recv, bias_sum), 0)
    recv = swap(send, "coarse", coarse_bits - 1)
    part = call(end_body, (message,), (keep, recv, bias_sum), 0, after=(other_back, cell_grads[0]))[0]
    grad_feats, feats_token = call(
        feats_body, (sds((nodes, width), BF), sds((8, LANES), F32)), (table, ids, grad_out), 2 * nodes * cells * width,
        vmem=24, scratch=(pltpu.VMEM((nodes, width), BF), pltpu.SemaphoreType.DMA((nodes // 256,))), far=1,
    )
    near = [swap(part, "coarse", 0), swap(part, "fine", 1), swap_both(part)]
    part = call(
        square_body, (sds((2 * (per + PACK), width), BF),), (part, *near), 0, after=(feats_token,)
    )[0]
    for bit in range(2, fine_bits):
        other = swap(part, "fine", bit)
        body = functools.partial(merge_body, bit=bit)
        part = call(body, (sds((2 * part.shape[0], width), BF),), (part, other), 0)[0]
    other = swap(part, "fine", 0)
    total_cells = cells * coarses
    scales = dict(edge_scale=float(total_cells * K) ** -0.5, cell_scale=float(total_cells) ** -0.5)
    grad_w1, grad_b, grad_wo, grad_up = call(
        functools.partial(weights_body, per=per, **scales),
        (
            sds((2 * width, width), F32), sds((1, width), F32), sds((width, width), F32), sds((width, width), F32),
        ),
        (part, other),
        0,
    )
    return grad_feats, grad_w1, grad_b.reshape(width), grad_wo, grad_up


def solution(mesh):
    both = ("coarse", "fine")
    return jax.shard_map(
        local,
        mesh=mesh,
        in_specs=(P(both, None), P(both, None), P(both), P("coarse"), P("coarse"), P(), P(), P(), P()),
        out_specs=(P(both, None), P(), P(), P(), P()),
        check_vma=False,
    )
```

```python
import functools

import jax
import jax.numpy as jnp
from jax import lax
from jax.experimental import pallas as pl
from jax.experimental.pallas import tpu as pltpu
from jax.sharding import PartitionSpec as P

K = 4
EARLY = 3
BF = jnp.bfloat16
F32 = jnp.float32
LANES = 128
PACK = 16
MIB = 1 << 20
AHEAD = 10**9


def dot(a, b):
    return jnp.dot(a, b, preferred_element_type=F32)


def dot_nt(a, b):
    return lax.dot_general(a, b, (((1,), (1,)), ((), ())), preferred_element_type=F32)


def dot_tn(a, b):
    return lax.dot_general(a, b, (((0,), (0,)), ((), ())), preferred_element_type=F32)


def bits_of(count):
    assert count > 1 and count & (count - 1) == 0
    return count.bit_length() - 1


def swap(x, axis, bit):
    count = lax.axis_size(axis)
    return lax.ppermute(x, axis, [(i, i ^ (1 << bit)) for i in range(count)])


def swap_owners(x):
    return lax.ppermute(x, "coarse", [(i, i ^ 3) for i in range(lax.axis_size("coarse"))])


def swap_both(x):
    owners, fines = lax.axis_size("coarse"), lax.axis_size("fine")
    pairs = [(g * fines + f, (g ^ 1) * fines + (f ^ 2)) for g in range(owners) for f in range(fines)]
    return lax.ppermute(x, ("coarse", "fine"), pairs)


def send_sides(x, flip=0):
    owners, fines = lax.axis_size("coarse"), lax.axis_size("fine")
    pairs = [
        (g * fines + f, (g + 1 - 2 * (f % 2)) % owners * fines + (f ^ (2 * flip)))
        for g in range(owners)
        for f in range(fines)
    ]
    return lax.ppermute(x, ("coarse", "fine"), pairs)


def call(body, outs, args, flops, vmem=16, scratch=(), after=(), into=None, far=0):
    moved = sum(a.size * a.dtype.itemsize for a in (*args, *outs)) if flops else 0
    count = len(args)
    unseen = (*after, into) if into is not None else after
    waited = len(unseen)

    def kernel(*refs):
        body(*refs[:count], *refs[count + waited :])

    anywhere = pl.BlockSpec(memory_space=pl.ANY)
    in_vmem = pl.BlockSpec(memory_space=pltpu.VMEM)
    places = tuple([anywhere] * far + [in_vmem] * (len(outs) - far))
    return pl.pallas_call(
        kernel,
        out_shape=outs,
        in_specs=[in_vmem] * count + [anywhere] * waited,
        out_specs=places,
        scratch_shapes=scratch,
        input_output_aliases={} if into is None else {count + waited - 1: 0},
        compiler_params=pltpu.CompilerParams(vmem_limit_bytes=vmem * MIB),
        cost_estimate=pl.CostEstimate(flops=int(flops), bytes_accessed=int(moved), transcendentals=0),
    )(*args, *unseen)


def sds(shape, dtype):
    return jax.ShapeDtypeStruct(shape, dtype)


def column(row):
    blocks = [
        jnp.broadcast_to(row[:, i : i + LANES], (LANES, LANES)).T
        for i in range(0, row.shape[1], LANES)
    ]
    return blocks[0] if len(blocks) == 1 else jnp.concatenate(blocks, axis=0)


def hot_rows(row, width):
    ids = column(row)
    ids = jnp.concatenate([ids] * (width // LANES), axis=1)
    lane = lax.broadcasted_iota(jnp.int32, ids.shape, 1)
    return jnp.where(lane == ids, 1.0, 0.0).astype(BF)


def hot_columns(row, height, start=0):
    shape = (height, row.shape[1])
    at = lax.broadcasted_iota(jnp.int32, shape, 0)
    return jnp.where(at == row - start, 1.0, 0.0).astype(BF)


def local_body(ids_ref, out_ref, *, cells):
    out_ref[...] = lax.rem(ids_ref[...], cells)


def source_body(src_ref, out_ref, mixed):
    per = LANES // K
    src = src_ref[...]
    at = lax.broadcasted_iota(jnp.int32, (LANES, LANES), 0)
    to = lax.broadcasted_iota(jnp.int32, (LANES, LANES), 1)
    order = jnp.where(to == (at % K) * per + at // K, 1.0, 0.0).astype(BF)
    high = lax.shift_right_logical(src, 6)
    low = (src - 64 * high).astype(F32).astype(BF)
    high = high.astype(F32).astype(BF)
    mixed[...] = (64.0 * dot(high, order) + dot(low, order)).astype(jnp.int32)
    count = mixed.shape[0] // K
    lane = lax.broadcasted_iota(jnp.int32, (count, LANES), 1) // per
    quarters = [mixed[pl.ds(j, count, stride=K), :] for j in range(K)]
    for k in range(K):
        rows = jnp.zeros((count, LANES), jnp.int32)
        for j in range(K):
            turned = quarters[j] if j == k else pltpu.roll(quarters[j], (j - k) % K * per, 1)
            rows = jnp.where(lane == j, turned, rows)
        for q in range(count):
            out_ref[k : k + 1, q * LANES : (q + 1) * LANES] = rows[q : q + 1, :]


def pool_body(ids_ref, x_ref, out_ref, *, other):
    half = out_ref.shape[0]
    core = lax.axis_index("fine") % 2
    first = ((1 - core) if other else core) * half
    ids = ids_ref[...] - first
    step = min(256, half)
    for t in range(0, half, step):
        out_ref[t : t + step, :] = dot(hot_columns(ids, step, t), x_ref[...])


def pick_body(part_ref, lists_ref, out_ref):
    half = part_ref.shape[0]
    core = lax.axis_index("fine") % 2
    out_ref[...] = dot(hot_rows(lists_ref[...] - core * half, half), part_ref[...]).astype(BF)


def side_body(own, other, out_ref):
    side = out_ref.shape[0]
    core = lax.axis_index("fine") % 2
    at = pl.ds(pl.multiple_of(core * side, side), side)
    out_ref[...] = own[at, :] + other[at, :]


def halo_sum_body(*refs):
    *parts, out_ref, slots = refs
    chip = lax.axis_index("fine") // 2
    for offset, part in enumerate(parts):
        slots[chip ^ offset] = part[...].astype(F32)
    total = slots[0]
    for i in range(1, len(parts)):
        total = total + slots[i]
    out_ref[...] = total.astype(BF)


def chip_body(keep, recv, part_ref, send_ref):
    total = keep[...] + recv[...]
    part_ref[...] = total
    send_ref[...] = total.astype(BF)


def across_body(part, recv, *out_refs):
    total = part[...] + recv[...].astype(F32)
    for ref in out_refs:
        ref[...] = total.astype(ref.dtype)


def core_order(half):
    core = lax.axis_index("fine") % 2
    at_own = pl.ds(pl.multiple_of(core * half, half), half)
    at_other = pl.ds(pl.multiple_of((1 - core) * half, half), half)
    return at_own, at_other


def near_body(own_p, src_ref, near):
    half = own_p.shape[0]
    cells = 2 * half
    core = lax.axis_index("fine") % 2
    block = 512
    for k in range(K):
        for t in range(0, cells, block):
            hot = hot_rows(src_ref[k : k + 1, t : t + block] - core * half, half)
            near[k * cells + t : k * cells + t + block, :] = dot(hot, own_p[...]).astype(BF)


def extend_body(*refs):
    *others, own_p, own_halo, other_halo, w1_ref, b_ref, table, far, base = refs
    half, width = own_p.shape
    side = own_halo.shape[0]
    core = lax.axis_index("fine") % 2
    n = half // len(others)
    for i, other in enumerate(others):
        far[i * n : (i + 1) * n, :] = other[...]
    far[pl.ds(pl.multiple_of(half + core * side, PACK), side), :] = own_halo[...]
    far[pl.ds(pl.multiple_of(half + (1 - core) * side, PACK), side), :] = other_halo[...]
    at_own, at_other = core_order(half)
    table[at_own, :] = own_p[...]
    table[at_other, :] = far[0:half, :]
    base[...] = dot(table[...], w1_ref[0:width, :]) + b_ref[...].astype(F32)


def forward_body(base, far, near, src_ref, w1_ref, hid, slope, feats, *tokens, first):
    cells, width = base.shape
    half = cells // 2
    core = lax.axis_index("fine") % 2
    for ref in tokens:
        ref[...] = jnp.zeros_like(ref)
    block = 512
    for i in range(slope.shape[0] // cells):
        for t in range(0, cells, block):
            src = src_ref[first + i : first + i + 1, t : t + block]
            mine = jnp.logical_and(src >= core * half, src < (core + 1) * half)
            place = jnp.where(src >= cells, src - half, src - (1 - core) * half)
            picked = dot(hot_rows(jnp.where(mine, -1, place), far.shape[0]), far[...])
            here = slice((first + i) * cells + t, (first + i) * cells + t + block)
            feats[i * cells + t : i * cells + t + block, :] = (picked + near[here, :].astype(F32)).astype(BF)
        at = slice(i * cells, (i + 1) * cells)
        pre = base[...] + dot(feats[at, :], w1_ref[width : 2 * width, :])
        sig = 0.5 * jnp.tanh(0.5 * pre) + 0.5
        hidden = pre * sig
        hid[...] = hidden if i == 0 else hid[...] + hidden
        slope[at, :] = sig + hidden * (1.0 - sig)


def split(x):
    high = x.astype(BF)
    return high, (x - high.astype(F32)).astype(BF)


def bias_rows(bias):
    high, low = (part.astype(F32) for part in split(bias))
    at = lax.broadcasted_iota(jnp.int32, (PACK, bias.shape[1]), 0)
    return jnp.where(at == 0, high, jnp.where(at == 1, low, 0.0)).astype(BF), high + low


def axis_bit(axis, bit):
    return lax.rem(lax.axis_index(axis) // (1 << bit), 2)


def emit(total, bias, keep_ref, send_ref, bias_ref):
    n = keep_ref.shape[0]
    sent = total.astype(BF)
    keep_ref[...] = sent.astype(F32)
    rows, bias = bias_rows(bias)
    send_ref[0:n, :] = sent
    send_ref[n : n + PACK, :] = rows
    bias_ref[...] = jnp.broadcast_to(bias, bias_ref.shape)


def backward_body(
    own_g, other_g, table, hid_1, slope_1, feats_1, hid_2, slope_2, feats_2, wo_ref, wu_ref,
    act, ga_ref, gn_ref, mine_ref, by_one, by_two, by_both,
    gsum, total,
):
    half, width = own_g.shape
    cells = 2 * half
    fine = lax.axis_index("fine")
    at_own, at_other = core_order(half)
    gsum[at_own, :] = own_g[...]
    gsum[at_other, :] = other_g[...]
    gn = dot_nt(gsum[...], wu_ref[...]).astype(BF)
    gn_ref[...] = gn
    grad = dot_nt(gn, wo_ref[...])
    ga = jnp.zeros((cells, width), F32)
    for k in range(K):
        at = slice(k * cells, (k + 1) * cells)
        slope, here = (slope_1, k) if k < EARLY else (slope_2, k - EARLY)
        part = (grad * slope[here * cells : (here + 1) * cells, :]).astype(BF)
        act[at, :] = part
        ga = ga + part.astype(F32)
    ga_ref[...] = ga

    fines = lax.axis_size("fine")
    per = 4 * width // fines
    n = min(per, width)
    for index in range(fines):

        @pl.when(fine == index)
        def _():
            for r in range(0, per, n):
                which, first = divmod(index * per + r, width)
                cols = slice(first, first + n)
                if which == 0:
                    high, low = split(ga_ref[...])
                    left = table[:, cols]
                    out = dot_tn(left, high) + dot_tn(left, low)
                elif which == 1:
                    n_1 = feats_1.shape[0]
                    out = dot_tn(feats_1[:, cols], act[0:n_1, :]) + dot_tn(feats_2[:, cols], act[n_1:, :])
                elif which == 2:
                    high, low = split(hid_1[:, cols] + hid_2[:, cols])
                    out = dot_tn(high, gn_ref[...]) + dot_tn(low, gn_ref[...])
                else:
                    high, low = split(hid_1[...] + hid_2[...])
                    agg = dot(high, wo_ref[:, cols]) + dot(low, wo_ref[:, cols])
                    new = (table[:, cols].astype(F32) + agg).astype(BF)
                    out = dot_tn(new, gsum[...])
                total[r : r + n, :] = out

    rows = bias_rows(jnp.sum(ga_ref[...], axis=0, keepdims=True))[0]
    half = axis_bit("coarse", 0)
    n = per // 2
    for ref, at in ((mine_ref, half), (by_one, 1 - half), (by_two, half), (by_both, 1 - half)):
        ref[0:n, :] = total[pl.ds(pl.multiple_of(at * n, n), n), :].astype(BF)
        ref[n : n + PACK, :] = rows


def square_sum_body(own, by_both, by_two, by_one, keep_ref, send_ref, bias_ref, slots):
    n = keep_ref.shape[0]
    me = lax.rem(lax.axis_index("coarse"), 4)
    for i, ref in enumerate((own, by_one, by_two, by_both)):
        slots[me ^ i] = ref[...].astype(F32)
    total = slots[0] + slots[1] + slots[2] + slots[3]
    emit(total[0:n], total[n : n + 1] + total[n + 1 : n + 2], keep_ref, send_ref, bias_ref)


def received_bias(recv, n):
    return recv[n : n + 1, :].astype(F32) + recv[n + 1 : n + 2, :].astype(F32)


def stage_body(keep_in, recv, bias_in, keep_ref, send_ref, bias_ref):
    n = keep_in.shape[0]
    total = keep_in[...] + recv[0:n, :].astype(F32)
    emit(total, bias_in[0:1, :] + received_bias(recv, n), keep_ref, send_ref, bias_ref)


def end_body(keep_in, recv, bias_in, out_ref):
    n = keep_in.shape[0]
    out_ref[0:n, :] = (keep_in[...] + recv[0:n, :].astype(F32)).astype(BF)
    out_ref[n : n + PACK, :] = bias_rows(bias_in[0:1, :] + received_bias(recv, n))[0]


def scatter(act, src_ref, first, count):
    cells = src_ref.shape[1]
    out = jnp.zeros((count, act.shape[1]), F32)
    for k in range(K):
        hot = hot_columns(src_ref[k : k + 1, :], count, first)
        out += dot(hot, act[k * cells : (k + 1) * cells, :])
    return out


def back_body(act, src_ref, w1_ref, out_ref):
    side, width = out_ref.shape
    core = lax.axis_index("fine") % 2
    rows = scatter(act, src_ref, src_ref.shape[1] + (1 - core) * side, side)
    out_ref[...] = dot_nt(rows.astype(BF), w1_ref[width : 2 * width, :]).astype(BF)


def cell_grad_body(act, src_ref, ga_ref, gn_ref, w1_ref, out_ref, *, first):
    count, width = out_ref.shape
    step = min(512, count)
    for r in range(0, count, step):
        at = slice(first + r, first + r + step)
        rows = scatter(act, src_ref, first + r, step)
        out_ref[r : r + step, :] = (
            gn_ref[at, :].astype(F32)
            + dot_nt(ga_ref[at, :].astype(BF), w1_ref[0:width, :])
            + dot_nt(rows.astype(BF), w1_ref[width : 2 * width, :])
        )


def merge_body(own, other, *rest, bit):
    n = own.shape[0]
    out_ref = rest[-1]
    side = axis_bit("fine", bit)
    out_ref[pl.ds(pl.multiple_of(side * n, PACK), n), :] = own[...]
    out_ref[pl.ds(pl.multiple_of((1 - side) * n, PACK), n), :] = other[...]


def square_body(own, by_owner, by_chip, by_both, out_ref):
    size = out_ref.shape[0] // 2
    n = own.shape[0] - PACK
    half, chip = axis_bit("coarse", 0), axis_bit("fine", 1)
    for block, i, j in ((own, half, chip), (by_owner, 1 - half, chip), (by_chip, half, 1 - chip), (by_both, 1 - half, 1 - chip)):
        out_ref[pl.ds(pl.multiple_of(j * size + i * n, PACK), n), :] = block[0:n, :]
    for block, j in ((own, chip), (by_chip, 1 - chip)):
        out_ref[pl.ds(pl.multiple_of(j * size + 2 * n, PACK), PACK), :] = block[n:, :]


def weights_body(own, other, w1_ref, gb_ref, wo_ref, up_ref, *, per, edge_scale, cell_scale):
    width = own.shape[1]
    core = lax.axis_index("fine") % 2
    outs = ((w1_ref, 0, edge_scale), (w1_ref, width, edge_scale), (wo_ref, 0, edge_scale), (up_ref, 0, cell_scale))
    size = per + PACK
    n = min(per, width)
    for index in range(lax.axis_size("fine")):
        at = slice((index // 2) * size, (index // 2 + 1) * size)
        value = jnp.where(core == index % 2, own[at, :].astype(F32), other[at, :].astype(F32))
        if index == 0:
            gb_ref[...] = (value[per : per + 1] + value[per + 1 : per + 2]) * edge_scale
        for r in range(0, per, n):
            which, row = divmod(index * per + r, width)
            out_ref, start, scale = outs[which]
            out_ref[start + row : start + row + n, :] = value[r : r + n] * scale


def table_body(*refs):
    *pool_refs, own_back, other_back, lists_ref, table = refs
    lists = lists_ref[...]
    core = lax.axis_index("fine") % 2
    side = own_back.shape[0]
    returned = jnp.concatenate([own_back[...], other_back[...]], axis=0)
    first, second = lists[:, :side], lists[:, side:]
    lists = jnp.where(core == 0, jnp.concatenate([second, first], axis=1), lists)
    step = pool_refs[0].shape[0]
    for i, pool_ref in enumerate(pool_refs):
        add = dot(hot_columns(lists, step, i * step), returned)
        table[i * step : (i + 1) * step, :] = (pool_ref[...] + add).astype(BF)


def feats_body(table, ids_ref, grad_ref, out_hbm, token_ref, out, sems):
    token_ref[...] = jnp.zeros_like(token_ref)
    cells = table.shape[0]
    block = out.shape[0] // sems.shape[0]
    stores = []
    for i in range(sems.shape[0]):
        at = slice(i * block, (i + 1) * block)
        rows = dot(hot_rows(ids_ref[:, at], cells), table[...])
        out[at, :] = (grad_ref[at, :].astype(F32) + rows).astype(BF)
        stores.append(pltpu.make_async_copy(out.at[at, :], out_hbm.at[at, :], sems.at[i]))
        stores[-1].start()
    for store in stores:
        store.wait()


def local(
    node_feats, grad_out, cluster_ids, halo_lists, edge_sources, w_edge_in, b_edge_in, w_edge_out, w_unpool,
):
    nodes, width = node_feats.shape
    cells = edge_sources.shape[0] // K
    half = cells // 2
    side = halo_lists.shape[0] // 2
    fines, coarses = lax.axis_size("fine"), lax.axis_size("coarse")
    fine_bits, coarse_bits = bits_of(fines), bits_of(coarses)
    ids = call(
        functools.partial(local_body, cells=cells), (sds((1, nodes), jnp.int32),), (cluster_ids.reshape(1, nodes),), AHEAD
    )[0]
    lists = halo_lists.reshape(1, 2 * side)
    flat = edge_sources.reshape(cells * K // LANES, LANES)
    src = call(
        source_body, (sds((K, cells), jnp.int32),), (flat,), 0, scratch=(pltpu.VMEM(flat.shape, jnp.int32),)
    )[0]
    bias = b_edge_in.reshape(1, width)

    def half_sums(x, other, after=()):
        body = functools.partial(pool_body, other=other)
        return call(body, (sds((half, width), F32),), (ids, x), nodes * cells * width, after=after)[0]

    def chip_sums(keep, recv, after=()):
        outs = (sds((half, width), F32), sds((half, width), BF))
        return call(chip_body, outs, (keep, recv), 0, after=after)

    def across(part, send, after=()):
        for bit in range(1, fine_bits):
            recv = swap(send, "fine", bit)
            last = bit == fine_bits - 1
            outs = (sds((half, width), BF),) if last else (sds((half, width), F32), sds((half, width), BF))
            part, send = (*call(across_body, outs, (part, recv), 0, after=after), None)[:2]
        return part

    recv_p = swap(half_sums(node_feats, True), "fine", 0)
    recv_g = swap(half_sums(grad_out, True), "fine", 0)
    part_p, send_p = chip_sums(half_sums(node_feats, False), recv_p)
    picked = call(pick_body, (sds((2 * side, width), BF),), (send_p, lists), 0)[0]
    sent = call(side_body, (sds((side, width), BF),), (picked, swap(picked, "fine", 0)), 0)[0]
    part_g, send_g = chip_sums(half_sums(grad_out, False, after=(send_p,)), recv_g)
    own_halo = call(
        halo_sum_body, (sds((side, width), BF),), [send_sides(sent, d) for d in range(fines // 2)], 0,
        scratch=(pltpu.VMEM((fines // 2, side, width), F32),),
    )[0]
    own_p = across(part_p, send_p, after=(own_halo, src, bias))
    other_halo = swap(own_halo, "fine", 0)
    others = [swap(x, "fine", 0) for x in (own_p[: half // 2], own_p[half // 2 :])]
    near = call(near_body, (sds((K * cells, width), BF),), (own_p, src), 0, vmem=24)[0]
    table, far, base = call(
        extend_body,
        (sds((cells, width), BF), sds((half + 2 * side, width), BF), sds((cells, width), F32)),
        (*others, own_p, own_halo, other_halo, w_edge_in, bias),
        0,
    )

    def forward(first, count, after=(), tokens=()):
        edges = count * cells
        return call(
            functools.partial(forward_body, first=first),
            (sds((cells, width), F32), sds((edges, width), F32), sds((edges, width), BF), *tokens),
            (base, far, near, src, w_edge_in),
            0,
            vmem=32,
            after=after,
        )

    *front, front_token = forward(0, EARLY, tokens=(sds((8, LANES), F32),))
    own_g = across(part_g, send_g, after=(front_token,))
    other_g = swap(own_g, "fine", 0)
    rear = forward(EARLY, K - EARLY, after=(own_g,))
    per = 4 * width // fines
    first = per // 2
    message = sds((first + PACK, width), BF)
    act, ga, gn, mine, *sends = call(
        backward_body,
        (
            sds((K * cells, width), BF), sds((cells, width), F32), sds((cells, width), BF),
            message, message, message, message,
        ),
        (own_g, other_g, table, *front, *rear, w_edge_out, w_unpool),
        2 * K * cells * width * width,
        vmem=32,
        scratch=(pltpu.VMEM((cells, width), BF), pltpu.VMEM((per, width), F32)),
    )

    back = call(
        back_body, (sds((side, width), BF),), (act, src, w_edge_in), 0
    )[0]
    own_back = send_sides(back)
    cell_grads = [
        call(
            functools.partial(cell_grad_body, first=at),
            (sds((half, width), F32),),
            (act, src, ga, gn, w_edge_in),
            2 * K * half * cells * width,
        )[0]
        for at in (0, half)
    ]
    recvs = swap_owners(sends[2]), swap(sends[1], "coarse", 1), swap(sends[0], "coarse", 0)
    outs = (sds((first, width), F32), message, sds((8, width), F32))
    keep, send, bias_sum = call(
        square_sum_body, outs, (mine, *recvs), 0, after=(own_back, cell_grads[1]),
        scratch=(pltpu.VMEM((4, first + PACK, width), F32),),
    )
    other_back = swap(own_back, "fine", 0)
    table = call(
        table_body, (sds((cells, width), BF),), (*cell_grads, own_back, other_back, lists), 0
    )[0]

    for bit in range(2, coarse_bits - 1):
        recv = swap(send, "coarse", bit)
        keep, send, bias_sum = call(stage_body, outs, (keep, recv, bias_sum), 0)
    recv = swap(send, "coarse", coarse_bits - 1)
    part = call(end_body, (message,), (keep, recv, bias_sum), 0, after=(other_back, cell_grads[0]))[0]
    grad_feats, feats_token = call(
        feats_body, (sds((nodes, width), BF), sds((8, LANES), F32)), (table, ids, grad_out), 2 * nodes * cells * width,
        vmem=24, scratch=(pltpu.VMEM((nodes, width), BF), pltpu.SemaphoreType.DMA((nodes // 256,))), far=1,
    )
    near = [swap(part, "coarse", 0), swap(part, "fine", 1), swap_both(part)]
    part = call(
        square_body, (sds((2 * (per + PACK), width), BF),), (part, *near), 0, after=(feats_token,)
    )[0]
    for bit in range(2, fine_bits):
        other = swap(part, "fine", bit)
        body = functools.partial(merge_body, bit=bit)
        part = call(body, (sds((2 * part.shape[0], width), BF),), (part, other), 0)[0]
    other = swap(part, "fine", 0)
    total_cells = cells * coarses
    scales = dict(edge_scale=float(total_cells * K) ** -0.5, cell_scale=float(total_cells) ** -0.5)
    grad_w1, grad_b, grad_wo, grad_up = call(
        functools.partial(weights_body, per=per, **scales),
        (
            sds((2 * width, width), F32), sds((1, width), F32), sds((width, width), F32), sds((width, width), F32),
        ),
        (part, other),
        0,
    )
    return grad_feats, grad_w1, grad_b.reshape(width), grad_wo, grad_up


def solution(mesh):
    both = ("coarse", "fine")
    return jax.shard_map(
        local,
        mesh=mesh,
        in_specs=(P(both, None), P(both, None), P(both), P("coarse"), P("coarse"), P(), P(), P(), P()),
        out_specs=(P(both, None), P(), P(), P(), P()),
        check_vma=False,
    )
```
